128 devices in a mesh: band: 16 (over y_lo, x, core), off: 2 (over y_hi), rep: 4 (over z).
Axes of the slice: x: 4, y: 4 (y_hi: 2, y_lo: 2; y = y_hi * 2 + y_lo), z: 4, core: 2. Of those that a mesh axis runs over, the one named last changes fastest.
Arguments:
- feats: bfloat16 [4096, 1024], P(('rep', 'band')), parts along dimension 0, may hold values from -6 to 6
- w_proj: bfloat16 [1024, 128], replicated, may hold values from -0.1875 to 0.1875
- conv_w: bfloat16 [576, 64], replicated, may hold values from -0.25 to 0.25
- conv_b: float32 [64], replicated, may hold values from -3 to 3
- w_out: float32 [64], replicated, may hold values from -0.75 to 0.75
- target: float32 [4096, 4, 64], P(('rep', 'band'), 'off'), parts along dimension 0, may hold values from -6 to 6
- mask: int32 [4096], P('rep'), parts along dimension 0, may hold values 0 or 1
Outputs:
- loss: float32 [4], P('rep'), parts along dimension 0
- grad_proj: float32 [4096, 128], P('rep'), parts along dimension 0
- grad_conv: float32 [2304, 64], P('rep'), parts along dimension 0
- grad_bias: float32 [256], P('rep'), parts along dimension 0
- grad_wout: float32 [256], P('rep'), parts along dimension 0
- grad_feats: bfloat16 [4096, 1024], P(('rep', 'band', 'off')), parts along dimension 0
The draws below stay inside these ranges and needn't reach their ends.
There are 4 independent parts, one for each index of `rep`. The reference program is written for one: setup_inputs(seed, part) draws one part's arguments, and reference() takes and returns one part's arrays. A program takes and returns all parts, laid end to end along the dimension named above; an argument that names none is the same for every part. Nothing has to cross between parts.
All inputs are finite; a program needn't handle non-finite values.
Results may differ from the reference program's by a relative error of at most 0.029.
Values may be sent and summed in bfloat16 or wider, within the bound.
No kernel may reach another device: no remote copies, remote signals or barrier semaphores. Data moves between devices by JAX's collectives and lax.ppermute only.
A program may use at most 192 MiB of HBM per device.

```python
import jax
import jax.numpy as jnp
from jax import lax

F = 1024
C = 64
TILE_BINS = 64
DILATION_STEP = 8
K = 4
NB = 1024
N_BAND = 16


def place_ends(values, own_key, low, largest):
    longest = values.shape.index(max(values.shape))
    spots = []
    for shift in (0, 1):
        where = [jax.random.randint(jax.random.fold_in(own_key, axis), (), 0, length) for axis, length in enumerate(values.shape)]
        where[longest] = (where[longest] + shift) % values.shape[longest]
        spots.append(tuple(where))
    return values.at[spots[0]].set(low).at[spots[1]].set(largest)


def shard_levels(key, shape, shards, smallest, high):
    factor_of = 1.0
    for dim, shards_of in shards:
        heights = jax.random.uniform(jax.random.fold_in(jax.random.fold_in(key, 6), dim), (shards_of,), jnp.float32, smallest / len(shards), high / len(shards))
        factor_of = factor_of * jnp.repeat(jnp.exp(heights), shape[dim] // shards_of).reshape((-1,) + (1,) * (len(shape) - 1 - dim))
    return factor_of


def centred(stream_key, shape, width, bound, pieces=(), held_as=jnp.bfloat16):
    drawn = width * jax.random.normal(stream_key, shape, jnp.float32)
    if pieces:
        drawn = drawn * shard_levels(stream_key, shape, pieces, -0.22, 0.18)
    return jnp.clip(drawn, -bound, bound).astype(held_as)


def setup_inputs(seed: int = 0, part: int = 0) -> dict:
    seeds = jax.random.split(jax.random.key(seed), 8)
    part_splits = jax.random.split(jax.random.fold_in(seeds[7], part), 8)
    feats = centred(part_splits[0], (NB, F), 1.0, 6.0, ((0, 16),))
    w_proj = centred(seeds[1], (F, 2 * C), F ** -0.5, 0.1875)
    conv_w = centred(seeds[2], (9 * C, C), (9 * C) ** -0.5, 0.25)
    conv_b = centred(seeds[3], (C,), 0.5, 3.0, (), jnp.float32)
    w_out = centred(seeds[4], (C,), C ** -0.5, 0.75, (), jnp.float32)
    target = centred(part_splits[5], (NB, K, TILE_BINS), 1.0, 6.0, ((0, 16), (1, 2)), jnp.float32)
    mask = place_ends((jax.random.randint(part_splits[6], (NB,), 0, 8) < 7).astype(jnp.int32), jax.random.fold_in(part_splits[6], 1), 0, 1)
    return {"feats": feats, "w_proj": w_proj, "conv_w": conv_w, "conv_b": conv_b, "w_out": w_out, "target": target, "mask": mask}


GELU_K = 0.7978845608028654


def gelu_both(preact):
    tangent = jnp.tanh(GELU_K * (preact + 0.044715 * preact * preact * preact))
    value = 0.5 * preact * (1.0 + tangent)
    slope = 0.5 * (1.0 + tangent) + 0.5 * preact * (1.0 - tangent * tangent) * GELU_K * (1.0 + 3.0 * 0.044715 * preact * preact)
    return value, slope


def tile_grads(row_ext, col_ext, row_valid, col_valid, row_kernel_weight, column_kernel_weight, target_tile, conv_w, conv_b, w_out, scale):
    tile_edge_length = row_kernel_weight.shape[0]
    kernel_width = conv_w.shape[1]
    inside = row_valid[:, None] * col_valid[None, :]
    pair_sum = row_ext.astype(jnp.float32)[:, None, :] + col_ext.astype(jnp.float32)[None, :, :]
    pair_value, pair_slope = gelu_both(pair_sum)
    pairwise_map = (pair_value * inside[:, :, None]).astype(jnp.bfloat16)
    tile_parts = [pairwise_map[row_kernel_tap * DILATION_STEP:row_kernel_tap * DILATION_STEP + tile_edge_length, column_kernel_tap * DILATION_STEP:column_kernel_tap * DILATION_STEP + tile_edge_length, :] for row_kernel_tap in range(3) for column_kernel_tap in range(3)]
    columns = jnp.concatenate(tile_parts, axis=-1).reshape(tile_edge_length * tile_edge_length, 9 * kernel_width)
    preact = jnp.dot(columns, conv_w, preferred_element_type=jnp.float32) + conv_b
    hidden, slope = gelu_both(preact)
    predicted = jnp.sum(hidden * w_out, axis=-1)
    weight = (row_kernel_weight[:, None] * column_kernel_weight[None, :]).reshape(-1)
    residue = predicted - target_tile.reshape(-1)
    numerator = jnp.sum(weight * residue * residue)
    grad_pred = 2.0 * weight * residue * scale
    grad_pre = grad_pred[:, None] * w_out[None, :] * slope
    grad_pre_b = grad_pre.astype(jnp.bfloat16)
    grad_bias = jnp.sum(grad_pre, axis=0)
    grad_wout = jnp.sum(grad_pred[:, None] * hidden, axis=0)
    grad_conv = lax.dot_general(columns, grad_pre_b, (((0,), (0,)), ((), ())), preferred_element_type=jnp.float32)
    column_gradient = lax.dot_general(grad_pre_b, conv_w, (((1,), (1,)), ((), ())), preferred_element_type=jnp.float32).reshape(tile_edge_length, tile_edge_length, 9, kernel_width)
    pair_gradient = jnp.zeros((tile_edge_length + 2 * DILATION_STEP, tile_edge_length + 2 * DILATION_STEP, kernel_width), jnp.float32)
    for kernel_tap_index in range(9):
        row_kernel_tap, column_kernel_tap = divmod(kernel_tap_index, 3)
        pair_gradient = pair_gradient.at[row_kernel_tap * DILATION_STEP:row_kernel_tap * DILATION_STEP + tile_edge_length, column_kernel_tap * DILATION_STEP:column_kernel_tap * DILATION_STEP + tile_edge_length, :].add(column_gradient[:, :, kernel_tap_index, :])
    pair_gradient = pair_gradient * (pair_slope * inside[:, :, None])
    return numerator, grad_conv, grad_bias, grad_wout, jnp.sum(pair_gradient, axis=1), jnp.sum(pair_gradient, axis=0)


def reference(feats, w_proj, conv_w, conv_b, w_out, target, mask):
    zero_index = jnp.zeros((), jnp.int32)
    chan_index = jnp.full((), C, jnp.int32)
    proj = jnp.dot(feats, w_proj, preferred_element_type=jnp.float32).astype(jnp.bfloat16)
    total_rows = (N_BAND + K + 2) * TILE_BINS
    proj_pad = jnp.zeros((total_rows, 2 * C), jnp.bfloat16).at[TILE_BINS:TILE_BINS + NB].set(proj)
    padding_mask = jnp.zeros((total_rows,), jnp.float32).at[TILE_BINS:TILE_BINS + NB].set(mask.astype(jnp.float32))
    position = jnp.arange(total_rows, dtype=jnp.int32) - TILE_BINS
    valid_pad = ((position >= 0) & (position < NB)).astype(jnp.float32)
    band_sums = jnp.sum(padding_mask.reshape(N_BAND + K + 2, TILE_BINS), axis=1)
    band_ids = jnp.arange(N_BAND, dtype=jnp.int32)
    offset_ids = jnp.arange(K, dtype=jnp.int32)
    count = jnp.sum(band_sums[1 + band_ids][:, None] * band_sums[1 + band_ids[:, None] + offset_ids[None, :]])
    scale = 1.0 / count
    padded_extent = TILE_BINS + 2 * DILATION_STEP

    def visit(carry, tile_id):
        numerator, grad_conv, grad_bias, grad_wout, grad_full = carry
        row_band_index = (tile_id // K).astype(jnp.int32)
        band_offset_index = (tile_id % K).astype(jnp.int32)
        row_begin = (row_band_index * TILE_BINS + TILE_BINS - DILATION_STEP).astype(jnp.int32)
        column_begin = ((row_band_index + band_offset_index) * TILE_BINS + TILE_BINS - DILATION_STEP).astype(jnp.int32)
        row_ext = lax.dynamic_slice(proj_pad, (row_begin, zero_index), (padded_extent, C))
        col_ext = lax.dynamic_slice(proj_pad, (column_begin, chan_index), (padded_extent, C))
        row_valid = lax.dynamic_slice(valid_pad, (row_begin,), (padded_extent,))
        col_valid = lax.dynamic_slice(valid_pad, (column_begin,), (padded_extent,))
        row_kernel_weight = lax.dynamic_slice(padding_mask, ((row_begin + DILATION_STEP).astype(jnp.int32),), (TILE_BINS,))
        column_kernel_weight = lax.dynamic_slice(padding_mask, ((column_begin + DILATION_STEP).astype(jnp.int32),), (TILE_BINS,))
        target_tile = lax.dynamic_slice(target, ((row_band_index * TILE_BINS).astype(jnp.int32), band_offset_index, zero_index), (TILE_BINS, 1, TILE_BINS)).reshape(TILE_BINS, TILE_BINS)
        terms = tile_grads(row_ext, col_ext, row_valid, col_valid, row_kernel_weight, column_kernel_weight, target_tile, conv_w, conv_b, w_out, scale)
        old_rows = lax.dynamic_slice(grad_full, (row_begin, zero_index), (padded_extent, C))
        grad_full = lax.dynamic_update_slice(grad_full, old_rows + terms[4], (row_begin, zero_index))
        old_cols = lax.dynamic_slice(grad_full, (column_begin, chan_index), (padded_extent, C))
        grad_full = lax.dynamic_update_slice(grad_full, old_cols + terms[5], (column_begin, chan_index))
        return (numerator + terms[0], grad_conv + terms[1], grad_bias + terms[2], grad_wout + terms[3], grad_full), None

    start = (jnp.zeros((), jnp.float32), jnp.zeros((9 * C, C), jnp.float32), jnp.zeros((C,), jnp.float32), jnp.zeros((C,), jnp.float32), jnp.zeros((total_rows, 2 * C), jnp.float32))
    final, unused = lax.scan(visit, start, jnp.arange(N_BAND * K, dtype=jnp.int32))
    numerator, grad_conv, grad_bias, grad_wout, grad_full = final
    gproj = grad_full[TILE_BINS:TILE_BINS + NB].astype(jnp.bfloat16)
    grad_feats = lax.dot_general(gproj, w_proj, (((1,), (1,)), ((), ())), preferred_element_type=jnp.float32).astype(jnp.bfloat16)
    grad_proj = lax.dot_general(feats, gproj, (((0,), (0,)), ((), ())), preferred_element_type=jnp.float32)
    loss = (numerator * scale).reshape(1)
    return (loss, grad_proj, grad_conv, grad_bias, grad_wout, grad_feats)
```

```python
import jax
import jax.numpy as jnp
from jax import lax
from jax.experimental import pallas as pl
from jax.experimental.pallas import tpu as pltpu
from jax.sharding import PartitionSpec as P

GELU_K = 0.7978845608028654
GELU_C = 0.044715
GROUP = ("band", "off")
PEERS = 32
SLOT = 48
F32 = jnp.float32
BF16 = jnp.bfloat16


def gelu_parts(x, half):
    square = x * x
    t = jnp.tanh(x * (GELU_K + (GELU_K * GELU_C) * square))
    one_plus = 1.0 + t
    scaled = x * half
    value = scaled * one_plus
    slope = one_plus * (half + (scaled * (1.0 - t)) * (GELU_K + (3.0 * GELU_K * GELU_C) * square))
    return value, slope


def lane_ids(shape):
    return lax.broadcasted_iota(jnp.int32, shape, len(shape) - 1)


def row_ids(shape):
    return lax.broadcasted_iota(jnp.int32, shape, len(shape) - 2)


def dot(a, b):
    return jnp.dot(a, b, preferred_element_type=F32)


def tile_kernel(
    own, before, after1, after2, after3, after4, mask, target, fwd_w, bwd_w, conv_b2, w_out2, pred_w,
    out,
    rows_u, cols_v, pair, slope, grads, goal, pre, hid16, hid32, weighted, guess, row_mask, col_mask,
    grad_rows, grad_cols, grad_w, bins,
):
    band = lax.axis_index("band")
    off = lax.axis_index("off")
    first = band + 2 * off
    near = off == 0
    half_lane = lane_ids((1, 128)) < 64

    zero_rows = jnp.zeros((128, 1280), BF16)
    grads[0:128, :] = zero_rows
    grads[640:768, :] = zero_rows
    grads[128:640, 0:128] = jnp.zeros((512, 128), BF16)
    grads[128:640, 1152:1280] = jnp.zeros((512, 128), BF16)
    bins[...] = jnp.zeros(bins.shape, F32)

    mine = own[...].astype(F32)
    b_before = before[...].astype(F32)
    b_1 = after1[...].astype(F32)
    b_2 = after2[...].astype(F32)
    b_3 = after3[...].astype(F32)
    b_4 = after4[...].astype(F32)
    u = jnp.concatenate([b_before[8:16], mine, b_1[0:8]], axis=0)
    rows_u[...] = jnp.where(half_lane, u, pltpu.roll(u, 64, 1))
    v = jnp.concatenate(
        [
            jnp.where(near, b_before[8:16], b_1[56:64]),
            jnp.where(near, mine, b_2),
            jnp.where(near, b_1, b_3),
            jnp.where(near, b_2[0:8], b_4[0:8]),
        ],
        axis=0,
    ).reshape(9, 2, 8, 128)
    v_low = v[:, 0].reshape(72, 128)
    v_high = v[:, 1].reshape(72, 128)
    cols_v[...] = jnp.where(half_lane, pltpu.roll(v_low, 64, 1), v_high)

    mask_all = mask[...].astype(F32)
    mask_lane = lane_ids((8, 128))
    by_band = jnp.concatenate(
        [jnp.where(mask_lane < 64, mask_all, 0.0), jnp.where(mask_lane < 64, 0.0, mask_all)], axis=0
    ).astype(BF16)
    sums_row = dot(by_band, jnp.ones((128, 128), BF16))
    sums_col = lax.dot_general(
        jnp.ones((16, 128), BF16), by_band, (((1,), (1,)), ((), ())), preferred_element_type=F32
    )
    at = lax.broadcasted_iota(jnp.int32, (16, 16), 0)
    to = lax.broadcasted_iota(jnp.int32, (16, 16), 1)
    apart = (2 * (to % 8) + to // 8) - (2 * (at % 8) + at // 8)
    near_diagonal = (apart >= 0) & (apart < 4)
    count = jnp.sum(jnp.where(near_diagonal, sums_row[:, 0:16] * sums_col, 0.0))
    scale = 1.0 / count

    def mask_rows(which):
        inside = jnp.minimum(which, 15)
        line = mask[pl.ds(inside // 2, 1), :].astype(F32)
        line = jnp.where(which < 16, line, 0.0)
        spot = row_ids((64, 128)) + 64 * (inside % 2)
        spread = jnp.where(lane_ids((64, 128)) == spot, line, 0.0)
        return dot(spread.astype(BF16), jnp.ones((128, 128), BF16))

    row_mask[...] = (
        jnp.broadcast_to(mask_rows(band)[:, None, :] * (2.0 * scale), (64, 8, 128)).reshape(512, 128)
    )
    col_all = jnp.concatenate([mask_rows(first), mask_rows(first + 1)], axis=0).reshape(8, 2, 8, 128)
    col_mask[...] = jnp.where(half_lane, col_all[:, 0].reshape(64, 128), col_all[:, 1].reshape(64, 128))

    lines = jnp.broadcast_to(target[...][:, None, :], (64, 8, 128)).reshape(512, 128)
    lines = jnp.where(lane_ids((512, 128)) % 8 == row_ids((512, 128)) % 8, lines, 0.0)
    lines_hi = lines.astype(BF16)
    lines_lo = (lines - lines_hi.astype(F32)).astype(BF16)
    spread = (
        (row_ids((128, 1024)) // 8 == lane_ids((128, 1024)) // 64).astype(F32).astype(BF16)
    )
    goal[...] = dot(
        jnp.concatenate([lines_hi, lines_lo], axis=1), jnp.concatenate([spread, spread], axis=0)
    )

    def pair_step(aq, carry):
        row = pl.multiple_of(aq * 64, 64)
        here = rows_u[pl.ds(pl.multiple_of(aq * 8, 8), 8), :]
        row_at = band * 8 + aq - 1
        row_in = (row_at >= 0) & (row_at < 128)
        for bp in range(9):
            block = first * 8 - 1 + 2 * bp
            spot = jnp.where(half_lane, block, block + 1)
            half = jnp.where((spot >= 0) & (spot < 128) & row_in, 0.5, 0.0)
            x = (here[:, None, :] + cols_v[bp * 8 : bp * 8 + 8, :][None, :, :]).reshape(64, 128)
            value, grade = gelu_parts(x, half)
            pair[pl.ds(row, 64), bp * 128 : bp * 128 + 128] = value.astype(BF16)
            slope[pl.ds(row, 64), bp * 128 : bp * 128 + 128] = grade
        return carry

    lax.fori_loop(0, 10, pair_step, 0)

    bias2 = conv_b2[...]
    out_w2 = w_out2[...]
    zero8 = jnp.zeros((8, 128), F32)
    totals = (zero8, zero8, zero8)
    for bp in range(8):
        lane = bp * 128
        pre[...] = (
            dot(pair[0:512, lane : lane + 256], fwd_w[0:256, :])
            + dot(pair[64:576, lane : lane + 256], fwd_w[256:512, :])
            + dot(pair[128:640, lane : lane + 256], fwd_w[512:768, :])
        )

        def act_step(aq, carry):
            row = pl.ds(pl.multiple_of(aq * 64, 64), 64)
            value, grade = gelu_parts(pre[row, :] + bias2, 0.5)
            hid32[row, :] = value
            hid16[row, :] = value.astype(BF16)
            weighted[row, :] = grade * out_w2
            return carry

        lax.fori_loop(0, 8, act_step, 0)
        low = hid16[...]
        guess[...] = dot(jnp.concatenate([low, low], axis=1), pred_w[...])

        def loss_step(aq, carry):
            loss_sum, bias_sum, out_sum = carry
            start = pl.multiple_of(aq * 64, 64)
            row = pl.ds(start, 64)
            weight = (row_mask[row, :].reshape(8, 8, 128) * col_mask[bp * 8 : bp * 8 + 8, :][None]).reshape(64, 128)
            residue = guess[row, :] - goal[row, lane : lane + 128]
            grad_pred = weight * residue
            grad_pre = grad_pred * weighted[row, :]
            grads[pl.ds(pl.multiple_of(start + 128, 64), 64), lane + 128 : lane + 256] = grad_pre.astype(BF16)
            loss_sum = loss_sum + jnp.sum((grad_pred * residue).reshape(8, 8, 128), axis=0)
            bias_sum = bias_sum + jnp.sum(grad_pre.reshape(8, 8, 128), axis=0)
            out_sum = out_sum + jnp.sum((grad_pred * hid32[row, :]).reshape(8, 8, 128), axis=0)
            return loss_sum, bias_sum, out_sum

        totals = lax.fori_loop(0, 8, loss_step, totals)

    for bp in range(8):
        lane = bp * 128
        turned = grads[128:640, lane + 128 : lane + 256].T
        for ty in range(3):
            part = dot(turned, pair[ty * 64 : ty * 64 + 512, lane : lane + 256])
            if bp == 0:
                grad_w[:, ty * 256 : ty * 256 + 256] = part
            else:
                grad_w[:, ty * 256 : ty * 256 + 256] += part

    for bp in range(9):
        lane = bp * 128
        part = (
            dot(grads[128:768, lane : lane + 256], bwd_w[0:256, :])
            + dot(grads[64:704, lane : lane + 256], bwd_w[256:512, :])
            + dot(grads[0:640, lane : lane + 256], bwd_w[512:768, :])
        ) * slope[:, lane : lane + 128]
        if bp == 0:
            grad_rows[...] = part
        else:
            grad_rows[...] += part
        grad_cols[bp * 8 : bp * 8 + 8, :] = jnp.sum(part.reshape(80, 8, 128), axis=0)

    row_part = jnp.sum(grad_rows[...].reshape(80, 8, 128), axis=1)
    row_part = jnp.where(half_lane, row_part + pltpu.roll(row_part, 64, 1), 0.0)
    bins[pl.ds(pl.multiple_of(band * 64 + 56, 8), 80), :] += row_part
    col_part = grad_cols[...]
    col_low = pltpu.roll(col_part, 64, 1).reshape(9, 1, 8, 128)
    col_part = jnp.concatenate([col_low, col_part.reshape(9, 1, 8, 128)], axis=1).reshape(144, 128)
    col_part = jnp.where(half_lane, 0.0, col_part)
    bins[pl.ds(pl.multiple_of(first * 64 + 56, 8), 144), :] += col_part
    out[:, 0:32, :] = bins[64:1088, :].reshape(32, 32, 128).astype(BF16)

    taps = []
    for ty in range(3):
        low = grad_w[0:64, ty * 256 : ty * 256 + 192]
        high = grad_w[64:128, ty * 256 + 64 : ty * 256 + 256]
        taps.append((low + high).T)
    conv_grad = jnp.concatenate(taps, axis=0)
    conv_grad = jnp.concatenate([conv_grad[0:288], conv_grad[288:576]], axis=1)

    loss_sum, bias_sum, out_sum = totals
    bias_row = jnp.sum(bias_sum, axis=0, keepdims=True)
    bias_row = bias_row + pltpu.roll(bias_row, 64, 1)
    out_row = jnp.sum(out_sum, axis=0, keepdims=True)
    out_row = out_row + pltpu.roll(out_row, 64, 1)
    small_row = jnp.where(half_lane, bias_row, out_row)
    loss_row = jnp.broadcast_to(jnp.sum(loss_sum, keepdims=True) * (0.5 / 64.0), (1, 128))
    small_hi = small_row.astype(BF16).astype(F32)
    loss_hi = loss_row.astype(BF16).astype(F32)
    tail = jnp.concatenate(
        [small_hi, small_row - small_hi, loss_hi, loss_row - loss_hi, jnp.zeros((3, 128), F32)], axis=0
    )
    tail = jnp.broadcast_to(tail[None], (PEERS, 7, 128))
    rest = jnp.concatenate([conv_grad[256:288].reshape(PEERS, 1, 128), tail], axis=1)
    out[:, 32:48, :] = jnp.concatenate([conv_grad[0:256].reshape(PEERS, 8, 128), rest], axis=1).astype(BF16)


def tile_call(*operands):
    shapes = [
        ((80, 128), F32), ((72, 128), F32), ((640, 1152), BF16), ((640, 1152), F32), ((768, 1280), BF16),
        ((512, 1024), F32), ((512, 128), F32), ((512, 128), BF16), ((512, 128), F32), ((512, 128), F32),
        ((512, 128), F32), ((512, 128), F32), ((64, 128), F32), ((640, 128), F32), ((72, 128), F32),
        ((128, 768), F32), ((1408, 128), F32),
    ]
    return pl.pallas_call(
        tile_kernel,
        out_shape=jax.ShapeDtypeStruct((PEERS, SLOT, 128), BF16),
        in_specs=[pl.BlockSpec(memory_space=pltpu.VMEM)] * len(operands),
        out_specs=pl.BlockSpec(memory_space=pltpu.VMEM),
        scratch_shapes=[pltpu.VMEM(shape, kind) for shape, kind in shapes],
        compiler_params=pltpu.CompilerParams(vmem_limit_bytes=40 * 2**20),
        cost_estimate=pl.CostEstimate(flops=2 * 10**9, bytes_accessed=10**6, transcendentals=10**6),
        name="tiles",
    )(*operands)


def sum_kernel(parts, out, small):
    total = jnp.sum(parts[...].astype(F32), axis=0)
    out[...] = jnp.broadcast_to(total.astype(BF16)[None], (PEERS, SLOT, 128))
    small[0:1, :] = total[41:42] + total[42:43]
    small[1:2, :] = total[43:44] + total[44:45]


def sum_call(parts):
    return pl.pallas_call(
        sum_kernel,
        out_shape=(jax.ShapeDtypeStruct((PEERS, SLOT, 128), BF16), jax.ShapeDtypeStruct((2, 128), F32)),
        in_specs=[pl.BlockSpec(memory_space=pltpu.VMEM)],
        out_specs=(pl.BlockSpec(memory_space=pltpu.VMEM),) * 2,
        name="sums",
    )(parts)


def final_kernel(every, feats, w_proj, grad_proj, grad_conv, grad_feats):
    me = lax.axis_index("band") * 2 + lax.axis_index("off")
    gproj = every[:, 0:32, :].reshape(1024, 128)
    grad_proj[...] = lax.dot_general(
        feats[...], gproj, (((0,), (0,)), ((), ())), preferred_element_type=F32
    )
    conv = every[:, 32:48, :].astype(F32)
    conv = jnp.concatenate([conv[:, 0:8].reshape(256, 128), conv[:, 8]], axis=0)
    grad_conv[0:288, :] = conv[:, 0:64]
    grad_conv[288:576, :] = conv[:, 64:128]
    mine = every[me, 0:32, :]
    grad_feats[...] = lax.dot_general(
        mine, w_proj[...], (((1,), (1,)), ((), ())), preferred_element_type=F32
    ).astype(BF16)


def final_call(every, feats, w_proj):
    return pl.pallas_call(
        final_kernel,
        out_shape=(
            jax.ShapeDtypeStruct((1024, 128), F32),
            jax.ShapeDtypeStruct((576, 64), F32),
            jax.ShapeDtypeStruct((32, 1024), BF16),
        ),
        in_specs=[pl.BlockSpec(memory_space=pltpu.VMEM)] * 3,
        out_specs=(pl.BlockSpec(memory_space=pltpu.VMEM),) * 3,
        compiler_params=pltpu.CompilerParams(vmem_limit_bytes=40 * 2**20),
        name="outputs",
    )(every, feats, w_proj)


def body(feats, w_proj, conv_w, conv_b, w_out, target, mask):
    bands = lax.axis_size("band")
    gathered = lax.all_gather(feats, "band", tiled=True)
    proj = dot(feats, w_proj).astype(BF16)

    def moved(x, by, offs=(0, 1)):
        pairs = [(2 * i + o, 2 * (i - by) + o) for i in range(bands) for o in offs if 0 <= i - by < bands]
        return lax.ppermute(x, GROUP, pairs)

    before = moved(proj[48:64], -1)
    after1 = moved(proj, 1)
    after2 = moved(proj, 2)
    after3 = moved(proj, 3, (1,))
    after4 = moved(proj[0:16], 4, (1,))

    def toeplitz(taps):
        low = jnp.pad(taps, ((0, 0), (0, 64), (0, 0)))
        high = jnp.pad(taps, ((0, 0), (64, 0), (0, 0)))
        return jnp.concatenate([low, high], axis=2).reshape(768, 128)

    fwd_w = toeplitz(conv_w.reshape(3, 192, 64))
    turned = conv_w.reshape(3, 3, 64, 64)[:, ::-1].transpose(0, 1, 3, 2)
    bwd_w = toeplitz(turned.reshape(3, 192, 64))
    twice = jnp.concatenate([w_out, w_out])
    at = jnp.arange(128, dtype=jnp.int32)
    spread = jnp.where((at[:, None] < 64) == (at[None, :] < 64), twice[:, None], 0.0)
    spread_hi = spread.astype(BF16)
    pred_w = jnp.concatenate([spread_hi, (spread - spread_hi.astype(F32)).astype(BF16)], axis=0)
    sent = tile_call(
        proj, before, after1, after2, after3, after4,
        mask.reshape(8, 128), target.reshape(64, 128), fwd_w, bwd_w,
        jnp.concatenate([conv_b, conv_b]).reshape(1, 128), twice.reshape(1, 128), pred_w,
    )
    parts = lax.all_to_all(sent, GROUP, 0, 0, tiled=True)
    sums, small = sum_call(parts)
    every = lax.all_to_all(sums, GROUP, 0, 0, tiled=True)
    grad_proj, grad_conv, grad_feats = final_call(every, gathered, w_proj)
    return (small[1, 0:1], grad_proj, grad_conv, small[0, 0:64], small[0, 64:128], grad_feats)


def solution(mesh):
    placed = (
        P(("rep", "band"), None),
        P(),
        P(),
        P(),
        P(),
        P(("rep", "band"), "off", None),
        P("rep"),
    )
    return jax.shard_map(
        body,
        mesh=mesh,
        in_specs=placed,
        out_specs=(
            P("rep"),
            P("rep", None),
            P("rep", None),
            P("rep"),
            P("rep"),
            P(("rep", "band", "off"), None),
        ),
        check_vma=False,
    )
```

```python
import jax
import jax.numpy as jnp
from jax import lax
from jax.experimental import pallas as pl
from jax.experimental.pallas import tpu as pltpu
from jax.sharding import PartitionSpec as P

GELU_K = 0.7978845608028654
GELU_C = 0.044715
GROUP = ("band", "off")
PEERS = 32
SLOT = 48
F32 = jnp.float32
BF16 = jnp.bfloat16


def gelu_parts(x, half):
    square = x * x
    t = jnp.tanh(x * (GELU_K + (GELU_K * GELU_C) * square))
    one_plus = 1.0 + t
    scaled = x * half
    value = scaled * one_plus
    slope = one_plus * (half + (scaled * (1.0 - t)) * (GELU_K + (3.0 * GELU_K * GELU_C) * square))
    return value, slope


def lane_ids(shape):
    return lax.broadcasted_iota(jnp.int32, shape, len(shape) - 1)


def row_ids(shape):
    return lax.broadcasted_iota(jnp.int32, shape, len(shape) - 2)


def dot(a, b):
    return jnp.dot(a, b, preferred_element_type=F32)


def prep_kernel(
    mask, target, conv_t, conv_b, w_out, fwd_w, bwd_w, pred_w, goal, row_mask, col_mask, small
):
    band = lax.axis_index("band")
    first = band + 2 * lax.axis_index("off")
    half_lane = lane_ids((1, 128)) < 64

    blank = jnp.zeros((64, 64), F32)
    for ty in range(3):
        taps = [conv_t[:, (3 * ty + tx) * 64 : (3 * ty + tx + 1) * 64].astype(F32) for tx in range(3)]
        low = jnp.concatenate(taps + [blank], axis=1)
        high = jnp.concatenate([blank] + taps, axis=1)
        fwd_w[ty * 256 : ty * 256 + 256, :] = jnp.concatenate([low, high], axis=0).T.astype(BF16)
        left = taps[::-1] + [blank]
        right = [blank] + taps[::-1]
        for k in range(4):
            row = ty * 256 + k * 64
            bwd_w[row : row + 64, :] = jnp.concatenate([left[k], right[k]], axis=1).astype(BF16)

    bias2 = jnp.concatenate([conv_b[...], conv_b[...]], axis=1)
    twice = jnp.concatenate([w_out[...], w_out[...]], axis=1)
    small[...] = jnp.concatenate([bias2, twice, jnp.zeros((6, 128), F32)], axis=0)
    diagonal = row_ids((128, 128)) == lane_ids((128, 128))
    halves = (row_ids((128, 128)) < 64) == (lane_ids((128, 128)) < 64)
    twice_hi = twice.astype(BF16).astype(F32)
    halves_b = halves.astype(F32).astype(BF16)
    for k, part in enumerate((twice_hi, twice - twice_hi)):
        line = jnp.where(diagonal, part, 0.0).astype(BF16)
        pred_w[k * 128 : k * 128 + 128, :] = dot(line, halves_b).astype(BF16)

    mask_all = mask[...].astype(F32)
    mask_lane = lane_ids((8, 128))
    by_band = jnp.concatenate(
        [jnp.where(mask_lane < 64, mask_all, 0.0), jnp.where(mask_lane < 64, 0.0, mask_all)], axis=0
    ).astype(BF16)
    sums_row = dot(by_band, jnp.ones((128, 128), BF16))
    sums_col = lax.dot_general(
        jnp.ones((16, 128), BF16), by_band, (((1,), (1,)), ((), ())), preferred_element_type=F32
    )
    at = lax.broadcasted_iota(jnp.int32, (16, 16), 0)
    to = lax.broadcasted_iota(jnp.int32, (16, 16), 1)
    apart = (2 * (to % 8) + to // 8) - (2 * (at % 8) + at // 8)
    near_diagonal = (apart >= 0) & (apart < 4)
    count = jnp.sum(jnp.where(near_diagonal, sums_row[:, 0:16] * sums_col, 0.0))
    scale = 1.0 / count

    def mask_rows(which):
        inside = jnp.minimum(which, 15)
        line = mask[pl.ds(inside // 2, 1), :].astype(F32)
        line = jnp.where(which < 16, line, 0.0)
        spot = row_ids((64, 128)) + 64 * (inside % 2)
        spread = jnp.where(lane_ids((64, 128)) == spot, line, 0.0)
        return dot(spread.astype(BF16), jnp.ones((128, 128), BF16))

    row_mask[...] = (
        jnp.broadcast_to(mask_rows(band)[:, None, :] * (2.0 * scale), (64, 8, 128)).reshape(512, 128)
    )
    col_all = jnp.concatenate([mask_rows(first), mask_rows(first + 1)], axis=0).reshape(8, 2, 8, 128)
    col_mask[...] = jnp.where(half_lane, col_all[:, 0].reshape(64, 128), col_all[:, 1].reshape(64, 128))

    line = jnp.concatenate([target[:, 0, :], target[:, 1, :]], axis=1)
    lines = jnp.broadcast_to(line[:, None, :], (64, 8, 128)).reshape(512, 128)
    lines = jnp.where(lane_ids((512, 128)) % 8 == row_ids((512, 128)) % 8, lines, 0.0)
    lines_hi = lines.astype(BF16)
    lines_lo = (lines - lines_hi.astype(F32)).astype(BF16)
    spread = (
        (row_ids((128, 1024)) // 8 == lane_ids((128, 1024)) // 64).astype(F32).astype(BF16)
    )
    goal[...] = dot(
        jnp.concatenate([lines_hi, lines_lo], axis=1), jnp.concatenate([spread, spread], axis=0)
    )


def prep_call(*operands):
    shapes = [
        ((768, 128), BF16), ((768, 128), BF16), ((256, 128), BF16), ((512, 1024), F32), ((512, 128), F32),
        ((64, 128), F32), ((8, 128), F32),
    ]
    return pl.pallas_call(
        prep_kernel,
        out_shape=tuple(jax.ShapeDtypeStruct(shape, kind) for shape, kind in shapes),
        in_specs=[pl.BlockSpec(memory_space=pltpu.VMEM)] * len(operands),
        out_specs=(pl.BlockSpec(memory_space=pltpu.VMEM),) * len(shapes),
        compiler_params=pltpu.CompilerParams(vmem_limit_bytes=16 * 2**20),
        cost_estimate=pl.CostEstimate(flops=3 * 10**8, bytes_accessed=4 * 10**6, transcendentals=0),
        name="prepare",
    )(*operands)


def tile_kernel(
    own, before, after1, after2, after3, after4, w_proj, fwd_w, bwd_w, pred_w, goal, row_mask, col_mask, small,
    out,
    rows_u, cols_v, pair, slope, grads, pre, hid16, hid32, weighted, guess, grad_rows, grad_cols, grad_w, bins,
):
    band = lax.axis_index("band")
    off = lax.axis_index("off")
    first = band + 2 * off
    near = off == 0
    half_lane = lane_ids((1, 128)) < 64

    zero_rows = jnp.zeros((128, 1280), BF16)
    grads[0:128, :] = zero_rows
    grads[640:768, :] = zero_rows
    grads[128:640, 0:128] = jnp.zeros((512, 128), BF16)
    grads[128:640, 1152:1280] = jnp.zeros((512, 128), BF16)
    bins[...] = jnp.zeros(bins.shape, F32)

    feats = jnp.concatenate(
        [before[...], own[...], after1[...], after2[...], after3[...], after4[...]], axis=0
    )
    proj = dot(feats, w_proj[...]).astype(BF16).astype(F32)
    b_before, mine, b_1 = proj[0:16], proj[16:80], proj[80:144]
    b_2, b_3, b_4 = proj[144:208], proj[208:272], proj[272:288]
    u = jnp.concatenate([b_before[8:16], mine, b_1[0:8]], axis=0)
    rows_u[...] = jnp.where(half_lane, u, pltpu.roll(u, 64, 1))
    v = jnp.concatenate(
        [
            jnp.where(near, b_before[8:16], b_1[56:64]),
            jnp.where(near, mine, b_2),
            jnp.where(near, b_1, b_3),
            jnp.where(near, b_2[0:8], b_4[0:8]),
        ],
        axis=0,
    ).reshape(9, 2, 8, 128)
    v_low = v[:, 0].reshape(72, 128)
    v_high = v[:, 1].reshape(72, 128)
    cols_v[...] = jnp.where(half_lane, pltpu.roll(v_low, 64, 1), v_high)

    def pair_step(aq, carry):
        row = pl.multiple_of(aq * 64, 64)
        here = rows_u[pl.ds(pl.multiple_of(aq * 8, 8), 8), :]
        row_at = band * 8 + aq - 1
        row_in = (row_at >= 0) & (row_at < 128)
        for bp in range(9):
            block = first * 8 - 1 + 2 * bp
            spot = jnp.where(half_lane, block, block + 1)
            half = jnp.where((spot >= 0) & (spot < 128) & row_in, 0.5, 0.0)
            x = (here[:, None, :] + cols_v[bp * 8 : bp * 8 + 8, :][None, :, :]).reshape(64, 128)
            value, grade = gelu_parts(x, half)
            pair[pl.ds(row, 64), bp * 128 : bp * 128 + 128] = value.astype(BF16)
            slope[pl.ds(row, 64), bp * 128 : bp * 128 + 128] = grade
        return carry

    lax.fori_loop(0, 10, pair_step, 0)

    bias2 = small[0:1, :]
    out_w2 = small[1:2, :]
    zero8 = jnp.zeros((8, 128), F32)
    totals = (zero8, zero8, zero8)
    for bp in range(8):
        lane = bp * 128
        pre[...] = (
            dot(pair[0:512, lane : lane + 256], fwd_w[0:256, :])
            + dot(pair[64:576, lane : lane + 256], fwd_w[256:512, :])
            + dot(pair[128:640, lane : lane + 256], fwd_w[512:768, :])
        )

        def act_step(aq, carry):
            row = pl.ds(pl.multiple_of(aq * 64, 64), 64)
            value, grade = gelu_parts(pre[row, :] + bias2, 0.5)
            hid32[row, :] = value
            hid16[row, :] = value.astype(BF16)
            weighted[row, :] = grade * out_w2
            return carry

        lax.fori_loop(0, 8, act_step, 0)
        low = hid16[...]
        guess[...] = dot(jnp.concatenate([low, low], axis=1), pred_w[...])

        def loss_step(aq, carry):
            loss_sum, bias_sum, out_sum = carry
            start = pl.multiple_of(aq * 64, 64)
            row = pl.ds(start, 64)
            weight = (row_mask[row, :].reshape(8, 8, 128) * col_mask[bp * 8 : bp * 8 + 8, :][None]).reshape(64, 128)
            residue = guess[row, :] - goal[row, lane : lane + 128]
            grad_pred = weight * residue
            grad_pre = grad_pred * weighted[row, :]
            grads[pl.ds(pl.multiple_of(start + 128, 64), 64), lane + 128 : lane + 256] = grad_pre.astype(BF16)
            loss_sum = loss_sum + jnp.sum((grad_pred * residue).reshape(8, 8, 128), axis=0)
            bias_sum = bias_sum + jnp.sum(grad_pre.reshape(8, 8, 128), axis=0)
            out_sum = out_sum + jnp.sum((grad_pred * hid32[row, :]).reshape(8, 8, 128), axis=0)
            return loss_sum, bias_sum, out_sum

        totals = lax.fori_loop(0, 8, loss_step, totals)

    for bp in range(8):
        lane = bp * 128
        turned = grads[128:640, lane + 128 : lane + 256].T
        for ty in range(3):
            part = dot(turned, pair[ty * 64 : ty * 64 + 512, lane : lane + 256])
            if bp == 0:
                grad_w[:, ty * 256 : ty * 256 + 256] = part
            else:
                grad_w[:, ty * 256 : ty * 256 + 256] += part

    for bp in range(9):
        lane = bp * 128
        part = (
            dot(grads[128:768, lane : lane + 256], bwd_w[0:256, :])
            + dot(grads[64:704, lane : lane + 256], bwd_w[256:512, :])
            + dot(grads[0:640, lane : lane + 256], bwd_w[512:768, :])
        ) * slope[:, lane : lane + 128]
        if bp == 0:
            grad_rows[...] = part
        else:
            grad_rows[...] += part
        grad_cols[bp * 8 : bp * 8 + 8, :] = jnp.sum(part.reshape(80, 8, 128), axis=0)

    row_part = jnp.sum(grad_rows[...].reshape(80, 8, 128), axis=1)
    row_part = jnp.where(half_lane, row_part + pltpu.roll(row_part, 64, 1), 0.0)
    bins[pl.ds(pl.multiple_of(band * 64 + 56, 8), 80), :] += row_part
    col_part = grad_cols[...]
    col_low = pltpu.roll(col_part, 64, 1).reshape(9, 1, 8, 128)
    col_part = jnp.concatenate([col_low, col_part.reshape(9, 1, 8, 128)], axis=1).reshape(144, 128)
    col_part = jnp.where(half_lane, 0.0, col_part)
    bins[pl.ds(pl.multiple_of(first * 64 + 56, 8), 144), :] += col_part
    out[:, 0:32, :] = bins[64:1088, :].reshape(32, 32, 128).astype(BF16)

    none8 = jnp.zeros((8, 128), F32)
    none48 = jnp.zeros((48, 128), F32)

    def if_near(x):
        return jnp.where(near, x, 0.0)

    def if_far(x):
        return jnp.where(near, 0.0, x)

    rows = jnp.concatenate(
        [
            none8,
            row_part[0:8] + if_near(col_part[0:8]),
            row_part[8:72] + if_near(col_part[8:72]),
            row_part[72:80] + if_near(col_part[72:80]),
            if_near(col_part[80:128]),
            jnp.where(near, col_part[128:136], col_part[0:8]),
            jnp.where(near, col_part[136:144], col_part[8:16]),
            if_far(col_part[16:72]),
            if_far(col_part[72:136]),
            if_far(col_part[136:144]),
            none8,
        ],
        axis=0,
    )
    proj_part = dot(rows.T.astype(BF16), feats)
    for k in range(8):
        out[k * 4 : k * 4 + 4, 32:64, :] = (
            proj_part[:, k * 128 : k * 128 + 128].reshape(4, 32, 128).astype(BF16)
        )

    taps = []
    for ty in range(3):
        taps.append(
            grad_w[0:64, ty * 256 : ty * 256 + 192] + grad_w[64:128, ty * 256 + 64 : ty * 256 + 256]
        )
    conv_grad = jnp.concatenate(taps, axis=1)
    wide = jnp.concatenate([conv_grad[:, k * 128 : k * 128 + 128] for k in range(4)], axis=0)
    last = jnp.concatenate([conv_grad[0:32, 512:576], conv_grad[32:64, 512:576]], axis=1)

    loss_sum, bias_sum, out_sum = totals
    bias_row = jnp.sum(bias_sum, axis=0, keepdims=True)
    bias_row = bias_row + pltpu.roll(bias_row, 64, 1)
    out_row = jnp.sum(out_sum, axis=0, keepdims=True)
    out_row = out_row + pltpu.roll(out_row, 64, 1)
    small_row = jnp.where(half_lane, bias_row, out_row)
    loss_row = jnp.broadcast_to(jnp.sum(loss_sum, keepdims=True) * (0.5 / 64.0), (1, 128))
    small_hi = small_row.astype(BF16).astype(F32)
    loss_hi = loss_row.astype(BF16).astype(F32)
    tail = jnp.concatenate(
        [small_hi, small_row - small_hi, loss_hi, loss_row - loss_hi, jnp.zeros((3, 128), F32)], axis=0
    )
    tail = jnp.broadcast_to(tail[None], (PEERS, 7, 128))
    rest = jnp.concatenate([last.reshape(PEERS, 1, 128), tail], axis=1)
    out[:, 64:80, :] = jnp.concatenate([wide.reshape(PEERS, 8, 128), rest], axis=1).astype(BF16)


def tile_call(*operands):
    shapes = [
        ((80, 128), F32), ((72, 128), F32), ((640, 1152), BF16), ((640, 1152), F32), ((768, 1280), BF16),
        ((512, 128), F32), ((512, 128), BF16), ((512, 128), F32), ((512, 128), F32), ((512, 128), F32),
        ((640, 128), F32), ((72, 128), F32), ((128, 768), F32), ((1408, 128), F32),
    ]
    return pl.pallas_call(
        tile_kernel,
        out_shape=jax.ShapeDtypeStruct((PEERS, 80, 128), BF16),
        in_specs=[pl.BlockSpec(memory_space=pltpu.VMEM)] * len(operands),
        out_specs=pl.BlockSpec(memory_space=pltpu.VMEM),
        scratch_shapes=[pltpu.VMEM(shape, kind) for shape, kind in shapes],
        compiler_params=pltpu.CompilerParams(vmem_limit_bytes=40 * 2**20),
        cost_estimate=pl.CostEstimate(flops=2 * 10**9, bytes_accessed=10**6, transcendentals=10**6),
        name="tiles",
    )(*operands)


def sum_kernel(parts, out, mine, small):
    total = jnp.sum(parts[...].astype(F32), axis=0)
    out[...] = jnp.broadcast_to(total[32:80].astype(BF16)[None], (PEERS, SLOT, 128))
    mine[...] = total[0:32].astype(BF16)
    small[0:1, :] = total[73:74] + total[74:75]
    small[1:2, :] = total[75:76] + total[76:77]


def sum_call(parts):
    return pl.pallas_call(
        sum_kernel,
        out_shape=(
            jax.ShapeDtypeStruct((PEERS, SLOT, 128), BF16),
            jax.ShapeDtypeStruct((32, 128), BF16),
            jax.ShapeDtypeStruct((2, 128), F32),
        ),
        in_specs=[pl.BlockSpec(memory_space=pltpu.VMEM)],
        out_specs=(pl.BlockSpec(memory_space=pltpu.VMEM),) * 3,
        name="sums",
    )(parts)


def final_kernel(every, grad_proj, grad_conv_t):
    for k in range(8):
        block = every[k * 4 : k * 4 + 4, 0:32, :].astype(F32).reshape(128, 128)
        grad_proj[k * 128 : k * 128 + 128, :] = block.T
    conv = every[:, 32:48, :].astype(F32)
    wide = conv[:, 0:8].reshape(256, 128)
    for k in range(4):
        grad_conv_t[:, k * 128 : k * 128 + 128] = wide[k * 64 : k * 64 + 64]
    last = conv[:, 8]
    grad_conv_t[0:32, 512:576] = last[:, 0:64]
    grad_conv_t[32:64, 512:576] = last[:, 64:128]


def final_call(every):
    return pl.pallas_call(
        final_kernel,
        out_shape=(jax.ShapeDtypeStruct((1024, 128), F32), jax.ShapeDtypeStruct((64, 576), F32)),
        in_specs=[pl.BlockSpec(memory_space=pltpu.VMEM)],
        out_specs=(pl.BlockSpec(memory_space=pltpu.VMEM),) * 2,
        name="outputs",
    )(every)


def body(feats, w_proj, conv_w, conv_b, w_out, target, mask):
    bands = lax.axis_size("band")

    def moved(x, by, offs=(0, 1)):
        pairs = [(2 * i + o, 2 * (i - by) + o) for i in range(bands) for o in offs if 0 <= i - by < bands]
        return lax.ppermute(x, GROUP, pairs)

    before = moved(feats[48:64], -1)
    after1 = moved(feats, 1)
    after2 = moved(feats, 2)
    after3 = moved(feats, 3, (1,))
    after4 = moved(feats[0:16], 4, (1,))
    ready = prep_call(
        mask.reshape(8, 128), target, conv_w.T, conv_b.reshape(1, 64), w_out.reshape(1, 64)
    )
    sent = tile_call(feats, before, after1, after2, after3, after4, w_proj, *ready)
    parts = lax.all_to_all(sent, GROUP, 0, 0, tiled=True)
    sums, mine, small = sum_call(parts)
    every = lax.all_to_all(sums, GROUP, 0, 0, tiled=True)
    grad_feats = lax.dot_general(
        mine, w_proj, (((1,), (1,)), ((), ())), preferred_element_type=F32
    ).astype(BF16)
    grad_proj, grad_conv_t = final_call(every)
    return (small[1, 0:1], grad_proj, grad_conv_t.T, small[0, 0:64], small[0, 64:128], grad_feats)


def solution(mesh):
    placed = (
        P(("rep", "band"), None),
        P(),
        P(),
        P(),
        P(),
        P(("rep", "band"), "off", None),
        P("rep"),
    )
    return jax.shard_map(
        body,
        mesh=mesh,
        in_specs=placed,
        out_specs=(
            P("rep"),
            P("rep", None),
            P("rep", None),
            P("rep"),
            P("rep"),
            P(("rep", "band", "off"), None),
        ),
        check_vma=False,
    )
```

```python
import jax
import jax.numpy as jnp
from jax import lax
from jax.experimental import pallas as pl
from jax.experimental.pallas import tpu as pltpu
from jax.sharding import PartitionSpec as P

GELU_K = 0.7978845608028654
GELU_C = 0.044715
GROUP = ("band", "off")
PEERS = 32
BANDS = 16
F32 = jnp.float32
BF16 = jnp.bfloat16


def gelu_parts(x, half):
    square = x * x
    t = jnp.tanh(x * (GELU_K + (GELU_K * GELU_C) * square))
    one_plus = 1.0 + t
    scaled = x * half
    value = scaled * one_plus
    slope = one_plus * (half + (scaled * (1.0 - t)) * (GELU_K + (3.0 * GELU_K * GELU_C) * square))
    return value, slope


def lane_ids(shape):
    return lax.broadcasted_iota(jnp.int32, shape, len(shape) - 1)


def row_ids(shape):
    return lax.broadcasted_iota(jnp.int32, shape, len(shape) - 2)


def dot(a, b):
    return jnp.dot(a, b, preferred_element_type=F32)


def front_kernel(feats, w_proj, out):
    off = lax.axis_index("off")
    proj = dot(feats[...], w_proj[...]).astype(BF16)
    out[:, 0:64, :] = jnp.broadcast_to(proj[None], (BANDS, 64, 128))
    group = lane_ids((16, 128)) // 32
    for q in range(8):
        block = feats[:, q * 128 : q * 128 + 128].astype(F32)
        for half in range(2):
            piece = 2 * half + off
            packed = jnp.zeros((16, 128), F32)
            for g in range(4):
                turned = pltpu.roll(block[g * 16 : g * 16 + 16], lax.rem(g - piece + 4, 4) * 32, 1)
                packed = jnp.where(group == g, turned, packed)
            out[2 * q + half, 64:80, :] = packed.astype(BF16)


def front_call(feats, w_proj):
    return pl.pallas_call(
        front_kernel,
        out_shape=jax.ShapeDtypeStruct((BANDS, 80, 128), BF16),
        in_specs=[pl.BlockSpec(memory_space=pltpu.VMEM)] * 2,
        out_specs=pl.BlockSpec(memory_space=pltpu.VMEM),
        compiler_params=pltpu.CompilerParams(vmem_limit_bytes=16 * 2**20),
        name="front",
    )(feats, w_proj)


def prep_kernel(
    mask, target, conv_t, conv_b, w_out, fwd_w, bwd_w, pred_w, goal, row_mask, col_mask, small
):
    band = lax.axis_index("band")
    first = band + 2 * lax.axis_index("off")
    half_lane = lane_ids((1, 128)) < 64

    blank = jnp.zeros((64, 64), F32)
    for ty in range(3):
        taps = [conv_t[:, (3 * ty + tx) * 64 : (3 * ty + tx + 1) * 64].astype(F32) for tx in range(3)]
        low = jnp.concatenate(taps + [blank], axis=1)
        high = jnp.concatenate([blank] + taps, axis=1)
        fwd_w[ty * 256 : ty * 256 + 256, :] = jnp.concatenate([low, high], axis=0).T.astype(BF16)
        left = taps[::-1] + [blank]
        right = [blank] + taps[::-1]
        for k in range(4):
            row = ty * 256 + k * 64
            bwd_w[row : row + 64, :] = jnp.concatenate([left[k], right[k]], axis=1).astype(BF16)

    bias2 = jnp.concatenate([conv_b[...], conv_b[...]], axis=1)
    twice = jnp.concatenate([w_out[...], w_out[...]], axis=1)
    small[...] = jnp.concatenate([bias2, twice, jnp.zeros((6, 128), F32)], axis=0)
    diagonal = row_ids((128, 128)) == lane_ids((128, 128))
    halves = (row_ids((128, 128)) < 64) == (lane_ids((128, 128)) < 64)
    twice_hi = twice.astype(BF16).astype(F32)
    halves_b = halves.astype(F32).astype(BF16)
    for k, part in enumerate((twice_hi, twice - twice_hi)):
        line = jnp.where(diagonal, part, 0.0).astype(BF16)
        pred_w[k * 128 : k * 128 + 128, :] = dot(line, halves_b).astype(BF16)

    mask_all = mask[...].astype(F32)
    mask_lane = lane_ids((8, 128))
    by_band = jnp.concatenate(
        [jnp.where(mask_lane < 64, mask_all, 0.0), jnp.where(mask_lane < 64, 0.0, mask_all)], axis=0
    ).astype(BF16)
    sums_row = dot(by_band, jnp.ones((128, 128), BF16))
    sums_col = lax.dot_general(
        jnp.ones((16, 128), BF16), by_band, (((1,), (1,)), ((), ())), preferred_element_type=F32
    )
    at = lax.broadcasted_iota(jnp.int32, (16, 16), 0)
    to = lax.broadcasted_iota(jnp.int32, (16, 16), 1)
    apart = (2 * (to % 8) + to // 8) - (2 * (at % 8) + at // 8)
    near_diagonal = (apart >= 0) & (apart < 4)
    count = jnp.sum(jnp.where(near_diagonal, sums_row[:, 0:16] * sums_col, 0.0))
    scale = 1.0 / count

    def mask_rows(which):
        inside = jnp.minimum(which, 15)
        line = mask[pl.ds(inside // 2, 1), :].astype(F32)
        line = jnp.where(which < 16, line, 0.0)
        spot = row_ids((64, 128)) + 64 * (inside % 2)
        spread = jnp.where(lane_ids((64, 128)) == spot, line, 0.0)
        return dot(spread.astype(BF16), jnp.ones((128, 128), BF16))

    row_mask[...] = (
        jnp.broadcast_to(mask_rows(band)[:, None, :] * (2.0 * scale), (64, 8, 128)).reshape(512, 128)
    )
    col_all = jnp.concatenate([mask_rows(first), mask_rows(first + 1)], axis=0).reshape(8, 2, 8, 128)
    col_mask[...] = jnp.where(half_lane, col_all[:, 0].reshape(64, 128), col_all[:, 1].reshape(64, 128))

    line = jnp.concatenate([target[:, 0, :], target[:, 1, :]], axis=1)
    lines = jnp.broadcast_to(line[:, None, :], (64, 8, 128)).reshape(512, 128)
    lines = jnp.where(lane_ids((512, 128)) % 8 == row_ids((512, 128)) % 8, lines, 0.0)
    lines_hi = lines.astype(BF16)
    lines_lo = (lines - lines_hi.astype(F32)).astype(BF16)
    spread = (
        (row_ids((128, 1024)) // 8 == lane_ids((128, 1024)) // 64).astype(F32).astype(BF16)
    )
    goal[...] = dot(
        jnp.concatenate([lines_hi, lines_lo], axis=1), jnp.concatenate([spread, spread], axis=0)
    )


def prep_call(*operands):
    shapes = [
        ((768, 128), BF16), ((768, 128), BF16), ((256, 128), BF16), ((512, 1024), F32), ((512, 128), F32),
        ((64, 128), F32), ((8, 128), F32),
    ]
    return pl.pallas_call(
        prep_kernel,
        out_shape=tuple(jax.ShapeDtypeStruct(shape, kind) for shape, kind in shapes),
        in_specs=[pl.BlockSpec(memory_space=pltpu.VMEM)] * len(operands),
        out_specs=(pl.BlockSpec(memory_space=pltpu.VMEM),) * len(shapes),
        compiler_params=pltpu.CompilerParams(vmem_limit_bytes=16 * 2**20),
        cost_estimate=pl.CostEstimate(flops=3 * 10**8, bytes_accessed=4 * 10**6, transcendentals=0),
        name="prepare",
    )(*operands)


def tile_kernel(
    proj, fwd_w, bwd_w, pred_w, goal, row_mask, col_mask, small,
    out,
    rows_u, cols_v, pair, slope, grads, pre, hid16, hid32, weighted, guess, grad_rows, grad_cols, grad_w,
):
    band = lax.axis_index("band")
    first = band + 2 * lax.axis_index("off")
    half_lane = lane_ids((1, 128)) < 64

    zero_rows = jnp.zeros((128, 1280), BF16)
    grads[0:128, :] = zero_rows
    grads[640:768, :] = zero_rows
    grads[128:640, 0:128] = jnp.zeros((512, 128), BF16)
    grads[128:640, 1152:1280] = jnp.zeros((512, 128), BF16)

    def ending(which):
        return proj[jnp.clip(which, 0, BANDS - 1), 48:64, :].astype(F32)[8:16]

    def whole(which):
        return proj[jnp.minimum(which, BANDS - 1), 0:64, :].astype(F32)

    def opening(which):
        return proj[jnp.minimum(which, BANDS - 1), 0:16, :].astype(F32)[0:8]

    u = jnp.concatenate([ending(band - 1), whole(band), opening(band + 1)], axis=0)
    rows_u[...] = jnp.where(half_lane, u, pltpu.roll(u, 64, 1))
    v = jnp.concatenate(
        [ending(first - 1), whole(first), whole(first + 1), opening(first + 2)], axis=0
    ).reshape(9, 2, 8, 128)
    v_low = v[:, 0].reshape(72, 128)
    v_high = v[:, 1].reshape(72, 128)
    cols_v[...] = jnp.where(half_lane, pltpu.roll(v_low, 64, 1), v_high)

    def pair_step(aq, carry):
        row = pl.multiple_of(aq * 64, 64)
        here = rows_u[pl.ds(pl.multiple_of(aq * 8, 8), 8), :]
        row_at = band * 8 + aq - 1
        row_in = (row_at >= 0) & (row_at < 128)
        for bp in range(9):
            block = first * 8 - 1 + 2 * bp
            spot = jnp.where(half_lane, block, block + 1)
            half = jnp.where((spot >= 0) & (spot < 128) & row_in, 0.5, 0.0)
            x = (here[:, None, :] + cols_v[bp * 8 : bp * 8 + 8, :][None, :, :]).reshape(64, 128)
            value, grade = gelu_parts(x, half)
            pair[pl.ds(row, 64), bp * 128 : bp * 128 + 128] = value.astype(BF16)
            slope[pl.ds(row, 64), bp * 128 : bp * 128 + 128] = grade
        return carry

    lax.fori_loop(0, 10, pair_step, 0)

    bias2 = small[0:1, :]
    out_w2 = small[1:2, :]
    zero8 = jnp.zeros((8, 128), F32)
    totals = (zero8, zero8, zero8)
    for bp in range(8):
        lane = bp * 128
        pre[...] = (
            dot(pair[0:512, lane : lane + 256], fwd_w[0:256, :])
            + dot(pair[64:576, lane : lane + 256], fwd_w[256:512, :])
            + dot(pair[128:640, lane : lane + 256], fwd_w[512:768, :])
        )

        def act_step(aq, carry):
            row = pl.ds(pl.multiple_of(aq * 64, 64), 64)
            value, grade = gelu_parts(pre[row, :] + bias2, 0.5)
            hid32[row, :] = value
            hid16[row, :] = value.astype(BF16)
            weighted[row, :] = grade * out_w2
            return carry

        lax.fori_loop(0, 8, act_step, 0)
        low = hid16[...]
        guess[...] = dot(jnp.concatenate([low, low], axis=1), pred_w[...])

        def loss_step(aq, carry):
            loss_sum, bias_sum, out_sum = carry
            start = pl.multiple_of(aq * 64, 64)
            row = pl.ds(start, 64)
            weight = (row_mask[row, :].reshape(8, 8, 128) * col_mask[bp * 8 : bp * 8 + 8, :][None]).reshape(64, 128)
            residue = guess[row, :] - goal[row, lane : lane + 128]
            grad_pred = weight * residue
            grad_pre = grad_pred * weighted[row, :]
            grads[pl.ds(pl.multiple_of(start + 128, 64), 64), lane + 128 : lane + 256] = grad_pre.astype(BF16)
            loss_sum = loss_sum + jnp.sum((grad_pred * residue).reshape(8, 8, 128), axis=0)
            bias_sum = bias_sum + jnp.sum(grad_pre.reshape(8, 8, 128), axis=0)
            out_sum = out_sum + jnp.sum((grad_pred * hid32[row, :]).reshape(8, 8, 128), axis=0)
            return loss_sum, bias_sum, out_sum

        totals = lax.fori_loop(0, 8, loss_step, totals)

    for bp in range(8):
        lane = bp * 128
        turned = grads[128:640, lane + 128 : lane + 256].T
        for ty in range(3):
            part = dot(turned, pair[ty * 64 : ty * 64 + 512, lane : lane + 256])
            if bp == 0:
                grad_w[:, ty * 256 : ty * 256 + 256] = part
            else:
                grad_w[:, ty * 256 : ty * 256 + 256] += part

    for bp in range(9):
        lane = bp * 128
        part = (
            dot(grads[128:768, lane : lane + 256], bwd_w[0:256, :])
            + dot(grads[64:704, lane : lane + 256], bwd_w[256:512, :])
            + dot(grads[0:640, lane : lane + 256], bwd_w[512:768, :])
        ) * slope[:, lane : lane + 128]
        if bp == 0:
            grad_rows[...] = part
        else:
            grad_rows[...] += part
        grad_cols[bp * 8 : bp * 8 + 8, :] = jnp.sum(part.reshape(80, 8, 128), axis=0)

    row_part = jnp.sum(grad_rows[...].reshape(80, 8, 128), axis=1)
    row_part = row_part + pltpu.roll(row_part, 64, 1)
    col_part = grad_cols[...]
    col_low = pltpu.roll(col_part, 64, 1).reshape(9, 1, 8, 128)
    col_part = jnp.concatenate([col_low, col_part.reshape(9, 1, 8, 128)], axis=1).reshape(144, 128)
    spare = pltpu.roll(col_part[112:144], 64, 1)
    packed = jnp.where(half_lane, jnp.concatenate([row_part, spare], axis=0), col_part[0:112])
    out[:, 0:112, :] = jnp.broadcast_to(packed.astype(BF16)[None], (PEERS, 112, 128))

    taps = []
    for ty in range(3):
        taps.append(
            grad_w[0:64, ty * 256 : ty * 256 + 192] + grad_w[64:128, ty * 256 + 64 : ty * 256 + 256]
        )
    conv_grad = jnp.concatenate(taps, axis=1)
    wide = jnp.concatenate([conv_grad[:, k * 128 : k * 128 + 128] for k in range(4)], axis=0)
    last = jnp.concatenate([conv_grad[0:32, 512:576], conv_grad[32:64, 512:576]], axis=1)

    loss_sum, bias_sum, out_sum = totals
    bias_row = jnp.sum(bias_sum, axis=0, keepdims=True)
    bias_row = bias_row + pltpu.roll(bias_row, 64, 1)
    out_row = jnp.sum(out_sum, axis=0, keepdims=True)
    out_row = out_row + pltpu.roll(out_row, 64, 1)
    small_row = jnp.where(half_lane, bias_row, out_row)
    loss_row = jnp.broadcast_to(jnp.sum(loss_sum, keepdims=True) * (0.5 / 64.0), (1, 128))
    small_hi = small_row.astype(BF16).astype(F32)
    loss_hi = loss_row.astype(BF16).astype(F32)
    tail = jnp.concatenate(
        [small_hi, small_row - small_hi, loss_hi, loss_row - loss_hi, jnp.zeros((3, 128), F32)], axis=0
    )
    tail = jnp.broadcast_to(tail[None], (PEERS, 7, 128))
    rest = jnp.concatenate([last.reshape(PEERS, 1, 128), tail], axis=1)
    out[:, 112:128, :] = jnp.concatenate([wide.reshape(PEERS, 8, 128), rest], axis=1).astype(BF16)


def tile_call(*operands):
    shapes = [
        ((80, 128), F32), ((72, 128), F32), ((640, 1152), BF16), ((640, 1152), F32), ((768, 1280), BF16),
        ((512, 128), F32), ((512, 128), BF16), ((512, 128), F32), ((512, 128), F32), ((512, 128), F32),
        ((640, 128), F32), ((72, 128), F32), ((128, 768), F32),
    ]
    return pl.pallas_call(
        tile_kernel,
        out_shape=jax.ShapeDtypeStruct((PEERS, 128, 128), BF16),
        in_specs=[pl.BlockSpec(memory_space=pltpu.VMEM)] * len(operands),
        out_specs=pl.BlockSpec(memory_space=pltpu.VMEM),
        scratch_shapes=[pltpu.VMEM(shape, kind) for shape, kind in shapes],
        compiler_params=pltpu.CompilerParams(vmem_limit_bytes=40 * 2**20),
        cost_estimate=pl.CostEstimate(flops=2 * 10**9, bytes_accessed=10**6, transcendentals=10**6),
        name="tiles",
    )(*operands)


def sum_kernel(parts, cols, out, mine, small, bins):
    me = 2 * lax.axis_index("band") + lax.axis_index("off")
    half_lane = lane_ids((1, 128)) < 64
    bins[...] = jnp.zeros(bins.shape, F32)
    for band in range(BANDS):
        for off in range(2):
            piece = parts[2 * band + off, 0:112, :].astype(F32)
            bins[band * 64 + 56 : band * 64 + 136, :] += jnp.where(half_lane, piece[0:80], 0.0)
            start = (band + 2 * off) * 64 + 56
            bins[start : start + 112, :] += jnp.where(half_lane, 0.0, piece)
            spare = pltpu.roll(piece[80:112], 64, 1)
            bins[start + 112 : start + 144, :] += jnp.where(half_lane, 0.0, spare)
    gproj = bins[64:1088, :].astype(BF16).reshape(BANDS, 4, 16, 128)
    mine[...] = bins[pl.ds(pl.multiple_of(64 + 32 * me, 32), 32), :].astype(BF16)
    wide = jnp.concatenate([gproj[:, g].reshape(256, 128) for g in range(4)], axis=1)
    product = lax.dot_general(
        cols[:, 64:80, :].reshape(256, 128), wide, (((0,), (0,)), ((), ())), preferred_element_type=F32
    )
    rows = product[0:32, 0:128]
    for g in range(1, 4):
        rows = rows + product[g * 32 : g * 32 + 32, g * 128 : g * 128 + 128]
    total = jnp.sum(parts[:, 112:128, :].astype(F32), axis=0)
    out[:, 0:32, :] = jnp.broadcast_to(rows.astype(BF16)[None], (PEERS, 32, 128))
    out[:, 32:48, :] = jnp.broadcast_to(total.astype(BF16)[None], (PEERS, 16, 128))
    small[0:1, :] = total[9:10] + total[10:11]
    small[1:2, :] = total[11:12] + total[12:13]


def sum_call(parts, cols):
    return pl.pallas_call(
        sum_kernel,
        out_shape=(
            jax.ShapeDtypeStruct((PEERS, 48, 128), BF16),
            jax.ShapeDtypeStruct((32, 128), BF16),
            jax.ShapeDtypeStruct((2, 128), F32),
        ),
        in_specs=[pl.BlockSpec(memory_space=pltpu.VMEM)] * 2,
        out_specs=(pl.BlockSpec(memory_space=pltpu.VMEM),) * 3,
        scratch_shapes=[pltpu.VMEM((1408, 128), F32)],
        compiler_params=pltpu.CompilerParams(vmem_limit_bytes=16 * 2**20),
        name="sums",
    )(parts, cols)


def final_kernel(every, grad_proj, grad_conv_t):
    grad_proj[...] = every[:, 0:32, :].astype(F32).reshape(1024, 128)
    conv = every[:, 32:48, :].astype(F32)
    wide = conv[:, 0:8].reshape(256, 128)
    for k in range(4):
        grad_conv_t[:, k * 128 : k * 128 + 128] = wide[k * 64 : k * 64 + 64]
    last = conv[:, 8]
    grad_conv_t[0:32, 512:576] = last[:, 0:64]
    grad_conv_t[32:64, 512:576] = last[:, 64:128]


def final_call(every):
    return pl.pallas_call(
        final_kernel,
        out_shape=(jax.ShapeDtypeStruct((1024, 128), F32), jax.ShapeDtypeStruct((64, 576), F32)),
        in_specs=[pl.BlockSpec(memory_space=pltpu.VMEM)],
        out_specs=(pl.BlockSpec(memory_space=pltpu.VMEM),) * 2,
        name="outputs",
    )(every)


def body(feats, w_proj, conv_w, conv_b, w_out, target, mask):
    spread = lax.all_to_all(front_call(feats, w_proj), "band", 0, 0, tiled=True)
    ready = prep_call(
        mask.reshape(8, 128), target, conv_w.T, conv_b.reshape(1, 64), w_out.reshape(1, 64)
    )
    parts = lax.all_to_all(tile_call(spread, *ready), GROUP, 0, 0, tiled=True)
    sums, mine, small = sum_call(parts, spread)
    every = lax.all_to_all(sums, GROUP, 0, 0, tiled=True)
    grad_feats = lax.dot_general(
        mine, w_proj, (((1,), (1,)), ((), ())), preferred_element_type=F32
    ).astype(BF16)
    grad_proj, grad_conv_t = final_call(every)
    return (small[1, 0:1], grad_proj, grad_conv_t.T, small[0, 0:64], small[0, 64:128], grad_feats)


def solution(mesh):
    placed = (
        P(("rep", "band"), None),
        P(),
        P(),
        P(),
        P(),
        P(("rep", "band"), "off", None),
        P("rep"),
    )
    return jax.shard_map(
        body,
        mesh=mesh,
        in_specs=placed,
        out_specs=(
            P("rep"),
            P("rep", None),
            P("rep", None),
            P("rep"),
            P("rep"),
            P(("rep", "band", "off"), None),
        ),
        check_vma=False,
    )
```

```python
import jax
import jax.numpy as jnp
from jax import lax
from jax.experimental import pallas as pl
from jax.experimental.pallas import tpu as pltpu
from jax.sharding import PartitionSpec as P

GELU_K = 0.7978845608028654
GELU_C = 0.044715
GROUP = ("band", "off")
PEERS = 32
BANDS = 16
F32 = jnp.float32
BF16 = jnp.bfloat16


def gelu_parts(x, half):
    square = x * x
    t = jnp.tanh(x * (GELU_K + (GELU_K * GELU_C) * square))
    one_plus = 1.0 + t
    scaled = x * half
    value = scaled * one_plus
    slope = one_plus * (half + (scaled * (1.0 - t)) * (GELU_K + (3.0 * GELU_K * GELU_C) * square))
    return value, slope


def lane_ids(shape):
    return lax.broadcasted_iota(jnp.int32, shape, len(shape) - 1)


def row_ids(shape):
    return lax.broadcasted_iota(jnp.int32, shape, len(shape) - 2)


def dot(a, b):
    return jnp.dot(a, b, preferred_element_type=F32)


def front_kernel(feats, w_proj, out):
    off = lax.axis_index("off")
    proj = dot(feats[...], w_proj[...]).astype(BF16)
    out[:, 0:64, :] = jnp.broadcast_to(proj[None], (BANDS, 64, 128))
    group = lane_ids((16, 128)) // 32
    for q in range(8):
        block = feats[:, q * 128 : q * 128 + 128].astype(F32)
        for half in range(2):
            piece = 2 * half + off
            packed = jnp.zeros((16, 128), F32)
            for g in range(4):
                turned = pltpu.roll(block[g * 16 : g * 16 + 16], lax.rem(g - piece + 4, 4) * 32, 1)
                packed = jnp.where(group == g, turned, packed)
            out[2 * q + half, 64:80, :] = packed.astype(BF16)


def front_call(feats, w_proj):
    return pl.pallas_call(
        front_kernel,
        out_shape=jax.ShapeDtypeStruct((BANDS, 80, 128), BF16),
        in_specs=[pl.BlockSpec(memory_space=pltpu.VMEM)] * 2,
        out_specs=pl.BlockSpec(memory_space=pltpu.VMEM),
        compiler_params=pltpu.CompilerParams(vmem_limit_bytes=16 * 2**20),
        name="front",
    )(feats, w_proj)


def prep_kernel(
    mask, target, conv_t, conv_b, w_out, fwd_w, bwd_w, pred_w, goal, row_mask, col_mask, small
):
    band = lax.axis_index("band")
    first = band + 2 * lax.axis_index("off")
    half_lane = lane_ids((1, 128)) < 64

    blank = jnp.zeros((64, 64), F32)
    for ty in range(3):
        taps = [conv_t[:, (3 * ty + tx) * 64 : (3 * ty + tx + 1) * 64].astype(F32) for tx in range(3)]
        low = jnp.concatenate(taps + [blank], axis=1)
        high = jnp.concatenate([blank] + taps, axis=1)
        fwd_w[ty * 256 : ty * 256 + 256, :] = jnp.concatenate([low, high], axis=0).T.astype(BF16)
        left = taps[::-1] + [blank]
        right = [blank] + taps[::-1]
        for k in range(4):
            row = ty * 256 + k * 64
            bwd_w[row : row + 64, :] = jnp.concatenate([left[k], right[k]], axis=1).astype(BF16)

    bias2 = jnp.concatenate([conv_b[...], conv_b[...]], axis=1)
    twice = jnp.concatenate([w_out[...], w_out[...]], axis=1)
    small[...] = jnp.concatenate([bias2, twice, jnp.zeros((6, 128), F32)], axis=0)
    diagonal = row_ids((128, 128)) == lane_ids((128, 128))
    halves = (row_ids((128, 128)) < 64) == (lane_ids((128, 128)) < 64)
    twice_hi = twice.astype(BF16).astype(F32)
    halves_b = halves.astype(F32).astype(BF16)
    for k, part in enumerate((twice_hi, twice - twice_hi)):
        line = jnp.where(diagonal, part, 0.0).astype(BF16)
        pred_w[k * 128 : k * 128 + 128, :] = dot(line, halves_b).astype(BF16)

    mask_all = mask[...].astype(F32)
    mask_lane = lane_ids((8, 128))
    by_band = jnp.concatenate(
        [jnp.where(mask_lane < 64, mask_all, 0.0), jnp.where(mask_lane < 64, 0.0, mask_all)], axis=0
    ).astype(BF16)
    sums_row = dot(by_band, jnp.ones((128, 128), BF16))
    sums_col = lax.dot_general(
        jnp.ones((16, 128), BF16), by_band, (((1,), (1,)), ((), ())), preferred_element_type=F32
    )
    at = lax.broadcasted_iota(jnp.int32, (16, 16), 0)
    to = lax.broadcasted_iota(jnp.int32, (16, 16), 1)
    apart = (2 * (to % 8) + to // 8) - (2 * (at % 8) + at // 8)
    near_diagonal = (apart >= 0) & (apart < 4)
    count = jnp.sum(jnp.where(near_diagonal, sums_row[:, 0:16] * sums_col, 0.0))
    scale = 1.0 / count

    def mask_rows(which):
        inside = jnp.minimum(which, 15)
        line = mask[pl.ds(inside // 2, 1), :].astype(F32)
        line = jnp.where(which < 16, line, 0.0)
        spot = row_ids((64, 128)) + 64 * (inside % 2)
        spread = jnp.where(lane_ids((64, 128)) == spot, line, 0.0)
        return dot(spread.astype(BF16), jnp.ones((128, 128), BF16))

    row_mask[...] = (
        jnp.broadcast_to(mask_rows(band)[:, None, :] * (2.0 * scale), (64, 8, 128)).reshape(512, 128)
    )
    col_all = jnp.concatenate([mask_rows(first), mask_rows(first + 1)], axis=0).reshape(8, 2, 8, 128)
    col_mask[...] = jnp.where(half_lane, col_all[:, 0].reshape(64, 128), col_all[:, 1].reshape(64, 128))

    line = jnp.concatenate([target[:, 0, :], target[:, 1, :]], axis=1)
    lines = jnp.broadcast_to(line[:, None, :], (64, 8, 128)).reshape(512, 128)
    lines = jnp.where(lane_ids((512, 128)) % 8 == row_ids((512, 128)) % 8, lines, 0.0)
    lines_hi = lines.astype(BF16)
    lines_lo = (lines - lines_hi.astype(F32)).astype(BF16)
    spread = (
        (row_ids((128, 1024)) // 8 == lane_ids((128, 1024)) // 64).astype(F32).astype(BF16)
    )
    goal[...] = dot(
        jnp.concatenate([lines_hi, lines_lo], axis=1), jnp.concatenate([spread, spread], axis=0)
    )


def prep_call(*operands):
    shapes = [
        ((768, 128), BF16), ((768, 128), BF16), ((256, 128), BF16), ((512, 1024), F32), ((512, 128), F32),
        ((64, 128), F32), ((8, 128), F32),
    ]
    return pl.pallas_call(
        prep_kernel,
        out_shape=tuple(jax.ShapeDtypeStruct(shape, kind) for shape, kind in shapes),
        in_specs=[pl.BlockSpec(memory_space=pltpu.VMEM)] * len(operands),
        out_specs=(pl.BlockSpec(memory_space=pltpu.VMEM),) * len(shapes),
        compiler_params=pltpu.CompilerParams(vmem_limit_bytes=16 * 2**20),
        cost_estimate=pl.CostEstimate(flops=3 * 10**8, bytes_accessed=4 * 10**6, transcendentals=0),
        name="prepare",
    )(*operands)


def tile_kernel(
    proj, fwd_w, bwd_w, pred_w, goal, row_mask, col_mask, small,
    out,
    rows_u, cols_v, pair, slope, grads, pre, hid16, hid32, weighted, guess, grad_rows, grad_cols, grad_w,
):
    band = lax.axis_index("band")
    first = band + 2 * lax.axis_index("off")
    half_lane = lane_ids((1, 128)) < 64

    zero_rows = jnp.zeros((128, 1280), BF16)
    grads[0:128, :] = zero_rows
    grads[640:768, :] = zero_rows
    grads[128:640, 0:128] = jnp.zeros((512, 128), BF16)
    grads[128:640, 1152:1280] = jnp.zeros((512, 128), BF16)

    def ending(which):
        return proj[jnp.clip(which, 0, BANDS - 1), 48:64, :].astype(F32)[8:16]

    def whole(which):
        return proj[jnp.minimum(which, BANDS - 1), 0:64, :].astype(F32)

    def opening(which):
        return proj[jnp.minimum(which, BANDS - 1), 0:16, :].astype(F32)[0:8]

    u = jnp.concatenate([ending(band - 1), whole(band), opening(band + 1)], axis=0)
    rows_u[...] = jnp.where(half_lane, u, pltpu.roll(u, 64, 1))
    v = jnp.concatenate(
        [ending(first - 1), whole(first), whole(first + 1), opening(first + 2)], axis=0
    ).reshape(9, 2, 8, 128)
    v_low = v[:, 0].reshape(72, 128)
    v_high = v[:, 1].reshape(72, 128)
    cols_v[...] = jnp.where(half_lane, pltpu.roll(v_low, 64, 1), v_high)

    def pair_step(aq, carry):
        row = pl.multiple_of(aq * 64, 64)
        here = rows_u[pl.ds(pl.multiple_of(aq * 8, 8), 8), :]
        row_at = band * 8 + aq - 1
        row_in = (row_at >= 0) & (row_at < 128)
        for bp in range(9):
            block = first * 8 - 1 + 2 * bp
            spot = jnp.where(half_lane, block, block + 1)
            half = jnp.where((spot >= 0) & (spot < 128) & row_in, 0.5, 0.0)
            x = (here[:, None, :] + cols_v[bp * 8 : bp * 8 + 8, :][None, :, :]).reshape(64, 128)
            value, grade = gelu_parts(x, half)
            pair[pl.ds(row, 64), bp * 128 : bp * 128 + 128] = value.astype(BF16)
            slope[pl.ds(row, 64), bp * 128 : bp * 128 + 128] = grade
        return carry

    lax.fori_loop(0, 10, pair_step, 0)

    for bp in range(8):
        lane = bp * 128
        pre[:, lane : lane + 128] = (
            dot(pair[0:512, lane : lane + 256], fwd_w[0:256, :])
            + dot(pair[64:576, lane : lane + 256], fwd_w[256:512, :])
            + dot(pair[128:640, lane : lane + 256], fwd_w[512:768, :])
        )

    bias2 = small[0:1, :]
    out_w2 = small[1:2, :]

    def act_step(aq, carry):
        row = pl.ds(pl.multiple_of(aq * 64, 64), 64)
        for bp in range(8):
            lane = slice(bp * 128, bp * 128 + 128)
            value, grade = gelu_parts(pre[row, lane] + bias2, 0.5)
            hid32[row, lane] = value
            hid16[row, lane] = value.astype(BF16)
            weighted[row, lane] = grade * out_w2
        return carry

    lax.fori_loop(0, 8, act_step, 0)

    for bp in range(8):
        lane = slice(bp * 128, bp * 128 + 128)
        low = hid16[:, lane]
        guess[:, lane] = dot(jnp.concatenate([low, low], axis=1), pred_w[...])

    def loss_step(aq, carry):
        loss_sum, bias_sum, out_sum = carry
        start = pl.multiple_of(aq * 64, 64)
        row = pl.ds(start, 64)
        row_weight = row_mask[row, :].reshape(8, 8, 128)
        for bp in range(8):
            lane = slice(bp * 128, bp * 128 + 128)
            weight = (row_weight * col_mask[bp * 8 : bp * 8 + 8, :][None]).reshape(64, 128)
            residue = guess[row, lane] - goal[row, lane]
            grad_pred = weight * residue
            grad_pre = grad_pred * weighted[row, lane]
            grads[pl.ds(pl.multiple_of(start + 128, 64), 64), bp * 128 + 128 : bp * 128 + 256] = grad_pre.astype(BF16)
            loss_sum = loss_sum + jnp.sum((grad_pred * residue).reshape(8, 8, 128), axis=0)
            bias_sum = bias_sum + jnp.sum(grad_pre.reshape(8, 8, 128), axis=0)
            out_sum = out_sum + jnp.sum((grad_pred * hid32[row, lane]).reshape(8, 8, 128), axis=0)
        return loss_sum, bias_sum, out_sum

    zero8 = jnp.zeros((8, 128), F32)
    totals = lax.fori_loop(0, 8, loss_step, (zero8, zero8, zero8))

    for bp in range(8):
        lane = bp * 128
        turned = grads[128:640, lane + 128 : lane + 256].T
        for ty in range(3):
            part = dot(turned, pair[ty * 64 : ty * 64 + 512, lane : lane + 256])
            if bp == 0:
                grad_w[:, ty * 256 : ty * 256 + 256] = part
            else:
                grad_w[:, ty * 256 : ty * 256 + 256] += part

    for bp in range(9):
        lane = bp * 128
        part = (
            dot(grads[128:768, lane : lane + 256], bwd_w[0:256, :])
            + dot(grads[64:704, lane : lane + 256], bwd_w[256:512, :])
            + dot(grads[0:640, lane : lane + 256], bwd_w[512:768, :])
        ) * slope[:, lane : lane + 128]
        if bp == 0:
            grad_rows[...] = part
        else:
            grad_rows[...] += part
        grad_cols[bp * 8 : bp * 8 + 8, :] = jnp.sum(part.reshape(80, 8, 128), axis=0)

    row_part = jnp.sum(grad_rows[...].reshape(80, 8, 128), axis=1)
    row_part = row_part + pltpu.roll(row_part, 64, 1)
    col_part = grad_cols[...]
    col_low = pltpu.roll(col_part, 64, 1).reshape(9, 1, 8, 128)
    col_part = jnp.concatenate([col_low, col_part.reshape(9, 1, 8, 128)], axis=1).reshape(144, 128)
    spare = pltpu.roll(col_part[112:144], 64, 1)
    packed = jnp.where(half_lane, jnp.concatenate([row_part, spare], axis=0), col_part[0:112])
    out[:, 0:112, :] = jnp.broadcast_to(packed.astype(BF16)[None], (PEERS, 112, 128))

    taps = []
    for ty in range(3):
        taps.append(
            grad_w[0:64, ty * 256 : ty * 256 + 192] + grad_w[64:128, ty * 256 + 64 : ty * 256 + 256]
        )
    conv_grad = jnp.concatenate(taps, axis=1)
    wide = jnp.concatenate([conv_grad[:, k * 128 : k * 128 + 128] for k in range(4)], axis=0)
    last = jnp.concatenate([conv_grad[0:32, 512:576], conv_grad[32:64, 512:576]], axis=1)

    loss_sum, bias_sum, out_sum = totals
    bias_row = jnp.sum(bias_sum, axis=0, keepdims=True)
    bias_row = bias_row + pltpu.roll(bias_row, 64, 1)
    out_row = jnp.sum(out_sum, axis=0, keepdims=True)
    out_row = out_row + pltpu.roll(out_row, 64, 1)
    small_row = jnp.where(half_lane, bias_row, out_row)
    loss_row = jnp.broadcast_to(jnp.sum(loss_sum, keepdims=True) * (0.5 / 64.0), (1, 128))
    small_hi = small_row.astype(BF16).astype(F32)
    loss_hi = loss_row.astype(BF16).astype(F32)
    tail = jnp.concatenate(
        [small_hi, small_row - small_hi, loss_hi, loss_row - loss_hi, jnp.zeros((3, 128), F32)], axis=0
    )
    tail = jnp.broadcast_to(tail[None], (PEERS, 7, 128))
    rest = jnp.concatenate([last.reshape(PEERS, 1, 128), tail], axis=1)
    out[:, 112:128, :] = jnp.concatenate([wide.reshape(PEERS, 8, 128), rest], axis=1).astype(BF16)


def tile_call(*operands):
    shapes = [
        ((80, 128), F32), ((72, 128), F32), ((640, 1152), BF16), ((640, 1152), F32), ((768, 1280), BF16),
        ((512, 1024), F32), ((512, 1024), BF16), ((512, 1024), F32), ((512, 1024), F32), ((512, 1024), F32),
        ((640, 128), F32), ((72, 128), F32), ((128, 768), F32),
    ]
    return pl.pallas_call(
        tile_kernel,
        out_shape=jax.ShapeDtypeStruct((PEERS, 128, 128), BF16),
        in_specs=[pl.BlockSpec(memory_space=pltpu.VMEM)] * len(operands),
        out_specs=pl.BlockSpec(memory_space=pltpu.VMEM),
        scratch_shapes=[pltpu.VMEM(shape, kind) for shape, kind in shapes],
        compiler_params=pltpu.CompilerParams(vmem_limit_bytes=40 * 2**20),
        cost_estimate=pl.CostEstimate(flops=2 * 10**9, bytes_accessed=10**6, transcendentals=10**6),
        name="tiles",
    )(*operands)


def sum_kernel(parts, cols, out, mine, small, bins):
    me = 2 * lax.axis_index("band") + lax.axis_index("off")
    half_lane = lane_ids((1, 128)) < 64
    bins[...] = jnp.zeros(bins.shape, F32)
    for band in range(BANDS):
        for off in range(2):
            piece = parts[2 * band + off, 0:112, :].astype(F32)
            bins[band * 64 + 56 : band * 64 + 136, :] += jnp.where(half_lane, piece[0:80], 0.0)
            start = (band + 2 * off) * 64 + 56
            bins[start : start + 112, :] += jnp.where(half_lane, 0.0, piece)
            spare = pltpu.roll(piece[80:112], 64, 1)
            bins[start + 112 : start + 144, :] += jnp.where(half_lane, 0.0, spare)
    gproj = bins[64:1088, :].astype(BF16).reshape(BANDS, 4, 16, 128)
    mine[...] = bins[pl.ds(pl.multiple_of(64 + 32 * me, 32), 32), :].astype(BF16)
    wide = jnp.concatenate([gproj[:, g].reshape(256, 128) for g in range(4)], axis=1)
    product = lax.dot_general(
        cols[:, 64:80, :].reshape(256, 128), wide, (((0,), (0,)), ((), ())), preferred_element_type=F32
    )
    rows = product[0:32, 0:128]
    for g in range(1, 4):
        rows = rows + product[g * 32 : g * 32 + 32, g * 128 : g * 128 + 128]
    total = jnp.sum(parts[:, 112:128, :].astype(F32), axis=0)
    out[:, 0:32, :] = jnp.broadcast_to(rows.astype(BF16)[None], (PEERS, 32, 128))
    out[:, 32:48, :] = jnp.broadcast_to(total.astype(BF16)[None], (PEERS, 16, 128))
    small[0:1, :] = total[9:10] + total[10:11]
    small[1:2, :] = total[11:12] + total[12:13]


def sum_call(parts, cols):
    return pl.pallas_call(
        sum_kernel,
        out_shape=(
            jax.ShapeDtypeStruct((PEERS, 48, 128), BF16),
            jax.ShapeDtypeStruct((32, 128), BF16),
            jax.ShapeDtypeStruct((2, 128), F32),
        ),
        in_specs=[pl.BlockSpec(memory_space=pltpu.VMEM)] * 2,
        out_specs=(pl.BlockSpec(memory_space=pltpu.VMEM),) * 3,
        scratch_shapes=[pltpu.VMEM((1408, 128), F32)],
        compiler_params=pltpu.CompilerParams(vmem_limit_bytes=16 * 2**20),
        name="sums",
    )(parts, cols)


def final_kernel(every, grad_proj, grad_conv_t):
    grad_proj[...] = every[:, 0:32, :].astype(F32).reshape(1024, 128)
    conv = every[:, 32:48, :].astype(F32)
    wide = conv[:, 0:8].reshape(256, 128)
    for k in range(4):
        grad_conv_t[:, k * 128 : k * 128 + 128] = wide[k * 64 : k * 64 + 64]
    last = conv[:, 8]
    grad_conv_t[0:32, 512:576] = last[:, 0:64]
    grad_conv_t[32:64, 512:576] = last[:, 64:128]


def final_call(every):
    return pl.pallas_call(
        final_kernel,
        out_shape=(jax.ShapeDtypeStruct((1024, 128), F32), jax.ShapeDtypeStruct((64, 576), F32)),
        in_specs=[pl.BlockSpec(memory_space=pltpu.VMEM)],
        out_specs=(pl.BlockSpec(memory_space=pltpu.VMEM),) * 2,
        name="outputs",
    )(every)


def body(feats, w_proj, conv_w, conv_b, w_out, target, mask):
    spread = lax.all_to_all(front_call(feats, w_proj), "band", 0, 0, tiled=True)
    ready = prep_call(
        mask.reshape(8, 128), target, conv_w.T, conv_b.reshape(1, 64), w_out.reshape(1, 64)
    )
    parts = lax.all_to_all(tile_call(spread, *ready), GROUP, 0, 0, tiled=True)
    sums, mine, small = sum_call(parts, spread)
    every = lax.all_to_all(sums, GROUP, 0, 0, tiled=True)
    grad_feats = lax.dot_general(
        mine, w_proj, (((1,), (1,)), ((), ())), preferred_element_type=F32
    ).astype(BF16)
    grad_proj, grad_conv_t = final_call(every)
    return (small[1, 0:1], grad_proj, grad_conv_t.T, small[0, 0:64], small[0, 64:128], grad_feats)


def solution(mesh):
    placed = (
        P(("rep", "band"), None),
        P(),
        P(),
        P(),
        P(),
        P(("rep", "band"), "off", None),
        P("rep"),
    )
    return jax.shard_map(
        body,
        mesh=mesh,
        in_specs=placed,
        out_specs=(
            P("rep"),
            P("rep", None),
            P("rep", None),
            P("rep"),
            P("rep"),
            P(("rep", "band", "off"), None),
        ),
        check_vma=False,
    )
```

```python
import jax
import jax.numpy as jnp
from jax import lax
from jax.experimental import pallas as pl
from jax.experimental.pallas import tpu as pltpu
from jax.sharding import PartitionSpec as P

GELU_K = 0.7978845608028654
GELU_C = 0.044715
GROUP = ("band", "off")
PEERS = 32
BANDS = 16
F32 = jnp.float32
BF16 = jnp.bfloat16


def gelu_parts(x, half):
    square = x * x
    t = jnp.tanh(x * (GELU_K + (GELU_K * GELU_C) * square))
    one_plus = 1.0 + t
    scaled = x * half
    value = scaled * one_plus
    slope = one_plus * (half + (scaled * (1.0 - t)) * (GELU_K + (3.0 * GELU_K * GELU_C) * square))
    return value, slope


def lane_ids(shape):
    return lax.broadcasted_iota(jnp.int32, shape, len(shape) - 1)


def row_ids(shape):
    return lax.broadcasted_iota(jnp.int32, shape, len(shape) - 2)


def dot(a, b):
    return jnp.dot(a, b, preferred_element_type=F32)


def front_kernel(feats_hbm, w_proj_hbm, out, feats, w_proj, sems):
    off = lax.axis_index("off")
    get_feats = pltpu.make_async_copy(feats_hbm, feats, sems.at[0])
    get_w = pltpu.make_async_copy(w_proj_hbm, w_proj, sems.at[1])
    get_feats.start()
    get_w.start()
    get_feats.wait()
    group = lane_ids((16, 128)) // 32
    for q in range(8):
        block = feats[:, q * 128 : q * 128 + 128].astype(F32)
        for half in range(2):
            piece = 2 * half + off
            packed = jnp.zeros((16, 128), F32)
            for g in range(4):
                turned = pltpu.roll(block[g * 16 : g * 16 + 16], lax.rem(g - piece + 4, 4) * 32, 1)
                packed = jnp.where(group == g, turned, packed)
            out[2 * q + half, 64:80, :] = packed.astype(BF16)
    get_w.wait()
    proj = dot(feats[...], w_proj[...]).astype(BF16)
    out[:, 0:64, :] = jnp.broadcast_to(proj[None], (BANDS, 64, 128))


def front_call(feats, w_proj):
    return pl.pallas_call(
        front_kernel,
        out_shape=jax.ShapeDtypeStruct((BANDS, 80, 128), BF16),
        in_specs=[pl.BlockSpec(memory_space=pltpu.HBM)] * 2,
        out_specs=pl.BlockSpec(memory_space=pltpu.VMEM),
        scratch_shapes=[
            pltpu.VMEM((64, 1024), BF16),
            pltpu.VMEM((1024, 128), BF16),
            pltpu.SemaphoreType.DMA((2,)),
        ],
        compiler_params=pltpu.CompilerParams(vmem_limit_bytes=60 * 2**20),
        name="front",
    )(feats, w_proj)


def prep_kernel(
    mask, target, conv_t, conv_b, w_out, fwd_w, bwd_w, pred_w, goal, row_mask, col_mask, small
):
    band = lax.axis_index("band")
    first = band + 2 * lax.axis_index("off")
    half_lane = lane_ids((1, 128)) < 64

    blank = jnp.zeros((64, 64), F32)
    for ty in range(3):
        taps = [conv_t[:, (3 * ty + tx) * 64 : (3 * ty + tx + 1) * 64].astype(F32) for tx in range(3)]
        low = jnp.concatenate(taps + [blank], axis=1)
        high = jnp.concatenate([blank] + taps, axis=1)
        fwd_w[ty * 256 : ty * 256 + 256, :] = jnp.concatenate([low, high], axis=0).T.astype(BF16)
        left = taps[::-1] + [blank]
        right = [blank] + taps[::-1]
        for k in range(4):
            row = ty * 256 + k * 64
            bwd_w[row : row + 64, :] = jnp.concatenate([left[k], right[k]], axis=1).astype(BF16)

    bias2 = jnp.concatenate([conv_b[...], conv_b[...]], axis=1)
    twice = jnp.concatenate([w_out[...], w_out[...]], axis=1)
    small[...] = jnp.concatenate([bias2, twice, jnp.zeros((6, 128), F32)], axis=0)
    diagonal = row_ids((128, 128)) == lane_ids((128, 128))
    halves = (row_ids((128, 128)) < 64) == (lane_ids((128, 128)) < 64)
    twice_hi = twice.astype(BF16).astype(F32)
    halves_b = halves.astype(F32).astype(BF16)
    for k, part in enumerate((twice_hi, twice - twice_hi)):
        line = jnp.where(diagonal, part, 0.0).astype(BF16)
        pred_w[k * 128 : k * 128 + 128, :] = dot(line, halves_b).astype(BF16)

    mask_all = mask[...].astype(F32)
    mask_lane = lane_ids((8, 128))
    by_band = jnp.concatenate(
        [jnp.where(mask_lane < 64, mask_all, 0.0), jnp.where(mask_lane < 64, 0.0, mask_all)], axis=0
    ).astype(BF16)
    sums_row = dot(by_band, jnp.ones((128, 128), BF16))
    sums_col = lax.dot_general(
        jnp.ones((16, 128), BF16), by_band, (((1,), (1,)), ((), ())), preferred_element_type=F32
    )
    at = lax.broadcasted_iota(jnp.int32, (16, 16), 0)
    to = lax.broadcasted_iota(jnp.int32, (16, 16), 1)
    apart = (2 * (to % 8) + to // 8) - (2 * (at % 8) + at // 8)
    near_diagonal = (apart >= 0) & (apart < 4)
    count = jnp.sum(jnp.where(near_diagonal, sums_row[:, 0:16] * sums_col, 0.0))
    scale = 1.0 / count

    def mask_rows(which):
        inside = jnp.minimum(which, 15)
        line = mask[pl.ds(inside // 2, 1), :].astype(F32)
        line = jnp.where(which < 16, line, 0.0)
        spot = row_ids((64, 128)) + 64 * (inside % 2)
        spread = jnp.where(lane_ids((64, 128)) == spot, line, 0.0)
        return dot(spread.astype(BF16), jnp.ones((128, 128), BF16))

    row_mask[...] = (
        jnp.broadcast_to(mask_rows(band)[:, None, :] * (2.0 * scale), (64, 8, 128)).reshape(512, 128)
    )
    col_all = jnp.concatenate([mask_rows(first), mask_rows(first + 1)], axis=0).reshape(8, 2, 8, 128)
    col_mask[...] = jnp.where(half_lane, col_all[:, 0].reshape(64, 128), col_all[:, 1].reshape(64, 128))

    line = jnp.concatenate([target[:, 0, :], target[:, 1, :]], axis=1)
    lines = jnp.broadcast_to(line[:, None, :], (64, 8, 128)).reshape(512, 128)
    lines = jnp.where(lane_ids((512, 128)) % 8 == row_ids((512, 128)) % 8, lines, 0.0)
    lines_hi = lines.astype(BF16)
    lines_lo = (lines - lines_hi.astype(F32)).astype(BF16)
    spread = (
        (row_ids((128, 1024)) // 8 == lane_ids((128, 1024)) // 64).astype(F32).astype(BF16)
    )
    goal[...] = dot(
        jnp.concatenate([lines_hi, lines_lo], axis=1), jnp.concatenate([spread, spread], axis=0)
    )


def prep_call(*operands):
    shapes = [
        ((768, 128), BF16), ((768, 128), BF16), ((256, 128), BF16), ((512, 1024), F32), ((512, 128), F32),
        ((64, 128), F32), ((8, 128), F32),
    ]
    return pl.pallas_call(
        prep_kernel,
        out_shape=tuple(jax.ShapeDtypeStruct(shape, kind) for shape, kind in shapes),
        in_specs=[pl.BlockSpec(memory_space=pltpu.VMEM)] * len(operands),
        out_specs=(pl.BlockSpec(memory_space=pltpu.VMEM),) * len(shapes),
        compiler_params=pltpu.CompilerParams(vmem_limit_bytes=16 * 2**20),
        cost_estimate=pl.CostEstimate(flops=3 * 10**8, bytes_accessed=4 * 10**6, transcendentals=0),
        name="prepare",
    )(*operands)


def tile_kernel(
    proj, fwd_w, bwd_w, pred_w, goal, row_mask, col_mask, small,
    out,
    rows_u, cols_v, pair, slope, grads, pre, hid16, hid32, weighted, guess, grad_rows, grad_cols, grad_w,
):
    band = lax.axis_index("band")
    first = band + 2 * lax.axis_index("off")
    half_lane = lane_ids((1, 128)) < 64

    zero_rows = jnp.zeros((128, 1280), BF16)
    grads[0:128, :] = zero_rows
    grads[640:768, :] = zero_rows
    grads[128:640, 0:128] = jnp.zeros((512, 128), BF16)
    grads[128:640, 1152:1280] = jnp.zeros((512, 128), BF16)

    def ending(which):
        return proj[jnp.clip(which, 0, BANDS - 1), 48:64, :].astype(F32)[8:16]

    def whole(which):
        return proj[jnp.minimum(which, BANDS - 1), 0:64, :].astype(F32)

    def opening(which):
        return proj[jnp.minimum(which, BANDS - 1), 0:16, :].astype(F32)[0:8]

    u = jnp.concatenate([ending(band - 1), whole(band), opening(band + 1)], axis=0)
    rows_u[...] = jnp.where(half_lane, u, pltpu.roll(u, 64, 1))
    v = jnp.concatenate(
        [ending(first - 1), whole(first), whole(first + 1), opening(first + 2)], axis=0
    ).reshape(9, 2, 8, 128)
    v_low = v[:, 0].reshape(72, 128)
    v_high = v[:, 1].reshape(72, 128)
    cols_v[...] = jnp.where(half_lane, pltpu.roll(v_low, 64, 1), v_high)

    bias2 = small[0:1, :]
    out_w2 = small[1:2, :]

    def pair_stage(bp):
        lane = slice(bp * 128, bp * 128 + 128)
        block = first * 8 - 1 + 2 * bp
        spot = jnp.where(half_lane, block, block + 1)
        col_in = jnp.where((spot >= 0) & (spot < 128), 0.5, 0.0)
        v_here = cols_v[bp * 8 : bp * 8 + 8, :][None]
        for aq in range(10):
            half = col_in
            if aq == 0:
                half = jnp.where(band == 0, 0.0, col_in)
            if aq == 9:
                half = jnp.where(band == BANDS - 1, 0.0, col_in)
            x = (rows_u[aq * 8 : aq * 8 + 8, :][:, None, :] + v_here).reshape(64, 128)
            value, grade = gelu_parts(x, half)
            pair[aq * 64 : aq * 64 + 64, lane] = value.astype(BF16)
            slope[aq * 64 : aq * 64 + 64, lane] = grade

    def conv_stage(bp):
        lane = bp * 128
        pre[:, lane : lane + 128] = (
            dot(pair[0:512, lane : lane + 256], fwd_w[0:256, :])
            + dot(pair[64:576, lane : lane + 256], fwd_w[256:512, :])
            + dot(pair[128:640, lane : lane + 256], fwd_w[512:768, :])
        )

    def act_stage(bp):
        lane = slice(bp * 128, bp * 128 + 128)
        for aq in range(8):
            row = slice(aq * 64, aq * 64 + 64)
            value, grade = gelu_parts(pre[row, lane] + bias2, 0.5)
            hid32[row, lane] = value
            hid16[row, lane] = value.astype(BF16)
            weighted[row, lane] = grade * out_w2

    def pred_stage(bp):
        lane = slice(bp * 128, bp * 128 + 128)
        low = hid16[:, lane]
        guess[:, lane] = dot(jnp.concatenate([low, low], axis=1), pred_w[...])

    def loss_stage(bp, sums):
        loss_sum, bias_sum, out_sum = sums
        lane = slice(bp * 128, bp * 128 + 128)
        col_weight = col_mask[bp * 8 : bp * 8 + 8, :][None]
        for aq in range(8):
            row = slice(aq * 64, aq * 64 + 64)
            weight = (row_mask[row, :].reshape(8, 8, 128) * col_weight).reshape(64, 128)
            residue = guess[row, lane] - goal[row, lane]
            grad_pred = weight * residue
            grad_pre = grad_pred * weighted[row, lane]
            grads[128 + aq * 64 : 192 + aq * 64, bp * 128 + 128 : bp * 128 + 256] = grad_pre.astype(BF16)
            loss_sum = loss_sum + jnp.sum((grad_pred * residue).reshape(8, 8, 128), axis=0)
            bias_sum = bias_sum + jnp.sum(grad_pre.reshape(8, 8, 128), axis=0)
            out_sum = out_sum + jnp.sum((grad_pred * hid32[row, lane]).reshape(8, 8, 128), axis=0)
        return loss_sum, bias_sum, out_sum

    def weights_stage(bp):
        lane = bp * 128
        turned = grads[128:640, lane + 128 : lane + 256].T
        for ty in range(3):
            part = dot(turned, pair[ty * 64 : ty * 64 + 512, lane : lane + 256])
            if bp == 0:
                grad_w[:, ty * 256 : ty * 256 + 256] = part
            else:
                grad_w[:, ty * 256 : ty * 256 + 256] += part

    def back_stage(bp):
        lane = bp * 128
        part = (
            dot(grads[128:768, lane : lane + 256], bwd_w[0:256, :])
            + dot(grads[64:704, lane : lane + 256], bwd_w[256:512, :])
            + dot(grads[0:640, lane : lane + 256], bwd_w[512:768, :])
        ) * slope[:, lane : lane + 128]
        if bp == 0:
            grad_rows[...] = part
        else:
            grad_rows[...] += part
        grad_cols[bp * 8 : bp * 8 + 8, :] = jnp.sum(part.reshape(80, 8, 128), axis=0)

    zero8 = jnp.zeros((8, 128), F32)
    totals = (zero8, zero8, zero8)
    for step in range(15):
        if 6 <= step:
            back_stage(step - 6)
        if 6 <= step < 14:
            weights_stage(step - 6)
        if 5 <= step < 13:
            totals = loss_stage(step - 5, totals)
        if 4 <= step < 12:
            pred_stage(step - 4)
        if 3 <= step < 11:
            act_stage(step - 3)
        if 2 <= step < 10:
            conv_stage(step - 2)
        if step < 9:
            pair_stage(step)

    row_part = jnp.sum(grad_rows[...].reshape(80, 8, 128), axis=1)
    row_part = row_part + pltpu.roll(row_part, 64, 1)
    col_part = grad_cols[...]
    col_low = pltpu.roll(col_part, 64, 1).reshape(9, 1, 8, 128)
    col_part = jnp.concatenate([col_low, col_part.reshape(9, 1, 8, 128)], axis=1).reshape(144, 128)
    spare = pltpu.roll(col_part[112:144], 64, 1)
    packed = jnp.where(half_lane, jnp.concatenate([row_part, spare], axis=0), col_part[0:112])
    out[:, 0:112, :] = jnp.broadcast_to(packed.astype(BF16)[None], (PEERS, 112, 128))

    taps = []
    for ty in range(3):
        taps.append(
            grad_w[0:64, ty * 256 : ty * 256 + 192] + grad_w[64:128, ty * 256 + 64 : ty * 256 + 256]
        )
    conv_grad = jnp.concatenate(taps, axis=1)
    wide = jnp.concatenate([conv_grad[:, k * 128 : k * 128 + 128] for k in range(4)], axis=0)
    last = jnp.concatenate([conv_grad[0:32, 512:576], conv_grad[32:64, 512:576]], axis=1)

    loss_sum, bias_sum, out_sum = totals
    bias_row = jnp.sum(bias_sum, axis=0, keepdims=True)
    bias_row = bias_row + pltpu.roll(bias_row, 64, 1)
    out_row = jnp.sum(out_sum, axis=0, keepdims=True)
    out_row = out_row + pltpu.roll(out_row, 64, 1)
    small_row = jnp.where(half_lane, bias_row, out_row)
    loss_row = jnp.broadcast_to(jnp.sum(loss_sum, keepdims=True) * (0.5 / 64.0), (1, 128))
    small_hi = small_row.astype(BF16).astype(F32)
    loss_hi = loss_row.astype(BF16).astype(F32)
    tail = jnp.concatenate(
        [small_hi, small_row - small_hi, loss_hi, loss_row - loss_hi, jnp.zeros((3, 128), F32)], axis=0
    )
    tail = jnp.broadcast_to(tail[None], (PEERS, 7, 128))
    rest = jnp.concatenate([last.reshape(PEERS, 1, 128), tail], axis=1)
    out[:, 112:128, :] = jnp.concatenate([wide.reshape(PEERS, 8, 128), rest], axis=1).astype(BF16)


def tile_call(*operands):
    shapes = [
        ((80, 128), F32), ((72, 128), F32), ((640, 1152), BF16), ((640, 1152), F32), ((768, 1280), BF16),
        ((512, 1024), F32), ((512, 1024), BF16), ((512, 1024), F32), ((512, 1024), F32), ((512, 1024), F32),
        ((640, 128), F32), ((72, 128), F32), ((128, 768), F32),
    ]
    return pl.pallas_call(
        tile_kernel,
        out_shape=jax.ShapeDtypeStruct((PEERS, 128, 128), BF16),
        in_specs=[pl.BlockSpec(memory_space=pltpu.VMEM)] * len(operands),
        out_specs=pl.BlockSpec(memory_space=pltpu.VMEM),
        scratch_shapes=[pltpu.VMEM(shape, kind) for shape, kind in shapes],
        compiler_params=pltpu.CompilerParams(vmem_limit_bytes=40 * 2**20),
        cost_estimate=pl.CostEstimate(flops=2 * 10**9, bytes_accessed=10**6, transcendentals=10**6),
        name="tiles",
    )(*operands)


def sum_kernel(parts, cols, out, mine, bias, w_out, loss, bins):
    me = 2 * lax.axis_index("band") + lax.axis_index("off")
    half_lane = lane_ids((1, 128)) < 64
    bins[...] = jnp.zeros(bins.shape, F32)
    for band in range(BANDS):
        for off in range(2):
            piece = parts[2 * band + off, 0:112, :].astype(F32)
            bins[band * 64 + 56 : band * 64 + 136, :] += jnp.where(half_lane, piece[0:80], 0.0)
            start = (band + 2 * off) * 64 + 56
            bins[start : start + 112, :] += jnp.where(half_lane, 0.0, piece)
            spare = pltpu.roll(piece[80:112], 64, 1)
            bins[start + 112 : start + 144, :] += jnp.where(half_lane, 0.0, spare)
    gproj = bins[64:1088, :].astype(BF16).reshape(BANDS, 4, 16, 128)
    mine[...] = bins[pl.ds(pl.multiple_of(64 + 32 * me, 32), 32), :].astype(BF16)
    wide = jnp.concatenate([gproj[:, g].reshape(256, 128) for g in range(4)], axis=1)
    product = lax.dot_general(
        cols[:, 64:80, :].reshape(256, 128), wide, (((0,), (0,)), ((), ())), preferred_element_type=F32
    )
    rows = product[0:32, 0:128]
    for g in range(1, 4):
        rows = rows + product[g * 32 : g * 32 + 32, g * 128 : g * 128 + 128]
    total = jnp.sum(parts[:, 112:128, :].astype(F32), axis=0)
    out[:, 0:32, :] = jnp.broadcast_to(rows.astype(BF16)[None], (PEERS, 32, 128))
    out[:, 32:48, :] = jnp.broadcast_to(total.astype(BF16)[None], (PEERS, 16, 128))
    small = total[9:10] + total[10:11]
    bias[...] = small[:, 0:64]
    w_out[...] = small[:, 64:128]
    loss[...] = (total[11:12] + total[12:13])[:, 0:1]


def sum_call(parts, cols):
    return pl.pallas_call(
        sum_kernel,
        out_shape=(
            jax.ShapeDtypeStruct((PEERS, 48, 128), BF16),
            jax.ShapeDtypeStruct((32, 128), BF16),
            jax.ShapeDtypeStruct((1, 64), F32),
            jax.ShapeDtypeStruct((1, 64), F32),
            jax.ShapeDtypeStruct((1, 1), F32),
        ),
        in_specs=[pl.BlockSpec(memory_space=pltpu.VMEM)] * 2,
        out_specs=(pl.BlockSpec(memory_space=pltpu.VMEM),) * 5,
        scratch_shapes=[pltpu.VMEM((1408, 128), F32)],
        compiler_params=pltpu.CompilerParams(vmem_limit_bytes=16 * 2**20),
        name="sums",
    )(parts, cols)


def final_kernel(every, grad_proj_hbm, grad_conv_hbm, grad_proj, grad_conv_t, sems):
    puts = []
    for k in range(4):
        rows = pl.ds(k * 256, 256)
        grad_proj[k * 256 : k * 256 + 256, :] = (
            every[k * 8 : k * 8 + 8, 0:32, :].astype(F32).reshape(256, 128)
        )
        puts.append(pltpu.make_async_copy(grad_proj.at[rows], grad_proj_hbm.at[rows], sems.at[k]))
        puts[k].start()
    conv = every[:, 32:48, :].astype(F32)
    wide = conv[:, 0:8].reshape(256, 128)
    for k in range(4):
        grad_conv_t[:, k * 128 : k * 128 + 128] = wide[k * 64 : k * 64 + 64]
    last = conv[:, 8]
    grad_conv_t[0:32, 512:576] = last[:, 0:64]
    grad_conv_t[32:64, 512:576] = last[:, 64:128]
    puts.append(pltpu.make_async_copy(grad_conv_t, grad_conv_hbm, sems.at[4]))
    puts[4].start()
    for put in puts:
        put.wait()


def final_call(every):
    return pl.pallas_call(
        final_kernel,
        out_shape=(jax.ShapeDtypeStruct((1024, 128), F32), jax.ShapeDtypeStruct((64, 576), F32)),
        in_specs=[pl.BlockSpec(memory_space=pltpu.VMEM)],
        out_specs=(pl.BlockSpec(memory_space=pltpu.HBM),) * 2,
        scratch_shapes=[
            pltpu.VMEM((1024, 128), F32),
            pltpu.VMEM((64, 576), F32),
            pltpu.SemaphoreType.DMA((5,)),
        ],
        compiler_params=pltpu.CompilerParams(vmem_limit_bytes=8 * 2**20),
        name="outputs",
    )(every)


def body(feats, w_proj, conv_w, conv_b, w_out, target, mask):
    spread = lax.all_to_all(front_call(feats, w_proj), "band", 0, 0, tiled=True)
    ready = prep_call(
        mask.reshape(8, 128), target, conv_w.T, conv_b.reshape(1, 64), w_out.reshape(1, 64)
    )
    parts = lax.all_to_all(tile_call(spread, *ready), GROUP, 0, 0, tiled=True)
    sums, mine, bias, w_out, loss = sum_call(parts, spread)
    every = lax.all_to_all(sums, GROUP, 0, 0, tiled=True)
    grad_feats = lax.dot_general(
        mine, w_proj, (((1,), (1,)), ((), ())), preferred_element_type=F32
    ).astype(BF16)
    grad_proj, grad_conv_t = final_call(every)
    return (loss.reshape(1), grad_proj, grad_conv_t.T, bias.reshape(64), w_out.reshape(64), grad_feats)


def solution(mesh):
    placed = (
        P(("rep", "band"), None),
        P(),
        P(),
        P(),
        P(),
        P(("rep", "band"), "off", None),
        P("rep"),
    )
    return jax.shard_map(
        body,
        mesh=mesh,
        in_specs=placed,
        out_specs=(
            P("rep"),
            P("rep", None),
            P("rep", None),
            P("rep"),
            P("rep"),
            P(("rep", "band", "off"), None),
        ),
        check_vma=False,
    )
```

```python
import jax
import jax.numpy as jnp
from jax import lax
from jax.experimental import pallas as pl
from jax.experimental.pallas import tpu as pltpu
from jax.sharding import PartitionSpec as P

GELU_K = 0.7978845608028654
GELU_C = 0.044715
GROUP = ("band", "off")
PEERS = 32
CHIPS = 16
BANDS = 16
F32 = jnp.float32
BF16 = jnp.bfloat16


def gelu_parts(x, half):
    square = x * x
    t = jnp.tanh(x * (GELU_K + (GELU_K * GELU_C) * square))
    one_plus = 1.0 + t
    scaled = x * half
    value = scaled * one_plus
    slope = one_plus * (half + (scaled * (1.0 - t)) * (GELU_K + (3.0 * GELU_K * GELU_C) * square))
    return value, slope


def lane_ids(shape):
    return lax.broadcasted_iota(jnp.int32, shape, len(shape) - 1)


def row_ids(shape):
    return lax.broadcasted_iota(jnp.int32, shape, len(shape) - 2)


def dot(a, b):
    return jnp.dot(a, b, preferred_element_type=F32)


def front_kernel(feats_hbm, w_proj_hbm, out, feats, w_proj, sems):
    off = lax.axis_index("off")
    get_feats = pltpu.make_async_copy(feats_hbm, feats, sems.at[0])
    get_w = pltpu.make_async_copy(w_proj_hbm, w_proj, sems.at[1])
    get_feats.start()
    get_w.start()
    get_feats.wait()
    half_lane = lane_ids((1, 128)) < 64
    for q in range(8):
        block = feats[:, q * 128 : q * 128 + 128].astype(F32)
        top, bottom = block[0:32], block[32:64]
        low = jnp.where(half_lane, top, pltpu.roll(bottom, 64, 1))
        high = jnp.where(half_lane, pltpu.roll(top, 64, 1), bottom)
        packed = jnp.where(off == 0, low, high).astype(BF16)
        out[2 * q, 64:96, :] = packed
        out[2 * q + 1, 64:96, :] = packed
    get_w.wait()
    proj = dot(feats[...], w_proj[...]).astype(BF16)
    out[:, 0:64, :] = jnp.broadcast_to(proj[None], (BANDS, 64, 128))


def front_call(feats, w_proj):
    return pl.pallas_call(
        front_kernel,
        out_shape=jax.ShapeDtypeStruct((BANDS, 96, 128), BF16),
        in_specs=[pl.BlockSpec(memory_space=pltpu.HBM)] * 2,
        out_specs=pl.BlockSpec(memory_space=pltpu.VMEM),
        scratch_shapes=[
            pltpu.VMEM((64, 1024), BF16),
            pltpu.VMEM((1024, 128), BF16),
            pltpu.SemaphoreType.DMA((2,)),
        ],
        compiler_params=pltpu.CompilerParams(vmem_limit_bytes=60 * 2**20),
        name="front",
    )(feats, w_proj)


def prep_kernel(
    mask, target, conv_t, conv_b, w_out, fwd_w, bwd_w, pred_w, goal, row_mask, col_mask, small
):
    band = lax.axis_index("band")
    first = band + 2 * lax.axis_index("off")
    half_lane = lane_ids((1, 128)) < 64

    blank = jnp.zeros((64, 64), F32)
    for ty in range(3):
        taps = [conv_t[:, (3 * ty + tx) * 64 : (3 * ty + tx + 1) * 64].astype(F32) for tx in range(3)]
        low = jnp.concatenate(taps + [blank], axis=1)
        high = jnp.concatenate([blank] + taps, axis=1)
        fwd_w[ty * 256 : ty * 256 + 256, :] = jnp.concatenate([low, high], axis=0).T.astype(BF16)
        left = taps[::-1] + [blank]
        right = [blank] + taps[::-1]
        for k in range(4):
            row = ty * 256 + k * 64
            bwd_w[row : row + 64, :] = jnp.concatenate([left[k], right[k]], axis=1).astype(BF16)

    bias2 = jnp.concatenate([conv_b[...], conv_b[...]], axis=1)
    twice = jnp.concatenate([w_out[...], w_out[...]], axis=1)
    small[...] = jnp.concatenate([bias2, twice, jnp.zeros((6, 128), F32)], axis=0)
    diagonal = row_ids((128, 128)) == lane_ids((128, 128))
    halves = (row_ids((128, 128)) < 64) == (lane_ids((128, 128)) < 64)
    twice_hi = twice.astype(BF16).astype(F32)
    halves_b = halves.astype(F32).astype(BF16)
    for k, part in enumerate((twice_hi, twice - twice_hi)):
        line = jnp.where(diagonal, part, 0.0).astype(BF16)
        pred_w[k * 128 : k * 128 + 128, :] = dot(line, halves_b).astype(BF16)

    mask_all = mask[...].astype(F32)
    mask_lane = lane_ids((8, 128))
    by_band = jnp.concatenate(
        [jnp.where(mask_lane < 64, mask_all, 0.0), jnp.where(mask_lane < 64, 0.0, mask_all)], axis=0
    ).astype(BF16)
    sums_row = dot(by_band, jnp.ones((128, 128), BF16))
    sums_col = lax.dot_general(
        jnp.ones((16, 128), BF16), by_band, (((1,), (1,)), ((), ())), preferred_element_type=F32
    )
    at = lax.broadcasted_iota(jnp.int32, (16, 16), 0)
    to = lax.broadcasted_iota(jnp.int32, (16, 16), 1)
    apart = (2 * (to % 8) + to // 8) - (2 * (at % 8) + at // 8)
    near_diagonal = (apart >= 0) & (apart < 4)
    count = jnp.sum(jnp.where(near_diagonal, sums_row[:, 0:16] * sums_col, 0.0))
    scale = 1.0 / count

    def mask_rows(which):
        inside = jnp.minimum(which, 15)
        line = mask[pl.ds(inside // 2, 1), :].astype(F32)
        line = jnp.where(which < 16, line, 0.0)
        spot = row_ids((64, 128)) + 64 * (inside % 2)
        spread = jnp.where(lane_ids((64, 128)) == spot, line, 0.0)
        return dot(spread.astype(BF16), jnp.ones((128, 128), BF16))

    row_mask[...] = (
        jnp.broadcast_to(mask_rows(band)[:, None, :] * (2.0 * scale), (64, 8, 128)).reshape(512, 128)
    )
    col_all = jnp.concatenate([mask_rows(first), mask_rows(first + 1)], axis=0).reshape(8, 2, 8, 128)
    col_mask[...] = jnp.where(half_lane, col_all[:, 0].reshape(64, 128), col_all[:, 1].reshape(64, 128))

    line = jnp.concatenate([target[:, 0, :], target[:, 1, :]], axis=1)
    lines = jnp.broadcast_to(line[:, None, :], (64, 8, 128)).reshape(512, 128)
    lines = jnp.where(lane_ids((512, 128)) % 8 == row_ids((512, 128)) % 8, lines, 0.0)
    lines_hi = lines.astype(BF16)
    lines_lo = (lines - lines_hi.astype(F32)).astype(BF16)
    spread = (
        (row_ids((128, 1024)) // 8 == lane_ids((128, 1024)) // 64).astype(F32).astype(BF16)
    )
    goal[...] = dot(
        jnp.concatenate([lines_hi, lines_lo], axis=1), jnp.concatenate([spread, spread], axis=0)
    )


def prep_call(*operands):
    shapes = [
        ((768, 128), BF16), ((768, 128), BF16), ((256, 128), BF16), ((512, 1024), F32), ((512, 128), F32),
        ((64, 128), F32), ((8, 128), F32),
    ]
    return pl.pallas_call(
        prep_kernel,
        out_shape=tuple(jax.ShapeDtypeStruct(shape, kind) for shape, kind in shapes),
        in_specs=[pl.BlockSpec(memory_space=pltpu.VMEM)] * len(operands),
        out_specs=(pl.BlockSpec(memory_space=pltpu.VMEM),) * len(shapes),
        compiler_params=pltpu.CompilerParams(vmem_limit_bytes=16 * 2**20),
        cost_estimate=pl.CostEstimate(flops=3 * 10**8, bytes_accessed=4 * 10**6, transcendentals=0),
        name="prepare",
    )(*operands)


def tile_kernel(
    proj, fwd_w, bwd_w, pred_w, goal, row_mask, col_mask, small,
    keep, send,
    rows_u, cols_v, pair, slope, grads, pre, hid16, hid32, weighted, guess, grad_rows, grad_cols, grad_w,
    place_u, place_v,
):
    band = lax.axis_index("band")
    first = band + 2 * lax.axis_index("off")
    half_lane = lane_ids((1, 128)) < 64

    zero_rows = jnp.zeros((128, 1280), BF16)
    grads[0:128, :] = zero_rows
    grads[640:768, :] = zero_rows
    grads[128:640, 0:128] = jnp.zeros((512, 128), BF16)
    grads[128:640, 1152:1280] = jnp.zeros((512, 128), BF16)

    def ending(which):
        return proj[jnp.clip(which, 0, BANDS - 1), 48:64, :].astype(F32)[8:16]

    def whole(which):
        return proj[jnp.minimum(which, BANDS - 1), 0:64, :].astype(F32)

    def opening(which):
        return proj[jnp.minimum(which, BANDS - 1), 0:16, :].astype(F32)[0:8]

    u = jnp.concatenate([ending(band - 1), whole(band), opening(band + 1)], axis=0)
    rows_u[...] = jnp.where(half_lane, u, pltpu.roll(u, 64, 1))
    v = jnp.concatenate(
        [ending(first - 1), whole(first), whole(first + 1), opening(first + 2)], axis=0
    ).reshape(9, 2, 8, 128)
    v_low = v[:, 0].reshape(72, 128)
    v_high = v[:, 1].reshape(72, 128)
    cols_v[...] = jnp.where(half_lane, pltpu.roll(v_low, 64, 1), v_high)

    bias2 = small[0:1, :]
    out_w2 = small[1:2, :]

    def pair_stage(bp):
        lane = slice(bp * 128, bp * 128 + 128)
        block = first * 8 - 1 + 2 * bp
        spot = jnp.where(half_lane, block, block + 1)
        col_in = jnp.where((spot >= 0) & (spot < 128), 0.5, 0.0)
        v_here = cols_v[bp * 8 : bp * 8 + 8, :][None]
        for aq in range(10):
            half = col_in
            if aq == 0:
                half = jnp.where(band == 0, 0.0, col_in)
            if aq == 9:
                half = jnp.where(band == BANDS - 1, 0.0, col_in)
            x = (rows_u[aq * 8 : aq * 8 + 8, :][:, None, :] + v_here).reshape(64, 128)
            value, grade = gelu_parts(x, half)
            pair[aq * 64 : aq * 64 + 64, lane] = value.astype(BF16)
            slope[aq * 64 : aq * 64 + 64, lane] = grade

    def conv_stage(bp):
        lane = bp * 128
        pre[:, lane : lane + 128] = (
            dot(pair[0:512, lane : lane + 256], fwd_w[0:256, :])
            + dot(pair[64:576, lane : lane + 256], fwd_w[256:512, :])
            + dot(pair[128:640, lane : lane + 256], fwd_w[512:768, :])
        )

    def act_stage(bp):
        lane = slice(bp * 128, bp * 128 + 128)
        for aq in range(8):
            row = slice(aq * 64, aq * 64 + 64)
            value, grade = gelu_parts(pre[row, lane] + bias2, 0.5)
            hid32[row, lane] = value
            hid16[row, lane] = value.astype(BF16)
            weighted[row, lane] = grade * out_w2

    def pred_stage(bp):
        lane = slice(bp * 128, bp * 128 + 128)
        low = hid16[:, lane]
        guess[:, lane] = dot(jnp.concatenate([low, low], axis=1), pred_w[...])

    def loss_stage(bp, sums):
        loss_sum, bias_sum, out_sum = sums
        lane = slice(bp * 128, bp * 128 + 128)
        col_weight = col_mask[bp * 8 : bp * 8 + 8, :][None]
        for aq in range(8):
            row = slice(aq * 64, aq * 64 + 64)
            weight = (row_mask[row, :].reshape(8, 8, 128) * col_weight).reshape(64, 128)
            residue = guess[row, lane] - goal[row, lane]
            grad_pred = weight * residue
            grad_pre = grad_pred * weighted[row, lane]
            grads[128 + aq * 64 : 192 + aq * 64, bp * 128 + 128 : bp * 128 + 256] = grad_pre.astype(BF16)
            loss_sum = loss_sum + jnp.sum((grad_pred * residue).reshape(8, 8, 128), axis=0)
            bias_sum = bias_sum + jnp.sum(grad_pre.reshape(8, 8, 128), axis=0)
            out_sum = out_sum + jnp.sum((grad_pred * hid32[row, lane]).reshape(8, 8, 128), axis=0)
        return loss_sum, bias_sum, out_sum

    def weights_stage(bp):
        lane = bp * 128
        turned = grads[128:640, lane + 128 : lane + 256].T
        for ty in range(3):
            part = dot(turned, pair[ty * 64 : ty * 64 + 512, lane : lane + 256])
            if bp == 0:
                grad_w[:, ty * 256 : ty * 256 + 256] = part
            else:
                grad_w[:, ty * 256 : ty * 256 + 256] += part

    def back_stage(bp):
        lane = bp * 128
        part = (
            dot(grads[128:768, lane : lane + 256], bwd_w[0:256, :])
            + dot(grads[64:704, lane : lane + 256], bwd_w[256:512, :])
            + dot(grads[0:640, lane : lane + 256], bwd_w[512:768, :])
        ) * slope[:, lane : lane + 128]
        if bp == 0:
            grad_rows[...] = part
        else:
            grad_rows[...] += part
        grad_cols[bp * 8 : bp * 8 + 8, :] = jnp.sum(part.reshape(80, 8, 128), axis=0)

    zero8 = jnp.zeros((8, 128), F32)
    totals = (zero8, zero8, zero8)
    for step in range(15):
        if 6 <= step:
            back_stage(step - 6)
        if 6 <= step < 14:
            weights_stage(step - 6)
        if 5 <= step < 13:
            totals = loss_stage(step - 5, totals)
        if 4 <= step < 12:
            pred_stage(step - 4)
        if 3 <= step < 11:
            act_stage(step - 3)
        if 2 <= step < 10:
            conv_stage(step - 2)
        if step < 9:
            pair_stage(step)

    row_part = jnp.sum(grad_rows[...].reshape(80, 8, 128), axis=1)
    core = band % 2
    place_u[...] = jnp.zeros(place_u.shape, F32)
    place_v[...] = jnp.zeros(place_v.shape, F32)
    place_u[pl.ds(pl.multiple_of(core * 64, 64), 80), :] = row_part + pltpu.roll(row_part, 64, 1)
    col_part = grad_cols[...]
    col_high = pltpu.roll(col_part, 64, 1).reshape(9, 1, 8, 128)
    place_v[pl.ds(pl.multiple_of(core * 64, 64), 144), :] = jnp.concatenate(
        [col_part.reshape(9, 1, 8, 128), col_high], axis=1
    ).reshape(144, 128)
    packed_u = jnp.where(half_lane, place_u[0:72, :], pltpu.roll(place_u[72:144, :], 64, 1))
    packed_v = jnp.where(half_lane, place_v[0:104, :], pltpu.roll(place_v[104:208, :], 64, 1))

    taps = []
    for ty in range(3):
        taps.append(
            grad_w[0:64, ty * 256 : ty * 256 + 192] + grad_w[64:128, ty * 256 + 64 : ty * 256 + 256]
        )
    conv_grad = jnp.concatenate(taps, axis=1)
    blocks = [conv_grad[:, k * 128 : k * 128 + 128] for k in range(4)]
    last = jnp.concatenate([conv_grad[0:32, 512:576], conv_grad[32:64, 512:576]], axis=1)

    loss_sum, bias_sum, out_sum = totals
    bias_row = jnp.sum(bias_sum, axis=0, keepdims=True)
    bias_row = bias_row + pltpu.roll(bias_row, 64, 1)
    out_row = jnp.sum(out_sum, axis=0, keepdims=True)
    out_row = out_row + pltpu.roll(out_row, 64, 1)
    small_row = jnp.where(half_lane, bias_row, out_row)
    loss_row = jnp.broadcast_to(jnp.sum(loss_sum, keepdims=True) * (0.5 / 64.0), (1, 128))
    small_hi = small_row.astype(BF16).astype(F32)
    loss_hi = loss_row.astype(BF16).astype(F32)
    tail = jnp.concatenate(
        [small_hi, small_row - small_hi, loss_hi, loss_row - loss_hi, jnp.zeros((4, 128), F32)], axis=0
    )
    first_core = jnp.concatenate([packed_u, last, blocks[2], blocks[3], tail], axis=0)
    second_core = jnp.concatenate([packed_v, blocks[0], blocks[1], tail], axis=0)
    keep[...] = jnp.where(core == 0, first_core, second_core)
    send[...] = jnp.where(core == 0, second_core, first_core).astype(BF16)


def tile_call(*operands):
    shapes = [
        ((80, 128), F32), ((72, 128), F32), ((640, 1152), BF16), ((640, 1152), F32), ((768, 1280), BF16),
        ((512, 1024), F32), ((512, 1024), BF16), ((512, 1024), F32), ((512, 1024), F32), ((512, 1024), F32),
        ((640, 128), F32), ((72, 128), F32), ((128, 768), F32), ((208, 128), F32), ((208, 128), F32),
    ]
    return pl.pallas_call(
        tile_kernel,
        out_shape=(jax.ShapeDtypeStruct((240, 128), F32), jax.ShapeDtypeStruct((240, 128), BF16)),
        in_specs=[pl.BlockSpec(memory_space=pltpu.VMEM)] * len(operands),
        out_specs=(pl.BlockSpec(memory_space=pltpu.VMEM),) * 2,
        scratch_shapes=[pltpu.VMEM(shape, kind) for shape, kind in shapes],
        compiler_params=pltpu.CompilerParams(vmem_limit_bytes=40 * 2**20),
        cost_estimate=pl.CostEstimate(flops=2 * 10**9, bytes_accessed=10**6, transcendentals=10**6),
        name="tiles",
    )(*operands)


def join_kernel(kept, received, out):
    first_core = lax.axis_index("band") % 2 == 0
    total = kept[...] + received[...].astype(F32)
    small = total[232:233] + total[233:234]
    loss = total[234:235] + total[235:236]
    small_hi = small.astype(BF16).astype(F32)
    loss_hi = loss.astype(BF16).astype(F32)
    tail = jnp.concatenate(
        [small_hi, small - small_hi, loss_hi, loss - loss_hi, jnp.zeros((2, 128), F32)], axis=0
    )

    def to_all(rows):
        return jnp.broadcast_to(rows[None], (CHIPS, rows.shape[0], 128))

    extra = jnp.concatenate(
        [total[72:88].reshape(CHIPS, 1, 128), total[88:104].reshape(CHIPS, 1, 128), to_all(tail)], axis=1
    )
    out[...] = jnp.concatenate(
        [
            to_all(total[0:72]),
            jnp.where(first_core, extra, to_all(total[72:80])),
            to_all(total[80:104]),
            total[104:232].reshape(CHIPS, 8, 128),
        ],
        axis=1,
    ).astype(BF16)


def join_call(kept, received):
    return pl.pallas_call(
        join_kernel,
        out_shape=jax.ShapeDtypeStruct((CHIPS, 112, 128), BF16),
        in_specs=[pl.BlockSpec(memory_space=pltpu.VMEM)] * 2,
        out_specs=pl.BlockSpec(memory_space=pltpu.VMEM),
        compiler_params=pltpu.CompilerParams(vmem_limit_bytes=16 * 2**20),
        name="join",
    )(kept, received)


def sum_kernel(parts, cols, out, mine, theirs, bins):
    band = lax.axis_index("band")
    off = lax.axis_index("off")
    core = band % 2
    half_lane = lane_ids((1, 128)) < 64
    bins[...] = jnp.zeros(bins.shape, F32)
    split = jnp.where(core == 0, 72, 104)
    used = row_ids((104, 128)) < split
    for chip in range(CHIPS):
        piece = jnp.where(used, parts[chip].astype(F32)[0:104], 0.0)
        start = pl.multiple_of(chip // 2 * 128 + core * (chip % 2 * 128) + 56, 8)
        bins[pl.ds(start, 104), :] += piece
        bins[pl.ds(pl.multiple_of(start + split, 8), 104), :] += pltpu.roll(piece, 64, 1)

    def own_half(x):
        return jnp.where(
            core == 0, jnp.where(half_lane, x, 0.0), jnp.where(half_lane, 0.0, pltpu.roll(x, 64, 1))
        ).astype(BF16)

    other = band + 1 - 2 * core
    mine[...] = own_half(bins[pl.ds(pl.multiple_of(64 + 64 * band + 32 * off, 32), 32), :])
    theirs[...] = own_half(bins[pl.ds(pl.multiple_of(64 + 64 * other + 32 * off, 32), 32), :])
    halves = bins[64:1088, :].reshape(BANDS, 2, 32, 128)
    dense = jnp.where(
        half_lane, halves[:, 0].reshape(512, 128), pltpu.roll(halves[:, 1].reshape(512, 128), 64, 1)
    ).astype(BF16)
    product = lax.dot_general(
        cols[:, 64:96, :].reshape(512, 128), dense, (((0,), (0,)), ((), ())), preferred_element_type=F32
    )
    rows = product[0:64] + pltpu.roll(product[64:128], 64, 1)
    rows = jnp.where(half_lane, rows[0:32], pltpu.roll(rows[32:64], 64, 1))
    weights = jnp.sum(parts[:, 96:112, :].astype(F32), axis=0)[8:16]
    extra = jnp.sum(parts[:, 64:80, :].astype(F32), axis=0)[8:16]
    small = extra[2:3] + extra[3:4]
    loss = extra[4:5] + extra[5:6]
    small_hi = small.astype(BF16).astype(F32)
    loss_hi = loss.astype(BF16).astype(F32)
    whole = jnp.concatenate(
        [
            rows, weights, extra[0:2], small_hi, small - small_hi, loss_hi, loss - loss_hi,
            jnp.zeros((2, 128), F32),
        ],
        axis=0,
    )
    out[...] = jnp.broadcast_to(whole.astype(BF16)[None], (PEERS, 48, 128))


def sum_call(parts, cols):
    return pl.pallas_call(
        sum_kernel,
        out_shape=(
            jax.ShapeDtypeStruct((PEERS, 48, 128), BF16),
            jax.ShapeDtypeStruct((32, 128), BF16),
            jax.ShapeDtypeStruct((32, 128), BF16),
        ),
        in_specs=[pl.BlockSpec(memory_space=pltpu.VMEM)] * 2,
        out_specs=(pl.BlockSpec(memory_space=pltpu.VMEM),) * 3,
        scratch_shapes=[pltpu.VMEM((1408, 128), F32)],
        compiler_params=pltpu.CompilerParams(vmem_limit_bytes=16 * 2**20),
        name="sums",
    )(parts, cols)


def final_kernel(every, grad_proj_hbm, grad_conv_hbm, bias, w_out, loss, grad_proj, grad_conv_t, sems):
    half_lane = lane_ids((1, 128)) < 64
    puts = []
    for k in range(4):
        for chip in range(4 * k, 4 * k + 4):
            source = chip // 2 * 4 + chip % 2
            left = every[source, 0:32, :].astype(F32)
            right = every[source + 2, 0:32, :].astype(F32)
            row = chip * 64
            grad_proj[row : row + 32, :] = jnp.where(half_lane, left, pltpu.roll(right, 64, 1))
            grad_proj[row + 32 : row + 64, :] = jnp.where(half_lane, pltpu.roll(left, 64, 1), right)
        rows = pl.ds(k * 256, 256)
        puts.append(pltpu.make_async_copy(grad_proj.at[rows], grad_proj_hbm.at[rows], sems.at[k]))
        puts[k].start()
    conv = every[:, 32:48, :].astype(F32).reshape(8, 2, 2, 16, 128)
    for core in range(2):
        wide = conv[:, core, :, 0:8].reshape(128, 128)
        for k in range(2):
            lane = (2 - 2 * core + k) * 128
            grad_conv_t[:, lane : lane + 128] = wide[k * 64 : k * 64 + 64]
    first = conv[:, 0].reshape(CHIPS, 16, 128)
    last = jnp.concatenate([first[:, 8], first[:, 9]], axis=0)
    grad_conv_t[0:32, 512:576] = last[:, 0:64]
    grad_conv_t[32:64, 512:576] = last[:, 64:128]
    puts.append(pltpu.make_async_copy(grad_conv_t, grad_conv_hbm, sems.at[4]))
    puts[4].start()
    small = first[0, 10:11] + first[0, 11:12]
    bias[...] = small[:, 0:64]
    w_out[...] = small[:, 64:128]
    loss[...] = (first[0, 12:13] + first[0, 13:14])[:, 0:1]
    for put in puts:
        put.wait()


def final_call(every):
    return pl.pallas_call(
        final_kernel,
        out_shape=(
            jax.ShapeDtypeStruct((1024, 128), F32),
            jax.ShapeDtypeStruct((64, 576), F32),
            jax.ShapeDtypeStruct((1, 64), F32),
            jax.ShapeDtypeStruct((1, 64), F32),
            jax.ShapeDtypeStruct((1, 1), F32),
        ),
        in_specs=[pl.BlockSpec(memory_space=pltpu.VMEM)],
        out_specs=(pl.BlockSpec(memory_space=pltpu.HBM),) * 2 + (pl.BlockSpec(memory_space=pltpu.VMEM),) * 3,
        scratch_shapes=[
            pltpu.VMEM((1024, 128), F32),
            pltpu.VMEM((64, 576), F32),
            pltpu.SemaphoreType.DMA((5,)),
        ],
        compiler_params=pltpu.CompilerParams(vmem_limit_bytes=8 * 2**20),
        name="outputs",
    )(every)


def body(feats, w_proj, conv_w, conv_b, w_out, target, mask):
    spread = lax.all_to_all(front_call(feats, w_proj), "band", 0, 0, tiled=True)
    ready = prep_call(
        mask.reshape(8, 128), target, conv_w.T, conv_b.reshape(1, 64), w_out.reshape(1, 64)
    )
    swap = [(2 * i + o, 2 * (i + 1 - 2 * (i % 2)) + o) for i in range(BANDS) for o in range(2)]
    same_core = [[2 * i + o for i in range(core, BANDS, 2) for o in range(2)] for core in range(2)]
    kept, given = tile_call(spread, *ready)
    joined = join_call(kept, lax.ppermute(given, GROUP, swap))
    parts = lax.all_to_all(joined, GROUP, 0, 0, tiled=True, axis_index_groups=same_core)
    sums, mine, theirs = sum_call(parts, spread)
    every = lax.all_to_all(sums, GROUP, 0, 0, tiled=True)
    own = mine + lax.ppermute(theirs, GROUP, swap)
    grad_feats = lax.dot_general(
        own, w_proj, (((1,), (1,)), ((), ())), preferred_element_type=F32
    ).astype(BF16)
    grad_proj, grad_conv_t, bias, w_out, loss = final_call(every)
    return (loss.reshape(1), grad_proj, grad_conv_t.T, bias.reshape(64), w_out.reshape(64), grad_feats)


def solution(mesh):
    placed = (
        P(("rep", "band"), None),
        P(),
        P(),
        P(),
        P(),
        P(("rep", "band"), "off", None),
        P("rep"),
    )
    return jax.shard_map(
        body,
        mesh=mesh,
        in_specs=placed,
        out_specs=(
            P("rep"),
            P("rep", None),
            P("rep", None),
            P("rep"),
            P("rep"),
            P(("rep", "band", "off"), None),
        ),
        check_vma=False,
    )
```

```python
import jax
import jax.numpy as jnp
from jax import lax
from jax.experimental import pallas as pl
from jax.experimental.pallas import tpu as pltpu
from jax.sharding import PartitionSpec as P

GELU_K = 0.7978845608028654
GELU_C = 0.044715
GROUP = ("band", "off")
CHIPS = 16
BANDS = 16
F32 = jnp.float32
BF16 = jnp.bfloat16


def gelu_parts(x, half):
    square = x * x
    t = jnp.tanh(x * (GELU_K + (GELU_K * GELU_C) * square))
    one_plus = 1.0 + t
    scaled = x * half
    value = scaled * one_plus
    slope = one_plus * (half + (scaled * (1.0 - t)) * (GELU_K + (3.0 * GELU_K * GELU_C) * square))
    return value, slope


def lane_ids(shape):
    return lax.broadcasted_iota(jnp.int32, shape, len(shape) - 1)


def row_ids(shape):
    return lax.broadcasted_iota(jnp.int32, shape, len(shape) - 2)


def dot(a, b):
    return jnp.dot(a, b, preferred_element_type=F32)


def front_kernel(feats_hbm, w_proj_hbm, out, feats, w_proj, sems):
    off = lax.axis_index("off")
    get_feats = pltpu.make_async_copy(feats_hbm, feats, sems.at[0])
    get_w = pltpu.make_async_copy(w_proj_hbm, w_proj, sems.at[1])
    get_feats.start()
    get_w.start()
    get_feats.wait()
    half_lane = lane_ids((1, 128)) < 64
    for q in range(8):
        block = feats[:, q * 128 : q * 128 + 128].astype(F32)
        top, bottom = block[0:32], block[32:64]
        low = jnp.where(half_lane, top, pltpu.roll(bottom, 64, 1))
        high = jnp.where(half_lane, pltpu.roll(top, 64, 1), bottom)
        out[q, 64:96, :] = jnp.where(off == 0, low, high).astype(BF16)
    get_w.wait()
    proj = dot(feats[...], w_proj[...]).astype(BF16)
    out[:, 0:64, :] = jnp.broadcast_to(proj[None], (8, 64, 128))


def front_call(feats, w_proj):
    return pl.pallas_call(
        front_kernel,
        out_shape=jax.ShapeDtypeStruct((8, 96, 128), BF16),
        in_specs=[pl.BlockSpec(memory_space=pltpu.HBM)] * 2,
        out_specs=pl.BlockSpec(memory_space=pltpu.VMEM),
        scratch_shapes=[
            pltpu.VMEM((64, 1024), BF16),
            pltpu.VMEM((1024, 128), BF16),
            pltpu.SemaphoreType.DMA((2,)),
        ],
        compiler_params=pltpu.CompilerParams(vmem_limit_bytes=60 * 2**20),
        name="front",
    )(feats, w_proj)


def prep_kernel(
    mask, target, conv_t, fwd_w, bwd_w, goal, row_mask, col_mask
):
    band = lax.axis_index("band")
    first = band + 2 * lax.axis_index("off")
    half_lane = lane_ids((1, 128)) < 64

    blank = jnp.zeros((64, 64), F32)
    for ty in range(3):
        taps = [conv_t[:, (3 * ty + tx) * 64 : (3 * ty + tx + 1) * 64].astype(F32) for tx in range(3)]
        low = jnp.concatenate(taps + [blank], axis=1)
        high = jnp.concatenate([blank] + taps, axis=1)
        fwd_w[ty * 256 : ty * 256 + 256, :] = jnp.concatenate([low, high], axis=0).T.astype(BF16)
        left = taps[::-1] + [blank]
        right = [blank] + taps[::-1]
        for k in range(4):
            row = ty * 256 + k * 64
            bwd_w[row : row + 64, :] = jnp.concatenate([left[k], right[k]], axis=1).astype(BF16)

    mask_all = mask[...].astype(F32)
    mask_lane = lane_ids((8, 128))
    by_band = jnp.concatenate(
        [jnp.where(mask_lane < 64, mask_all, 0.0), jnp.where(mask_lane < 64, 0.0, mask_all)], axis=0
    ).astype(BF16)
    sums_row = dot(by_band, jnp.ones((128, 128), BF16))
    sums_col = lax.dot_general(
        jnp.ones((16, 128), BF16), by_band, (((1,), (1,)), ((), ())), preferred_element_type=F32
    )
    at = lax.broadcasted_iota(jnp.int32, (16, 16), 0)
    to = lax.broadcasted_iota(jnp.int32, (16, 16), 1)
    apart = (2 * (to % 8) + to // 8) - (2 * (at % 8) + at // 8)
    near_diagonal = (apart >= 0) & (apart < 4)
    count = jnp.sum(jnp.where(near_diagonal, sums_row[:, 0:16] * sums_col, 0.0))
    scale = 1.0 / count

    def mask_rows(which):
        inside = jnp.minimum(which, 15)
        line = mask[pl.ds(inside // 2, 1), :].astype(F32)
        line = jnp.where(which < 16, line, 0.0)
        spot = row_ids((64, 128)) + 64 * (inside % 2)
        spread = jnp.where(lane_ids((64, 128)) == spot, line, 0.0)
        return dot(spread.astype(BF16), jnp.ones((128, 128), BF16))

    row_mask[...] = (
        jnp.broadcast_to(mask_rows(band)[:, None, :] * (2.0 * scale), (64, 8, 128)).reshape(512, 128)
    )
    col_all = jnp.concatenate([mask_rows(first), mask_rows(first + 1)], axis=0).reshape(8, 2, 8, 128)
    col_mask[...] = jnp.where(half_lane, col_all[:, 0].reshape(64, 128), col_all[:, 1].reshape(64, 128))

    line = jnp.concatenate([target[:, 0, :], target[:, 1, :]], axis=1)
    lines = jnp.broadcast_to(line[:, None, :], (64, 8, 128)).reshape(512, 128)
    lines = jnp.where(lane_ids((512, 128)) % 8 == row_ids((512, 128)) % 8, lines, 0.0)
    lines_hi = lines.astype(BF16)
    lines_lo = (lines - lines_hi.astype(F32)).astype(BF16)
    spread = (
        (row_ids((128, 1024)) // 8 == lane_ids((128, 1024)) // 64).astype(F32).astype(BF16)
    )
    goal[...] = dot(
        jnp.concatenate([lines_hi, lines_lo], axis=1), jnp.concatenate([spread, spread], axis=0)
    )


def prep_call(*operands):
    shapes = [
        ((768, 128), BF16), ((768, 128), BF16), ((512, 1024), F32), ((512, 128), F32), ((64, 128), F32),
    ]
    return pl.pallas_call(
        prep_kernel,
        out_shape=tuple(jax.ShapeDtypeStruct(shape, kind) for shape, kind in shapes),
        in_specs=[pl.BlockSpec(memory_space=pltpu.VMEM)] * len(operands),
        out_specs=(pl.BlockSpec(memory_space=pltpu.VMEM),) * len(shapes),
        compiler_params=pltpu.CompilerParams(vmem_limit_bytes=16 * 2**20),
        cost_estimate=pl.CostEstimate(flops=3 * 10**8, bytes_accessed=4 * 10**6, transcendentals=0),
        name="prepare",
    )(*operands)


def tile_kernel(
    same, other, conv_b, w_out, fwd_w, bwd_w, goal, row_mask, col_mask,
    keep, send,
    rows_u, cols_v, pair, slope, grads, pre, hid16, hid32, weighted, guess, grad_rows, grad_cols, grad_w,
    place_u, place_v,
):
    band = lax.axis_index("band")
    core = band % 2
    first = band + 2 * lax.axis_index("off")
    half_lane = lane_ids((1, 128)) < 64

    zero_rows = jnp.zeros((128, 1280), BF16)
    grads[0:128, :] = zero_rows
    grads[640:768, :] = zero_rows
    grads[128:640, 0:128] = jnp.zeros((512, 128), BF16)
    grads[128:640, 1152:1280] = jnp.zeros((512, 128), BF16)

    def channels(which, rows):
        inside = jnp.clip(which, 0, BANDS - 1)
        at = inside // 2
        return jnp.where(
            inside % 2 == core, same[at, rows, :].astype(F32), other[at, rows, :].astype(F32)
        )

    def ending(which):
        return channels(which, slice(48, 64))[8:16]

    def whole(which):
        return channels(which, slice(0, 64))

    def opening(which):
        return channels(which, slice(0, 16))[0:8]

    u = jnp.concatenate([ending(band - 1), whole(band), opening(band + 1)], axis=0)
    rows_u[...] = jnp.where(half_lane, u, pltpu.roll(u, 64, 1))
    v = jnp.concatenate(
        [ending(first - 1), whole(first), whole(first + 1), opening(first + 2)], axis=0
    ).reshape(9, 2, 8, 128)
    v_low = v[:, 0].reshape(72, 128)
    v_high = v[:, 1].reshape(72, 128)
    cols_v[...] = jnp.where(half_lane, pltpu.roll(v_low, 64, 1), v_high)

    bias2 = jnp.concatenate([conv_b[...], conv_b[...]], axis=1)
    out_w2 = jnp.concatenate([w_out[...], w_out[...]], axis=1)
    halves = ((row_ids((128, 128)) < 64) == (lane_ids((128, 128)) < 64)).astype(F32).astype(BF16)

    def pair_stage(bp):
        lane = slice(bp * 128, bp * 128 + 128)
        block = first * 8 - 1 + 2 * bp
        spot = jnp.where(half_lane, block, block + 1)
        col_in = jnp.where((spot >= 0) & (spot < 128), 0.5, 0.0)
        v_here = cols_v[bp * 8 : bp * 8 + 8, :][None]
        for aq in range(10):
            half = col_in
            if aq == 0:
                half = jnp.where(band == 0, 0.0, col_in)
            if aq == 9:
                half = jnp.where(band == BANDS - 1, 0.0, col_in)
            x = (rows_u[aq * 8 : aq * 8 + 8, :][:, None, :] + v_here).reshape(64, 128)
            value, grade = gelu_parts(x, half)
            pair[aq * 64 : aq * 64 + 64, lane] = value.astype(BF16)
            slope[aq * 64 : aq * 64 + 64, lane] = grade

    def conv_stage(bp):
        lane = bp * 128
        pre[:, lane : lane + 128] = (
            dot(pair[0:512, lane : lane + 256], fwd_w[0:256, :])
            + dot(pair[64:576, lane : lane + 256], fwd_w[256:512, :])
            + dot(pair[128:640, lane : lane + 256], fwd_w[512:768, :])
        )

    def act_stage(bp):
        lane = slice(bp * 128, bp * 128 + 128)
        for aq in range(8):
            row = slice(aq * 64, aq * 64 + 64)
            value, grade = gelu_parts(pre[row, lane] + bias2, 0.5)
            hid32[row, lane] = value
            hid16[row, lane] = (value * out_w2).astype(BF16)
            weighted[row, lane] = grade * out_w2

    def pred_stage(bp):
        lane = slice(bp * 128, bp * 128 + 128)
        guess[:, lane] = dot(hid16[:, lane], halves)

    def loss_stage(bp, sums):
        loss_sum, bias_sum, out_sum = sums
        lane = slice(bp * 128, bp * 128 + 128)
        col_weight = col_mask[bp * 8 : bp * 8 + 8, :][None]
        for aq in range(8):
            row = slice(aq * 64, aq * 64 + 64)
            weight = (row_mask[row, :].reshape(8, 8, 128) * col_weight).reshape(64, 128)
            residue = guess[row, lane] - goal[row, lane]
            grad_pred = weight * residue
            grad_pre = grad_pred * weighted[row, lane]
            grads[128 + aq * 64 : 192 + aq * 64, bp * 128 + 128 : bp * 128 + 256] = grad_pre.astype(BF16)
            loss_sum = loss_sum + jnp.sum((grad_pred * residue).reshape(8, 8, 128), axis=0)
            bias_sum = bias_sum + jnp.sum(grad_pre.reshape(8, 8, 128), axis=0)
            out_sum = out_sum + jnp.sum((grad_pred * hid32[row, lane]).reshape(8, 8, 128), axis=0)
        return loss_sum, bias_sum, out_sum

    def weights_stage(bp):
        lane = bp * 128
        turned = grads[128:640, lane + 128 : lane + 256].T
        for ty in range(3):
            part = dot(turned, pair[ty * 64 : ty * 64 + 512, lane : lane + 256])
            if bp == 0:
                grad_w[:, ty * 256 : ty * 256 + 256] = part
            else:
                grad_w[:, ty * 256 : ty * 256 + 256] += part

    def back_stage(bp):
        lane = bp * 128
        part = (
            dot(grads[128:768, lane : lane + 256], bwd_w[0:256, :])
            + dot(grads[64:704, lane : lane + 256], bwd_w[256:512, :])
            + dot(grads[0:640, lane : lane + 256], bwd_w[512:768, :])
        ) * slope[:, lane : lane + 128]
        if bp == 0:
            grad_rows[...] = part
        else:
            grad_rows[...] += part
        grad_cols[bp * 8 : bp * 8 + 8, :] = jnp.sum(part.reshape(80, 8, 128), axis=0)

    zero8 = jnp.zeros((8, 128), F32)
    totals = (zero8, zero8, zero8)
    for step in range(15):
        if 6 <= step:
            back_stage(step - 6)
        if 6 <= step < 14:
            weights_stage(step - 6)
        if 5 <= step < 13:
            totals = loss_stage(step - 5, totals)
        if 4 <= step < 12:
            pred_stage(step - 4)
        if 3 <= step < 11:
            act_stage(step - 3)
        if 2 <= step < 10:
            conv_stage(step - 2)
        if step < 9:
            pair_stage(step)

    row_part = jnp.sum(grad_rows[...].reshape(80, 8, 128), axis=1)
    place_u[...] = jnp.zeros(place_u.shape, F32)
    place_v[...] = jnp.zeros(place_v.shape, F32)
    place_u[pl.ds(pl.multiple_of(core * 64, 64), 80), :] = row_part + pltpu.roll(row_part, 64, 1)
    col_part = grad_cols[...]
    col_high = pltpu.roll(col_part, 64, 1).reshape(9, 1, 8, 128)
    place_v[pl.ds(pl.multiple_of(core * 64, 64), 144), :] = jnp.concatenate(
        [col_part.reshape(9, 1, 8, 128), col_high], axis=1
    ).reshape(144, 128)
    packed_u = jnp.where(half_lane, place_u[0:72, :], pltpu.roll(place_u[72:144, :], 64, 1))
    packed_v = jnp.where(half_lane, place_v[0:104, :], pltpu.roll(place_v[104:208, :], 64, 1))

    taps = []
    for ty in range(3):
        taps.append(
            grad_w[0:64, ty * 256 : ty * 256 + 192] + grad_w[64:128, ty * 256 + 64 : ty * 256 + 256]
        )
    conv_grad = jnp.concatenate(taps, axis=1)
    blocks = [conv_grad[:, k * 128 : k * 128 + 128] for k in range(4)]
    last = jnp.concatenate([conv_grad[0:32, 512:576], conv_grad[32:64, 512:576]], axis=1)

    loss_sum, bias_sum, out_sum = totals
    bias_row = jnp.sum(bias_sum, axis=0, keepdims=True)
    bias_row = bias_row + pltpu.roll(bias_row, 64, 1)
    out_row = jnp.sum(out_sum, axis=0, keepdims=True)
    out_row = out_row + pltpu.roll(out_row, 64, 1)
    small_row = jnp.where(half_lane, bias_row, out_row)
    loss_row = jnp.broadcast_to(jnp.sum(loss_sum, keepdims=True) * (0.5 / 64.0), (1, 128))
    small_hi = small_row.astype(BF16).astype(F32)
    loss_hi = loss_row.astype(BF16).astype(F32)
    tail = jnp.concatenate(
        [small_hi, small_row - small_hi, loss_hi, loss_row - loss_hi, jnp.zeros((4, 128), F32)], axis=0
    )
    first_core = jnp.concatenate([packed_u, last, blocks[2], blocks[3], tail], axis=0)
    second_core = jnp.concatenate([packed_v, blocks[0], blocks[1], tail], axis=0)
    keep[...] = jnp.where(core == 0, first_core, second_core)
    send[...] = jnp.where(core == 0, second_core, first_core).astype(BF16)


def tile_call(*operands):
    shapes = [
        ((80, 128), F32), ((72, 128), F32), ((640, 1152), BF16), ((640, 1152), F32), ((768, 1280), BF16),
        ((512, 1024), F32), ((512, 1024), BF16), ((512, 1024), F32), ((512, 1024), F32), ((512, 1024), F32),
        ((640, 128), F32), ((72, 128), F32), ((128, 768), F32), ((208, 128), F32), ((208, 128), F32),
    ]
    return pl.pallas_call(
        tile_kernel,
        out_shape=(jax.ShapeDtypeStruct((240, 128), F32), jax.ShapeDtypeStruct((240, 128), BF16)),
        in_specs=[pl.BlockSpec(memory_space=pltpu.VMEM)] * len(operands),
        out_specs=(pl.BlockSpec(memory_space=pltpu.VMEM),) * 2,
        scratch_shapes=[pltpu.VMEM(shape, kind) for shape, kind in shapes],
        compiler_params=pltpu.CompilerParams(vmem_limit_bytes=40 * 2**20),
        cost_estimate=pl.CostEstimate(flops=2 * 10**9, bytes_accessed=10**6, transcendentals=10**6),
        name="tiles",
    )(*operands)


def join_kernel(kept, received, out):
    first_core = lax.axis_index("band") % 2 == 0
    total = kept[...] + received[...].astype(F32)
    small = total[232:233] + total[233:234]
    loss = total[234:235] + total[235:236]
    small_hi = small.astype(BF16).astype(F32)
    loss_hi = loss.astype(BF16).astype(F32)
    tail = jnp.concatenate(
        [small_hi, small - small_hi, loss_hi, loss - loss_hi, jnp.zeros((2, 128), F32)], axis=0
    )

    def to_all(rows):
        return jnp.broadcast_to(rows[None], (CHIPS, rows.shape[0], 128))

    extra = jnp.concatenate(
        [total[72:88].reshape(CHIPS, 1, 128), total[88:104].reshape(CHIPS, 1, 128), to_all(tail)], axis=1
    )
    out[...] = jnp.concatenate(
        [
            to_all(total[0:72]),
            jnp.where(first_core, extra, to_all(total[72:80])),
            to_all(total[80:104]),
            total[104:232].reshape(CHIPS, 8, 128),
        ],
        axis=1,
    ).astype(BF16)


def join_call(kept, received):
    return pl.pallas_call(
        join_kernel,
        out_shape=jax.ShapeDtypeStruct((CHIPS, 112, 128), BF16),
        in_specs=[pl.BlockSpec(memory_space=pltpu.VMEM)] * 2,
        out_specs=pl.BlockSpec(memory_space=pltpu.VMEM),
        compiler_params=pltpu.CompilerParams(vmem_limit_bytes=16 * 2**20),
        name="join",
    )(kept, received)


def sum_kernel(parts, same, other, out, mine, theirs, bins):
    band = lax.axis_index("band")
    off = lax.axis_index("off")
    core = band % 2
    half_lane = lane_ids((1, 128)) < 64
    bins[...] = jnp.zeros(bins.shape, F32)
    split = jnp.where(core == 0, 72, 104)
    used = row_ids((104, 128)) < split
    for chip in range(CHIPS):
        piece = jnp.where(used, parts[chip].astype(F32)[0:104], 0.0)
        start = pl.multiple_of(chip // 2 * 128 + core * (chip % 2 * 128) + 56, 8)
        bins[pl.ds(start, 104), :] += piece
        bins[pl.ds(pl.multiple_of(start + split, 8), 104), :] += pltpu.roll(piece, 64, 1)

    def own_half(x):
        return jnp.where(
            core == 0, jnp.where(half_lane, x, 0.0), jnp.where(half_lane, 0.0, pltpu.roll(x, 64, 1))
        ).astype(BF16)

    sibling = band + 1 - 2 * core
    mine[...] = own_half(bins[pl.ds(pl.multiple_of(64 + 64 * band + 32 * off, 32), 32), :])
    theirs[...] = own_half(bins[pl.ds(pl.multiple_of(64 + 64 * sibling + 32 * off, 32), 32), :])
    halves = bins[64:1088, :].reshape(8, 2, 2, 32, 128)

    def dense(bands):
        return jnp.where(
            half_lane, bands[:, 0].reshape(256, 128), pltpu.roll(bands[:, 1].reshape(256, 128), 64, 1)
        )

    even, odd = dense(halves[:, 0]), dense(halves[:, 1])
    product = 0.0
    for cols, bands in (
        (same, jnp.where(core == 0, even, odd)), (other, jnp.where(core == 0, odd, even))
    ):
        product = product + lax.dot_general(
            cols[:, 64:96, :].reshape(256, 128), bands.astype(BF16), (((0,), (0,)), ((), ())),
            preferred_element_type=F32,
        )
    rows = product[0:64] + pltpu.roll(product[64:128], 64, 1)
    rows = jnp.where(half_lane, rows[0:32], pltpu.roll(rows[32:64], 64, 1))
    weights = jnp.sum(parts[:, 96:112, :].astype(F32), axis=0)[8:16]
    extra = jnp.sum(parts[:, 64:80, :].astype(F32), axis=0)[8:16]
    small = extra[2:3] + extra[3:4]
    loss = extra[4:5] + extra[5:6]
    small_hi = small.astype(BF16).astype(F32)
    loss_hi = loss.astype(BF16).astype(F32)
    whole = jnp.concatenate(
        [
            rows, weights, extra[0:2], small_hi, small - small_hi, loss_hi, loss - loss_hi,
            jnp.zeros((2, 128), F32),
        ],
        axis=0,
    )
    out[...] = jnp.broadcast_to(whole.astype(BF16)[None], (CHIPS, 48, 128))


def sum_call(parts, same, other):
    return pl.pallas_call(
        sum_kernel,
        out_shape=(
            jax.ShapeDtypeStruct((CHIPS, 48, 128), BF16),
            jax.ShapeDtypeStruct((32, 128), BF16),
            jax.ShapeDtypeStruct((32, 128), BF16),
        ),
        in_specs=[pl.BlockSpec(memory_space=pltpu.VMEM)] * 3,
        out_specs=(pl.BlockSpec(memory_space=pltpu.VMEM),) * 3,
        scratch_shapes=[pltpu.VMEM((1408, 128), F32)],
        compiler_params=pltpu.CompilerParams(vmem_limit_bytes=16 * 2**20),
        name="sums",
    )(parts, same, other)


def final_kernel(
    same, other, mine, received, w_proj, grad_proj_hbm, grad_conv_hbm, grad_feats_hbm, bias, w_out, loss,
    grad_proj, grad_conv_t, grad_feats, sems,
):
    is_first = lax.axis_index("band") % 2 == 0
    half_lane = lane_ids((1, 128)) < 64
    firsts, seconds = [], []
    puts = []
    gproj = mine[...] + received[...]
    grad_feats[...] = lax.dot_general(
        gproj, w_proj[...], (((1,), (1,)), ((), ())), preferred_element_type=F32
    ).astype(BF16)
    put_feats = pltpu.make_async_copy(grad_feats, grad_feats_hbm, sems.at[5])
    put_feats.start()
    for k in range(4):
        for chip in range(4 * k, 4 * k + 4):
            here = same[chip].astype(F32)
            there = other[chip].astype(F32)
            left = jnp.where(is_first, here, there)
            right = jnp.where(is_first, there, here)
            firsts.append(left[32:48])
            seconds.append(right[32:40])
            left, right = left[0:32], right[0:32]
            row = chip * 64
            grad_proj[row : row + 32, :] = jnp.where(half_lane, left, pltpu.roll(right, 64, 1))
            grad_proj[row + 32 : row + 64, :] = jnp.where(half_lane, pltpu.roll(left, 64, 1), right)
        rows = pl.ds(k * 256, 256)
        puts.append(pltpu.make_async_copy(grad_proj.at[rows], grad_proj_hbm.at[rows], sems.at[k]))
        puts[k].start()
    wide = jnp.concatenate(seconds + [first[0:8] for first in firsts], axis=0)
    for k in range(4):
        grad_conv_t[:, k * 128 : k * 128 + 128] = wide[k * 64 : k * 64 + 64]
    last = jnp.concatenate([first[8:9] for first in firsts] + [first[9:10] for first in firsts], axis=0)
    grad_conv_t[0:32, 512:576] = last[:, 0:64]
    grad_conv_t[32:64, 512:576] = last[:, 64:128]
    puts.append(pltpu.make_async_copy(grad_conv_t, grad_conv_hbm, sems.at[4]))
    puts[4].start()
    small = firsts[0][10:11] + firsts[0][11:12]
    bias[...] = small[:, 0:64]
    w_out[...] = small[:, 64:128]
    loss[...] = (firsts[0][12:13] + firsts[0][13:14])[:, 0:1]
    for put in puts + [put_feats]:
        put.wait()


def final_call(*operands):
    return pl.pallas_call(
        final_kernel,
        out_shape=(
            jax.ShapeDtypeStruct((1024, 128), F32),
            jax.ShapeDtypeStruct((64, 576), F32),
            jax.ShapeDtypeStruct((32, 1024), BF16),
            jax.ShapeDtypeStruct((1, 64), F32),
            jax.ShapeDtypeStruct((1, 64), F32),
            jax.ShapeDtypeStruct((1, 1), F32),
        ),
        in_specs=[pl.BlockSpec(memory_space=pltpu.VMEM)] * len(operands),
        out_specs=(pl.BlockSpec(memory_space=pltpu.HBM),) * 3 + (pl.BlockSpec(memory_space=pltpu.VMEM),) * 3,
        scratch_shapes=[
            pltpu.VMEM((1024, 128), F32),
            pltpu.VMEM((64, 576), F32),
            pltpu.VMEM((32, 1024), BF16),
            pltpu.SemaphoreType.DMA((6,)),
        ],
        compiler_params=pltpu.CompilerParams(vmem_limit_bytes=8 * 2**20),
        name="outputs",
    )(*operands)


def body(feats, w_proj, conv_w, conv_b, w_out, target, mask):
    swap = [(2 * i + o, 2 * (i + 1 - 2 * (i % 2)) + o) for i in range(BANDS) for o in range(2)]
    same_core = [[2 * i + o for i in range(core, BANDS, 2) for o in range(2)] for core in range(2)]
    same_row = [[2 * i + o for i in range(core, BANDS, 2)] for core in range(2) for o in range(2)]
    same = lax.all_to_all(front_call(feats, w_proj), GROUP, 0, 0, tiled=True, axis_index_groups=same_row)
    ready = prep_call(mask.reshape(8, 128), target, conv_w.T)
    same, ready = lax.optimization_barrier((same, ready))
    other = lax.ppermute(same, GROUP, swap)
    kept, given = tile_call(same, other, conv_b.reshape(1, 64), w_out.reshape(1, 64), *ready)
    joined = join_call(kept, lax.ppermute(given, GROUP, swap))
    parts = lax.all_to_all(joined, GROUP, 0, 0, tiled=True, axis_index_groups=same_core)
    sums, mine, theirs = sum_call(parts, same, other)
    every = lax.all_to_all(sums, GROUP, 0, 0, tiled=True, axis_index_groups=same_core)
    every, theirs = lax.optimization_barrier((every, theirs))
    grad_proj, grad_conv_t, grad_feats, bias, w_out, loss = final_call(
        every, lax.ppermute(every, GROUP, swap), mine, lax.ppermute(theirs, GROUP, swap), w_proj
    )
    return (loss.reshape(1), grad_proj, grad_conv_t.T, bias.reshape(64), w_out.reshape(64), grad_feats)


def solution(mesh):
    placed = (
        P(("rep", "band"), None),
        P(),
        P(),
        P(),
        P(),
        P(("rep", "band"), "off", None),
        P("rep"),
    )
    return jax.shard_map(
        body,
        mesh=mesh,
        in_specs=placed,
        out_specs=(
            P("rep"),
            P("rep", None),
            P("rep", None),
            P("rep"),
            P("rep"),
            P(("rep", "band", "off"), None),
        ),
        check_vma=False,
    )
```

```python
import jax
import jax.numpy as jnp
from jax import lax
from jax.experimental import pallas as pl
from jax.experimental.pallas import tpu as pltpu
from jax.sharding import PartitionSpec as P

GELU_K = 0.7978845608028654
GELU_C = 0.044715
GROUP = ("band", "off")
CHIPS = 16
BANDS = 16
F32 = jnp.float32
BF16 = jnp.bfloat16


def gelu_parts(x, half):
    inner = GELU_K + (GELU_K * GELU_C) * (x * x)
    gate = half + half * jnp.tanh(x * inner)
    value = x * gate
    slope = gate + (value * (1.0 - gate)) * (6.0 * inner - 4.0 * GELU_K)
    return value, slope


def lane_ids(shape):
    return lax.broadcasted_iota(jnp.int32, shape, len(shape) - 1)


def row_ids(shape):
    return lax.broadcasted_iota(jnp.int32, shape, len(shape) - 2)


def dot(a, b):
    return jnp.dot(a, b, preferred_element_type=F32)


def front_kernel(feats_hbm, w_proj_hbm, out, feats, w_proj, sems):
    off = lax.axis_index("off")
    get_feats = pltpu.make_async_copy(feats_hbm, feats, sems.at[0])
    get_w = pltpu.make_async_copy(w_proj_hbm, w_proj, sems.at[1])
    get_feats.start()
    get_w.start()
    get_feats.wait()
    half_lane = lane_ids((1, 128)) < 64
    for q in range(8):
        block = feats[:, q * 128 : q * 128 + 128].astype(F32)
        top, bottom = block[0:32], block[32:64]
        low = jnp.where(half_lane, top, pltpu.roll(bottom, 64, 1))
        high = jnp.where(half_lane, pltpu.roll(top, 64, 1), bottom)
        out[q, 64:96, :] = jnp.where(off == 0, low, high).astype(BF16)
    get_w.wait()
    proj = dot(feats[...], w_proj[...]).astype(BF16)
    out[:, 0:64, :] = jnp.broadcast_to(proj[None], (8, 64, 128))


def front_call(feats, w_proj):
    return pl.pallas_call(
        front_kernel,
        out_shape=jax.ShapeDtypeStruct((8, 96, 128), BF16),
        in_specs=[pl.BlockSpec(memory_space=pltpu.HBM)] * 2,
        out_specs=pl.BlockSpec(memory_space=pltpu.VMEM),
        scratch_shapes=[
            pltpu.VMEM((64, 1024), BF16),
            pltpu.VMEM((1024, 128), BF16),
            pltpu.SemaphoreType.DMA((2,)),
        ],
        compiler_params=pltpu.CompilerParams(vmem_limit_bytes=60 * 2**20),
        name="front",
    )(feats, w_proj)


def prep_kernel(
    mask, target, conv_t, fwd_w, bwd_w, goal, row_mask, col_mask
):
    band = lax.axis_index("band")
    first = band + 2 * lax.axis_index("off")
    half_lane = lane_ids((1, 128)) < 64

    blank = jnp.zeros((64, 64), F32)
    for ty in range(3):
        taps = [conv_t[:, (3 * ty + tx) * 64 : (3 * ty + tx + 1) * 64].astype(F32) for tx in range(3)]
        low = jnp.concatenate(taps + [blank], axis=1)
        high = jnp.concatenate([blank] + taps, axis=1)
        fwd_w[ty * 256 : ty * 256 + 256, :] = jnp.concatenate([low, high], axis=0).T.astype(BF16)
        left = taps[::-1] + [blank]
        right = [blank] + taps[::-1]
        for k in range(4):
            row = ty * 256 + k * 64
            bwd_w[row : row + 64, :] = jnp.concatenate([left[k], right[k]], axis=1).astype(BF16)
    mask_all = mask[...].astype(F32)
    mask_lane = lane_ids((8, 128))
    by_band = jnp.concatenate(
        [jnp.where(mask_lane < 64, mask_all, 0.0), jnp.where(mask_lane < 64, 0.0, mask_all)], axis=0
    ).astype(BF16)
    sums_row = dot(by_band, jnp.ones((128, 128), BF16))
    sums_col = lax.dot_general(
        jnp.ones((16, 128), BF16), by_band, (((1,), (1,)), ((), ())), preferred_element_type=F32
    )
    at = lax.broadcasted_iota(jnp.int32, (16, 16), 0)
    to = lax.broadcasted_iota(jnp.int32, (16, 16), 1)
    apart = (2 * (to % 8) + to // 8) - (2 * (at % 8) + at // 8)
    near_diagonal = (apart >= 0) & (apart < 4)
    count = jnp.sum(jnp.where(near_diagonal, sums_row[:, 0:16] * sums_col, 0.0))
    scale = 1.0 / count

    def mask_rows(which):
        inside = jnp.minimum(which, 15)
        line = mask[pl.ds(inside // 2, 1), :].astype(F32)
        line = jnp.where(which < 16, line, 0.0)
        spot = row_ids((64, 128)) + 64 * (inside % 2)
        spread = jnp.where(lane_ids((64, 128)) == spot, line, 0.0)
        return dot(spread.astype(BF16), jnp.ones((128, 128), BF16))

    row_mask[...] = (
        jnp.broadcast_to(mask_rows(band)[:, None, :] * (2.0 * scale), (64, 8, 128)).reshape(512, 128)
    )
    col_all = jnp.concatenate([mask_rows(first), mask_rows(first + 1)], axis=0).reshape(8, 2, 8, 128)
    col_mask[...] = jnp.where(half_lane, col_all[:, 0].reshape(64, 128), col_all[:, 1].reshape(64, 128))

    line = jnp.concatenate([target[:, 0, :], target[:, 1, :]], axis=1)
    lines = jnp.broadcast_to(line[:, None, :], (64, 8, 128)).reshape(512, 128)
    lines = jnp.where(lane_ids((512, 128)) % 8 == row_ids((512, 128)) % 8, lines, 0.0)
    lines_hi = lines.astype(BF16)
    lines_lo = (lines - lines_hi.astype(F32)).astype(BF16)
    spread = (
        (row_ids((128, 1024)) // 8 == lane_ids((128, 1024)) // 64).astype(F32).astype(BF16)
    )
    goal[...] = dot(
        jnp.concatenate([lines_hi, lines_lo], axis=1), jnp.concatenate([spread, spread], axis=0)
    )


def prep_call(*operands):
    shapes = [
        ((768, 128), BF16), ((768, 128), BF16), ((512, 1024), F32), ((512, 128), F32), ((64, 128), F32),
    ]
    return pl.pallas_call(
        prep_kernel,
        out_shape=tuple(jax.ShapeDtypeStruct(shape, kind) for shape, kind in shapes),
        in_specs=[pl.BlockSpec(memory_space=pltpu.VMEM)] * len(operands),
        out_specs=(pl.BlockSpec(memory_space=pltpu.VMEM),) * len(shapes),
        compiler_params=pltpu.CompilerParams(vmem_limit_bytes=16 * 2**20),
        cost_estimate=pl.CostEstimate(flops=3 * 10**8, bytes_accessed=4 * 10**6, transcendentals=0),
        name="prepare",
    )(*operands)


def tile_kernel(
    same, other, conv_b, w_out, fwd_w, bwd_w, goal, row_mask, col_mask,
    keep, send,
    rows_u, cols_v, pair, slope, grads, pre, hid16, hid32, weighted, guess, grad_rows, grad_cols, grad_w,
    place_u, place_v, fwd_2, bwd_2,
):
    band = lax.axis_index("band")
    core = band % 2
    first = band + 2 * lax.axis_index("off")
    half_lane = lane_ids((1, 128)) < 64

    zero_rows = jnp.zeros((128, 1280), BF16)
    grads[0:128, :] = zero_rows
    grads[640:768, :] = zero_rows
    grads[128:640, 0:128] = jnp.zeros((512, 128), BF16)
    grads[128:640, 1152:1280] = jnp.zeros((512, 128), BF16)

    none = jnp.zeros((256, 128), BF16)
    for t in range(4):
        row = slice(t * 256, t * 256 + 256)
        for parity in range(2):
            lane = slice(parity * 128, parity * 128 + 128)
            ty = t - parity
            fwd_2[row, lane] = fwd_w[ty * 256 : ty * 256 + 256, :] if 0 <= ty < 3 else none
            ty = parity - t + 2
            bwd_2[row, lane] = bwd_w[ty * 256 : ty * 256 + 256, :] if 0 <= ty < 3 else none

    def channels(which, rows):
        inside = jnp.clip(which, 0, BANDS - 1)
        at = inside // 2
        return jnp.where(
            inside % 2 == core, same[at, rows, :].astype(F32), other[at, rows, :].astype(F32)
        )

    def ending(which):
        return channels(which, slice(48, 64))[8:16]

    def whole(which):
        return channels(which, slice(0, 64))

    def opening(which):
        return channels(which, slice(0, 16))[0:8]

    u = jnp.concatenate([ending(band - 1), whole(band), opening(band + 1)], axis=0)
    rows_u[...] = jnp.where(half_lane, u, pltpu.roll(u, 64, 1))
    v = jnp.concatenate(
        [ending(first - 1), whole(first), whole(first + 1), opening(first + 2)], axis=0
    ).reshape(9, 2, 8, 128)
    v_low = v[:, 0].reshape(72, 128)
    v_high = v[:, 1].reshape(72, 128)
    cols_v[...] = jnp.where(half_lane, pltpu.roll(v_low, 64, 1), v_high)

    bias2 = jnp.concatenate([conv_b[...], conv_b[...]], axis=1)
    out_w2 = jnp.concatenate([w_out[...], w_out[...]], axis=1)
    halves = ((row_ids((128, 128)) < 64) == (lane_ids((128, 128)) < 64)).astype(F32).astype(BF16)

    def pair_stage(bp):
        lane = slice(bp * 128, bp * 128 + 128)
        block = first * 8 - 1 + 2 * bp
        spot = jnp.where(half_lane, block, block + 1)
        col_in = jnp.where((spot >= 0) & (spot < 128), 0.5, 0.0)
        v_here = cols_v[bp * 8 : bp * 8 + 8, :][None]
        for aq in range(10):
            half = col_in
            if aq == 0:
                half = jnp.where(band == 0, 0.0, col_in)
            if aq == 9:
                half = jnp.where(band == BANDS - 1, 0.0, col_in)
            x = (rows_u[aq * 8 : aq * 8 + 8, :][:, None, :] + v_here).reshape(64, 128)
            value, grade = gelu_parts(x, half)
            pair[aq * 64 : aq * 64 + 64, lane] = value.astype(BF16)
            slope[aq * 64 : aq * 64 + 64, lane] = grade

    def conv_stage(bp):
        lane = bp * 128
        part = dot(
            jnp.concatenate(
                [
                    jnp.concatenate(
                        [pair[(2 * a + t) * 64 : (2 * a + t) * 64 + 64, lane : lane + 256] for a in range(4)], axis=0
                    )
                    for t in range(4)
                ],
                axis=1,
            ),
            fwd_2[...],
        )
        for a in range(4):
            for parity in range(2):
                row = (2 * a + parity) * 64
                pre[row : row + 64, lane : lane + 128] = part[a * 64 : a * 64 + 64, parity * 128 : parity * 128 + 128]

    def act_stage(bp):
        lane = slice(bp * 128, bp * 128 + 128)
        for aq in range(8):
            row = slice(aq * 64, aq * 64 + 64)
            value, grade = gelu_parts(pre[row, lane] + bias2, 0.5)
            hid32[row, lane] = value
            hid16[row, lane] = (value * out_w2).astype(BF16)
            weighted[row, lane] = grade * out_w2

    def pred_stage(bp):
        lane = slice(bp * 128, bp * 128 + 128)
        guess[:, lane] = dot(hid16[:, lane], halves)

    def loss_stage(bp, sums):
        loss_sum, bias_sum, out_sum = sums
        lane = slice(bp * 128, bp * 128 + 128)
        col_weight = col_mask[bp * 8 : bp * 8 + 8, :][None]
        for aq in range(8):
            row = slice(aq * 64, aq * 64 + 64)
            weight = (row_mask[row, :].reshape(8, 8, 128) * col_weight).reshape(64, 128)
            residue = guess[row, lane] - goal[row, lane]
            grad_pred = weight * residue
            grad_pre = grad_pred * weighted[row, lane]
            grads[128 + aq * 64 : 192 + aq * 64, bp * 128 + 128 : bp * 128 + 256] = grad_pre.astype(BF16)
            loss_sum = loss_sum + jnp.sum((grad_pred * residue).reshape(8, 8, 128), axis=0)
            bias_sum = bias_sum + jnp.sum(grad_pre.reshape(8, 8, 128), axis=0)
            out_sum = out_sum + jnp.sum((grad_pred * hid32[row, lane]).reshape(8, 8, 128), axis=0)
        return loss_sum, bias_sum, out_sum

    def weights_stage(bp):
        lane = bp * 128
        turned = grads[128:640, lane + 128 : lane + 256].T
        for ty in range(3):
            part = dot(turned, pair[ty * 64 : ty * 64 + 512, lane : lane + 256])
            if bp == 0:
                grad_w[:, ty * 256 : ty * 256 + 256] = part
            else:
                grad_w[:, ty * 256 : ty * 256 + 256] += part

    def back_stage(bp):
        lane = bp * 128
        part = dot(
            jnp.concatenate(
                [
                    jnp.concatenate(
                        [grads[(2 * a + t) * 64 : (2 * a + t) * 64 + 64, lane : lane + 256] for a in range(5)], axis=0
                    )
                    for t in range(4)
                ],
                axis=1,
            ),
            bwd_2[...],
        )
        col_sum = jnp.zeros((8, 128), F32)
        for a in range(5):
            for parity in range(2):
                row = (2 * a + parity) * 64
                block = (
                    part[a * 64 : a * 64 + 64, parity * 128 : parity * 128 + 128]
                    * slope[row : row + 64, lane : lane + 128]
                )
                if bp == 0:
                    grad_rows[row : row + 64, :] = block
                else:
                    grad_rows[row : row + 64, :] += block
                col_sum = col_sum + jnp.sum(block.reshape(8, 8, 128), axis=0)
        grad_cols[bp * 8 : bp * 8 + 8, :] = col_sum

    zero8 = jnp.zeros((8, 128), F32)
    totals = (zero8, zero8, zero8)
    for step in range(15):
        if step < 9:
            pair_stage(step)
        if 2 <= step < 10:
            conv_stage(step - 2)
        if 3 <= step < 11:
            act_stage(step - 3)
        if 6 <= step:
            back_stage(step - 6)
        if 5 <= step < 13:
            totals = loss_stage(step - 5, totals)
        if 6 <= step < 14:
            weights_stage(step - 6)
        if 4 <= step < 12:
            pred_stage(step - 4)

    row_part = jnp.sum(grad_rows[...].reshape(80, 8, 128), axis=1)
    place_u[...] = jnp.zeros(place_u.shape, F32)
    place_v[...] = jnp.zeros(place_v.shape, F32)
    place_u[pl.ds(pl.multiple_of(core * 64, 64), 80), :] = row_part + pltpu.roll(row_part, 64, 1)
    col_part = grad_cols[...]
    col_high = pltpu.roll(col_part, 64, 1).reshape(9, 1, 8, 128)
    place_v[pl.ds(pl.multiple_of(core * 64, 64), 144), :] = jnp.concatenate(
        [col_part.reshape(9, 1, 8, 128), col_high], axis=1
    ).reshape(144, 128)
    packed_u = jnp.where(half_lane, place_u[0:72, :], pltpu.roll(place_u[72:144, :], 64, 1))
    packed_v = jnp.where(half_lane, place_v[0:104, :], pltpu.roll(place_v[104:208, :], 64, 1))

    taps = []
    for ty in range(3):
        taps.append(
            grad_w[0:64, ty * 256 : ty * 256 + 192] + grad_w[64:128, ty * 256 + 64 : ty * 256 + 256]
        )
    conv_grad = jnp.concatenate(taps, axis=1)
    blocks = [conv_grad[:, k * 128 : k * 128 + 128] for k in range(4)]
    last = jnp.concatenate([conv_grad[0:32, 512:576], conv_grad[32:64, 512:576]], axis=1)

    loss_sum, bias_sum, out_sum = totals
    bias_row = jnp.sum(bias_sum, axis=0, keepdims=True)
    bias_row = bias_row + pltpu.roll(bias_row, 64, 1)
    out_row = jnp.sum(out_sum, axis=0, keepdims=True)
    out_row = out_row + pltpu.roll(out_row, 64, 1)
    small_row = jnp.where(half_lane, bias_row, out_row)
    loss_row = jnp.broadcast_to(jnp.sum(loss_sum, keepdims=True) * (0.5 / 64.0), (1, 128))
    small_hi = small_row.astype(BF16).astype(F32)
    loss_hi = loss_row.astype(BF16).astype(F32)
    tail = jnp.concatenate(
        [small_hi, small_row - small_hi, loss_hi, loss_row - loss_hi, jnp.zeros((4, 128), F32)], axis=0
    )
    first_core = jnp.concatenate([packed_u, last, blocks[2], blocks[3], tail], axis=0)
    second_core = jnp.concatenate([packed_v, blocks[0], blocks[1], tail], axis=0)
    keep[...] = jnp.where(core == 0, first_core, second_core)
    send[...] = jnp.where(core == 0, second_core, first_core).astype(BF16)


def tile_call(*operands):
    shapes = [
        ((80, 128), F32), ((72, 128), F32), ((640, 1152), BF16), ((640, 1152), F32), ((768, 1280), BF16),
        ((512, 1024), F32), ((512, 1024), BF16), ((512, 1024), F32), ((512, 1024), F32), ((512, 1024), F32),
        ((640, 128), F32), ((72, 128), F32), ((128, 768), F32), ((208, 128), F32), ((208, 128), F32),
        ((1024, 256), BF16), ((1024, 256), BF16),
    ]
    return pl.pallas_call(
        tile_kernel,
        out_shape=(jax.ShapeDtypeStruct((240, 128), F32), jax.ShapeDtypeStruct((240, 128), BF16)),
        in_specs=[pl.BlockSpec(memory_space=pltpu.VMEM)] * len(operands),
        out_specs=(pl.BlockSpec(memory_space=pltpu.VMEM),) * 2,
        scratch_shapes=[pltpu.VMEM(shape, kind) for shape, kind in shapes],
        compiler_params=pltpu.CompilerParams(vmem_limit_bytes=40 * 2**20),
        cost_estimate=pl.CostEstimate(flops=2 * 10**9, bytes_accessed=10**6, transcendentals=10**6),
        name="tiles",
    )(*operands)


def join_kernel(kept, received, out):
    first_core = lax.axis_index("band") % 2 == 0
    total = kept[...] + received[...].astype(F32)
    small = total[232:233] + total[233:234]
    loss = total[234:235] + total[235:236]
    small_hi = small.astype(BF16).astype(F32)
    loss_hi = loss.astype(BF16).astype(F32)
    tail = jnp.concatenate(
        [small_hi, small - small_hi, loss_hi, loss - loss_hi, jnp.zeros((2, 128), F32)], axis=0
    )

    def to_all(rows):
        return jnp.broadcast_to(rows[None], (CHIPS, rows.shape[0], 128))

    extra = jnp.concatenate(
        [total[72:88].reshape(CHIPS, 1, 128), total[88:104].reshape(CHIPS, 1, 128), to_all(tail)], axis=1
    )
    out[...] = jnp.concatenate(
        [
            to_all(total[0:72]),
            jnp.where(first_core, extra, to_all(total[72:80])),
            to_all(total[80:104]),
            total[104:232].reshape(CHIPS, 8, 128),
        ],
        axis=1,
    ).astype(BF16)


def join_call(kept, received):
    return pl.pallas_call(
        join_kernel,
        out_shape=jax.ShapeDtypeStruct((CHIPS, 112, 128), BF16),
        in_specs=[pl.BlockSpec(memory_space=pltpu.VMEM)] * 2,
        out_specs=pl.BlockSpec(memory_space=pltpu.VMEM),
        compiler_params=pltpu.CompilerParams(vmem_limit_bytes=16 * 2**20),
        name="join",
    )(kept, received)


def sum_kernel(parts, same, other, out, mine, theirs, bins):
    band = lax.axis_index("band")
    off = lax.axis_index("off")
    core = band % 2
    half_lane = lane_ids((1, 128)) < 64
    bins[...] = jnp.zeros(bins.shape, F32)
    split = jnp.where(core == 0, 72, 104)
    used = row_ids((104, 128)) < split
    for chip in range(CHIPS):
        piece = jnp.where(used, parts[chip].astype(F32)[0:104], 0.0)
        start = pl.multiple_of(chip // 2 * 128 + core * (chip % 2 * 128) + 56, 8)
        bins[pl.ds(start, 104), :] += piece
        bins[pl.ds(pl.multiple_of(start + split, 8), 104), :] += pltpu.roll(piece, 64, 1)

    def own_half(x):
        return jnp.where(
            core == 0, jnp.where(half_lane, x, 0.0), jnp.where(half_lane, 0.0, pltpu.roll(x, 64, 1))
        ).astype(BF16)

    sibling = band + 1 - 2 * core
    mine[...] = own_half(bins[pl.ds(pl.multiple_of(64 + 64 * band + 32 * off, 32), 32), :])
    theirs[...] = own_half(bins[pl.ds(pl.multiple_of(64 + 64 * sibling + 32 * off, 32), 32), :])
    halves = bins[64:1088, :].reshape(8, 2, 2, 32, 128)

    def dense(bands):
        return jnp.where(
            half_lane, bands[:, 0].reshape(256, 128), pltpu.roll(bands[:, 1].reshape(256, 128), 64, 1)
        )

    even, odd = dense(halves[:, 0]), dense(halves[:, 1])
    product = 0.0
    for cols, bands in (
        (same, jnp.where(core == 0, even, odd)), (other, jnp.where(core == 0, odd, even))
    ):
        product = product + lax.dot_general(
            cols[:, 64:96, :].reshape(256, 128), bands.astype(BF16), (((0,), (0,)), ((), ())),
            preferred_element_type=F32,
        )
    rows = product[0:64] + pltpu.roll(product[64:128], 64, 1)
    rows = jnp.where(half_lane, rows[0:32], pltpu.roll(rows[32:64], 64, 1))
    weights = jnp.sum(parts[:, 96:112, :].astype(F32), axis=0)[8:16]
    extra = jnp.sum(parts[:, 64:80, :].astype(F32), axis=0)[8:16]
    small = extra[2:3] + extra[3:4]
    loss = extra[4:5] + extra[5:6]
    small_hi = small.astype(BF16).astype(F32)
    loss_hi = loss.astype(BF16).astype(F32)
    whole = jnp.concatenate(
        [
            rows, weights, extra[0:2], small_hi, small - small_hi, loss_hi, loss - loss_hi,
            jnp.zeros((2, 128), F32),
        ],
        axis=0,
    )
    out[...] = jnp.broadcast_to(whole.astype(BF16)[None], (CHIPS, 48, 128))


def sum_call(parts, same, other):
    return pl.pallas_call(
        sum_kernel,
        out_shape=(
            jax.ShapeDtypeStruct((CHIPS, 48, 128), BF16),
            jax.ShapeDtypeStruct((32, 128), BF16),
            jax.ShapeDtypeStruct((32, 128), BF16),
        ),
        in_specs=[pl.BlockSpec(memory_space=pltpu.VMEM)] * 3,
        out_specs=(pl.BlockSpec(memory_space=pltpu.VMEM),) * 3,
        scratch_shapes=[pltpu.VMEM((1408, 128), F32)],
        compiler_params=pltpu.CompilerParams(vmem_limit_bytes=16 * 2**20),
        name="sums",
    )(parts, same, other)


def final_kernel(
    same, other, mine, received, w_proj,
    grad_proj_hbm, grad_conv_hbm, grad_feats_hbm, bias_hbm, w_out_hbm, loss_hbm,
    grad_proj, grad_conv_t, grad_feats, bias, w_out, loss, sems,
):
    is_first = lax.axis_index("band") % 2 == 0
    half_lane = lane_ids((1, 128)) < 64
    firsts, seconds = [], []
    puts = []
    for k in range(4):
        for chip in range(4 * k, 4 * k + 4):
            here = same[chip].astype(F32)
            there = other[chip].astype(F32)
            left = jnp.where(is_first, here, there)
            right = jnp.where(is_first, there, here)
            firsts.append(left[32:48])
            seconds.append(right[32:40])
            left, right = left[0:32], right[0:32]
            row = chip * 64
            grad_proj[row : row + 32, :] = jnp.where(half_lane, left, pltpu.roll(right, 64, 1))
            grad_proj[row + 32 : row + 64, :] = jnp.where(half_lane, pltpu.roll(left, 64, 1), right)
        rows = pl.ds(k * 256, 256)
        puts.append(pltpu.make_async_copy(grad_proj.at[rows], grad_proj_hbm.at[rows], sems.at[k]))
        puts[k].start()
    wide = jnp.concatenate(seconds + [first[0:8] for first in firsts], axis=0)
    for k in range(4):
        grad_conv_t[:, k * 128 : k * 128 + 128] = wide[k * 64 : k * 64 + 64]
    last = jnp.concatenate([first[8:9] for first in firsts] + [first[9:10] for first in firsts], axis=0)
    grad_conv_t[0:32, 512:576] = last[:, 0:64]
    grad_conv_t[32:64, 512:576] = last[:, 64:128]
    puts.append(pltpu.make_async_copy(grad_conv_t, grad_conv_hbm, sems.at[4]))
    puts[4].start()
    small = firsts[0][10:11] + firsts[0][11:12]
    bias[...] = small[:, 0:64]
    w_out[...] = small[:, 64:128]
    loss[...] = (firsts[0][12:13] + firsts[0][13:14])[:, 0:1]
    for k, (held, result) in enumerate(((bias, bias_hbm), (w_out, w_out_hbm), (loss, loss_hbm))):
        puts.append(pltpu.make_async_copy(held, result, sems.at[6 + k]))
        puts[5 + k].start()
    gproj = mine[...] + received[...]
    grad_feats[...] = lax.dot_general(
        gproj, w_proj[...], (((1,), (1,)), ((), ())), preferred_element_type=F32
    ).astype(BF16)
    put_feats = pltpu.make_async_copy(grad_feats, grad_feats_hbm, sems.at[5])
    put_feats.start()
    for put in puts + [put_feats]:
        put.wait()


def final_call(*operands):
    return pl.pallas_call(
        final_kernel,
        out_shape=(
            jax.ShapeDtypeStruct((1024, 128), F32),
            jax.ShapeDtypeStruct((64, 576), F32),
            jax.ShapeDtypeStruct((32, 1024), BF16),
            jax.ShapeDtypeStruct((1, 64), F32),
            jax.ShapeDtypeStruct((1, 64), F32),
            jax.ShapeDtypeStruct((1, 1), F32),
        ),
        in_specs=[pl.BlockSpec(memory_space=pltpu.VMEM)] * len(operands),
        out_specs=(pl.BlockSpec(memory_space=pltpu.HBM),) * 6,
        scratch_shapes=[
            pltpu.VMEM((1024, 128), F32),
            pltpu.VMEM((64, 576), F32),
            pltpu.VMEM((32, 1024), BF16),
            pltpu.VMEM((1, 64), F32),
            pltpu.VMEM((1, 64), F32),
            pltpu.VMEM((1, 1), F32),
            pltpu.SemaphoreType.DMA((9,)),
        ],
        compiler_params=pltpu.CompilerParams(vmem_limit_bytes=8 * 2**20),
        name="outputs",
    )(*operands)


def body(feats, w_proj, conv_w, conv_b, w_out, target, mask):
    swap = [(2 * i + o, 2 * (i + 1 - 2 * (i % 2)) + o) for i in range(BANDS) for o in range(2)]
    same_core = [[2 * i + o for i in range(core, BANDS, 2) for o in range(2)] for core in range(2)]
    same_row = [[2 * i + o for i in range(core, BANDS, 2)] for core in range(2) for o in range(2)]
    same = lax.all_to_all(front_call(feats, w_proj), GROUP, 0, 0, tiled=True, axis_index_groups=same_row)
    ready = prep_call(mask.reshape(8, 128), target, conv_w.T)
    same, ready = lax.optimization_barrier((same, ready))
    other = lax.ppermute(same, GROUP, swap)
    kept, given = tile_call(same, other, conv_b.reshape(1, 64), w_out.reshape(1, 64), *ready)
    joined = join_call(kept, lax.ppermute(given, GROUP, swap))
    parts = lax.all_to_all(joined, GROUP, 0, 0, tiled=True, axis_index_groups=same_core)
    sums, mine, theirs = sum_call(parts, same, other)
    every = lax.all_to_all(sums, GROUP, 0, 0, tiled=True, axis_index_groups=same_core)
    every, theirs = lax.optimization_barrier((every, theirs))
    grad_proj, grad_conv_t, grad_feats, bias, w_out, loss = final_call(
        every, lax.ppermute(every, GROUP, swap), mine, lax.ppermute(theirs, GROUP, swap), w_proj
    )
    return (loss.reshape(1), grad_proj, grad_conv_t.T, bias.reshape(64), w_out.reshape(64), grad_feats)


def solution(mesh):
    placed = (
        P(("rep", "band"), None),
        P(),
        P(),
        P(),
        P(),
        P(("rep", "band"), "off", None),
        P("rep"),
    )
    return jax.shard_map(
        body,
        mesh=mesh,
        in_specs=placed,
        out_specs=(
            P("rep"),
            P("rep", None),
            P("rep", None),
            P("rep"),
            P("rep"),
            P(("rep", "band", "off"), None),
        ),
        check_vma=False,
    )
```

```python
import jax
import jax.numpy as jnp
from jax import lax
from jax.experimental import pallas as pl
from jax.experimental.pallas import tpu as pltpu
from jax.sharding import PartitionSpec as P

GELU_K = 0.7978845608028654
GELU_C = 0.044715
GROUP = ("band", "off")
CHIPS = 16
BANDS = 16
F32 = jnp.float32
BF16 = jnp.bfloat16


def gelu_parts(x, half):
    inner = GELU_K + (GELU_K * GELU_C) * (x * x)
    gate = half + half * jnp.tanh(x * inner)
    value = x * gate
    slope = gate + (value * (1.0 - gate)) * (6.0 * inner - 4.0 * GELU_K)
    return value, slope


def lane_ids(shape):
    return lax.broadcasted_iota(jnp.int32, shape, len(shape) - 1)


def row_ids(shape):
    return lax.broadcasted_iota(jnp.int32, shape, len(shape) - 2)


def dot(a, b):
    return jnp.dot(a, b, preferred_element_type=F32)


def front_kernel(feats_hbm, w_proj_hbm, out, feats, w_proj, sems):
    off = lax.axis_index("off")
    get_feats = pltpu.make_async_copy(feats_hbm, feats, sems.at[0])
    get_w = pltpu.make_async_copy(w_proj_hbm, w_proj, sems.at[1])
    get_feats.start()
    get_w.start()
    get_feats.wait()
    half_lane = lane_ids((1, 128)) < 64
    for q in range(8):
        block = feats[:, q * 128 : q * 128 + 128].astype(F32)
        top, bottom = block[0:32], block[32:64]
        low = jnp.where(half_lane, top, pltpu.roll(bottom, 64, 1))
        high = jnp.where(half_lane, pltpu.roll(top, 64, 1), bottom)
        out[q, 64:96, :] = jnp.where(off == 0, low, high).astype(BF16)
    get_w.wait()
    proj = dot(feats[...], w_proj[...]).astype(BF16)
    out[:, 0:64, :] = jnp.broadcast_to(proj[None], (8, 64, 128))


def front_call(feats, w_proj):
    return pl.pallas_call(
        front_kernel,
        out_shape=jax.ShapeDtypeStruct((8, 96, 128), BF16),
        in_specs=[pl.BlockSpec(memory_space=pltpu.HBM)] * 2,
        out_specs=pl.BlockSpec(memory_space=pltpu.VMEM),
        scratch_shapes=[
            pltpu.VMEM((64, 1024), BF16),
            pltpu.VMEM((1024, 128), BF16),
            pltpu.SemaphoreType.DMA((2,)),
        ],
        compiler_params=pltpu.CompilerParams(vmem_limit_bytes=60 * 2**20),
        name="front",
    )(feats, w_proj)


def prep_kernel(
    mask, target, conv_t, fwd_w, bwd_w, goal, row_mask, col_mask
):
    band = lax.axis_index("band")
    first = band + 2 * lax.axis_index("off")
    half_lane = lane_ids((1, 128)) < 64

    blank = jnp.zeros((64, 64), F32)
    for ty in range(3):
        taps = [conv_t[:, (3 * ty + tx) * 64 : (3 * ty + tx + 1) * 64].astype(F32) for tx in range(3)]
        low = jnp.concatenate(taps + [blank], axis=1)
        high = jnp.concatenate([blank] + taps, axis=1)
        fwd_w[ty * 256 : ty * 256 + 256, :] = jnp.concatenate([low, high], axis=0).T.astype(BF16)
        left = taps[::-1] + [blank]
        right = [blank] + taps[::-1]
        for k in range(4):
            row = ty * 256 + k * 64
            bwd_w[row : row + 64, :] = jnp.concatenate([left[k], right[k]], axis=1).astype(BF16)
    mask_all = mask[...].astype(F32)
    mask_lane = lane_ids((8, 128))
    by_band = jnp.concatenate(
        [jnp.where(mask_lane < 64, mask_all, 0.0), jnp.where(mask_lane < 64, 0.0, mask_all)], axis=0
    ).astype(BF16)
    sums_row = dot(by_band, jnp.ones((128, 128), BF16))
    sums_col = lax.dot_general(
        jnp.ones((16, 128), BF16), by_band, (((1,), (1,)), ((), ())), preferred_element_type=F32
    )
    at = lax.broadcasted_iota(jnp.int32, (16, 16), 0)
    to = lax.broadcasted_iota(jnp.int32, (16, 16), 1)
    apart = (2 * (to % 8) + to // 8) - (2 * (at % 8) + at // 8)
    near_diagonal = (apart >= 0) & (apart < 4)
    count = jnp.sum(jnp.where(near_diagonal, sums_row[:, 0:16] * sums_col, 0.0))
    scale = 1.0 / count

    def mask_rows(which):
        inside = jnp.minimum(which, 15)
        line = mask[pl.ds(inside // 2, 1), :].astype(F32)
        line = jnp.where(which < 16, line, 0.0)
        spot = row_ids((64, 128)) + 64 * (inside % 2)
        spread = jnp.where(lane_ids((64, 128)) == spot, line, 0.0)
        return dot(spread.astype(BF16), jnp.ones((128, 128), BF16))

    row_mask[...] = (
        jnp.broadcast_to(mask_rows(band)[:, None, :] * (2.0 * scale), (64, 8, 128)).reshape(512, 128)
    )
    col_all = jnp.concatenate([mask_rows(first), mask_rows(first + 1)], axis=0).reshape(8, 2, 8, 128)
    col_mask[...] = jnp.where(half_lane, col_all[:, 0].reshape(64, 128), col_all[:, 1].reshape(64, 128))

    line = jnp.concatenate([target[:, 0, :], target[:, 1, :]], axis=1)
    lines = jnp.broadcast_to(line[:, None, :], (64, 8, 128)).reshape(512, 128)
    lines = jnp.where(lane_ids((512, 128)) % 8 == row_ids((512, 128)) % 8, lines, 0.0)
    lines_hi = lines.astype(BF16)
    lines_lo = (lines - lines_hi.astype(F32)).astype(BF16)
    spread = (
        (row_ids((128, 1024)) // 8 == lane_ids((128, 1024)) // 64).astype(F32).astype(BF16)
    )
    goal[...] = dot(
        jnp.concatenate([lines_hi, lines_lo], axis=1), jnp.concatenate([spread, spread], axis=0)
    )


def prep_call(*operands):
    shapes = [
        ((768, 128), BF16), ((768, 128), BF16), ((512, 1024), F32), ((512, 128), F32), ((64, 128), F32),
    ]
    return pl.pallas_call(
        prep_kernel,
        out_shape=tuple(jax.ShapeDtypeStruct(shape, kind) for shape, kind in shapes),
        in_specs=[pl.BlockSpec(memory_space=pltpu.VMEM)] * len(operands),
        out_specs=(pl.BlockSpec(memory_space=pltpu.VMEM),) * len(shapes),
        compiler_params=pltpu.CompilerParams(vmem_limit_bytes=16 * 2**20),
        cost_estimate=pl.CostEstimate(flops=3 * 10**8, bytes_accessed=4 * 10**6, transcendentals=0),
        name="prepare",
    )(*operands)


def tile_kernel(
    same, other, conv_b, w_out, fwd_w, bwd_w, goal, row_mask, col_mask,
    keep, send,
    rows_u, cols_v, pair, slope, grads, pre, hid16, hid32, weighted, guess, grad_rows, grad_cols, grad_w,
    place_u, place_v, fwd_2, bwd_2,
):
    band = lax.axis_index("band")
    core = band % 2
    first = band + 2 * lax.axis_index("off")
    half_lane = lane_ids((1, 128)) < 64

    none = jnp.zeros((256, 128), BF16)
    for t in range(4):
        for parity in range(2):
            ty = t - parity
            fwd_2[t * 256 : t * 256 + 256, parity * 128 : parity * 128 + 128] = (
                fwd_w[ty * 256 : ty * 256 + 256, :] if 0 <= ty < 3 else none
            )
    for t, taps in enumerate(((2, None, 0, 1), (1, 2, None, 0))):
        for k, ty in enumerate(taps):
            bwd_2[t * 256 : t * 256 + 256, k * 128 : k * 128 + 128] = (
                none if ty is None else bwd_w[ty * 256 : ty * 256 + 256, :]
            )

    def channels(which, rows):
        inside = jnp.clip(which, 0, BANDS - 1)
        at = inside // 2
        return jnp.where(
            inside % 2 == core, same[at, rows, :].astype(F32), other[at, rows, :].astype(F32)
        )

    def ending(which):
        return channels(which, slice(48, 64))[8:16]

    def whole(which):
        return channels(which, slice(0, 64))

    def opening(which):
        return channels(which, slice(0, 16))[0:8]

    u = jnp.concatenate([ending(band - 1), whole(band), opening(band + 1)], axis=0)
    rows_u[...] = jnp.where(half_lane, u, pltpu.roll(u, 64, 1))
    v = jnp.concatenate(
        [ending(first - 1), whole(first), whole(first + 1), opening(first + 2)], axis=0
    ).reshape(9, 2, 8, 128)
    v_low = v[:, 0].reshape(72, 128)
    v_high = v[:, 1].reshape(72, 128)
    cols_v[...] = jnp.where(half_lane, pltpu.roll(v_low, 64, 1), v_high)

    bias2 = jnp.concatenate([conv_b[...], conv_b[...]], axis=1)
    out_w2 = jnp.concatenate([w_out[...], w_out[...]], axis=1)
    halves = ((row_ids((128, 128)) < 64) == (lane_ids((128, 128)) < 64)).astype(F32).astype(BF16)

    def pair_stage(bp):
        lane = slice(bp * 128, bp * 128 + 128)
        block = first * 8 - 1 + 2 * bp
        spot = jnp.where(half_lane, block, block + 1)
        col_in = jnp.where((spot >= 0) & (spot < 128), 0.5, 0.0)
        v_here = cols_v[bp * 8 : bp * 8 + 8, :][None]
        for aq in range(10):
            half = col_in
            if aq == 0:
                half = jnp.where(band == 0, 0.0, col_in)
            if aq == 9:
                half = jnp.where(band == BANDS - 1, 0.0, col_in)
            x = (rows_u[aq * 8 : aq * 8 + 8, :][:, None, :] + v_here).reshape(64, 128)
            value, grade = gelu_parts(x, half)
            pair[aq * 64 : aq * 64 + 64, lane] = value.astype(BF16)
            slope[aq * 64 : aq * 64 + 64, lane] = grade

    def conv_stage(bp):
        lane = bp * 128
        part = dot(
            jnp.concatenate(
                [
                    jnp.concatenate(
                        [pair[(2 * a + t) * 64 : (2 * a + t) * 64 + 64, lane : lane + 256] for a in range(4)], axis=0
                    )
                    for t in range(4)
                ],
                axis=1,
            ),
            fwd_2[...],
        )
        for a in range(4):
            for parity in range(2):
                row = (2 * a + parity) * 64
                pre[row : row + 64, lane : lane + 128] = part[a * 64 : a * 64 + 64, parity * 128 : parity * 128 + 128]

    def act_stage(bp):
        lane = slice(bp * 128, bp * 128 + 128)
        for aq in range(8):
            row = slice(aq * 64, aq * 64 + 64)
            value, grade = gelu_parts(pre[row, lane] + bias2, 0.5)
            hid32[row, lane] = value
            hid16[row, lane] = (value * out_w2).astype(BF16)
            weighted[row, lane] = grade * out_w2

    def pred_stage(bp):
        lane = slice(bp * 128, bp * 128 + 128)
        guess[:, lane] = dot(hid16[:, lane], halves)

    def loss_stage(bp, sums):
        loss_sum, bias_sum, out_sum = sums
        lane = slice(bp * 128, bp * 128 + 128)
        col_weight = col_mask[bp * 8 : bp * 8 + 8, :][None]
        for aq in range(8):
            row = slice(aq * 64, aq * 64 + 64)
            weight = (row_mask[row, :].reshape(8, 8, 128) * col_weight).reshape(64, 128)
            residue = guess[row, lane] - goal[row, lane]
            grad_pred = weight * residue
            grad_pre = grad_pred * weighted[row, lane]
            grads[row, lane] = grad_pre.astype(BF16)
            loss_sum = loss_sum + jnp.sum((grad_pred * residue).reshape(8, 8, 128), axis=0)
            bias_sum = bias_sum + jnp.sum(grad_pre.reshape(8, 8, 128), axis=0)
            out_sum = out_sum + jnp.sum((grad_pred * hid32[row, lane]).reshape(8, 8, 128), axis=0)
        return loss_sum, bias_sum, out_sum

    def weights_stage(bp):
        lane = bp * 128
        turned = grads[:, lane : lane + 128].T
        for ty in range(3):
            part = dot(turned, pair[ty * 64 : ty * 64 + 512, lane : lane + 256])
            if bp == 0:
                grad_w[:, ty * 256 : ty * 256 + 256] = part
            else:
                grad_w[:, ty * 256 : ty * 256 + 256] += part

    def back_stage(bp):
        lane = bp * 128
        left, right = max(bp - 1, 0) * 128, min(bp + 1, 8) * 128
        rows = jnp.concatenate(
            [
                jnp.concatenate(
                    [grads[(2 * a + t) * 64 : (2 * a + t) * 64 + 64, left:right] for a in range(4)], axis=0
                )
                for t in range(2)
            ],
            axis=1,
        )
        if bp == 0:
            both = dot(rows, jnp.concatenate([bwd_2[128:256, :], bwd_2[384:512, :]], axis=0))
        elif bp == 8:
            both = dot(rows, jnp.concatenate([bwd_2[0:128, :], bwd_2[256:384, :]], axis=0))
        else:
            both = dot(rows, bwd_2[...])
        col_sum = jnp.zeros((8, 128), F32)
        for a in range(5):
            for parity in range(2):
                row = (2 * a + parity) * 64
                block = 0.0
                if a < 4:
                    block = both[a * 64 : a * 64 + 64, 256 + parity * 128 : 384 + parity * 128]
                if a > 0:
                    block = block + both[a * 64 - 64 : a * 64, parity * 128 : parity * 128 + 128]
                block = block * slope[row : row + 64, lane : lane + 128]
                if bp == 0:
                    grad_rows[row : row + 64, :] = block
                else:
                    grad_rows[row : row + 64, :] += block
                col_sum = col_sum + jnp.sum(block.reshape(8, 8, 128), axis=0)
        grad_cols[bp * 8 : bp * 8 + 8, :] = col_sum

    zero8 = jnp.zeros((8, 128), F32)
    totals = (zero8, zero8, zero8)
    for step in range(15):
        if step < 9:
            pair_stage(step)
        if 2 <= step < 10:
            conv_stage(step - 2)
        if 3 <= step < 11:
            act_stage(step - 3)
        if 6 <= step:
            back_stage(step - 6)
        if 5 <= step < 13:
            totals = loss_stage(step - 5, totals)
        if 6 <= step < 14:
            weights_stage(step - 6)
        if 4 <= step < 12:
            pred_stage(step - 4)

    row_part = jnp.sum(grad_rows[...].reshape(80, 8, 128), axis=1)
    place_u[...] = jnp.zeros(place_u.shape, F32)
    place_v[...] = jnp.zeros(place_v.shape, F32)
    place_u[pl.ds(pl.multiple_of(core * 64, 64), 80), :] = row_part + pltpu.roll(row_part, 64, 1)
    col_part = grad_cols[...]
    col_high = pltpu.roll(col_part, 64, 1).reshape(9, 1, 8, 128)
    place_v[pl.ds(pl.multiple_of(core * 64, 64), 144), :] = jnp.concatenate(
        [col_part.reshape(9, 1, 8, 128), col_high], axis=1
    ).reshape(144, 128)
    packed_u = jnp.where(half_lane, place_u[0:72, :], pltpu.roll(place_u[72:144, :], 64, 1))
    packed_v = jnp.where(half_lane, place_v[0:104, :], pltpu.roll(place_v[104:208, :], 64, 1))

    taps = []
    for ty in range(3):
        taps.append(
            grad_w[0:64, ty * 256 : ty * 256 + 192] + grad_w[64:128, ty * 256 + 64 : ty * 256 + 256]
        )
    conv_grad = jnp.concatenate(taps, axis=1)
    blocks = [conv_grad[:, k * 128 : k * 128 + 128] for k in range(4)]
    last = jnp.concatenate([conv_grad[0:32, 512:576], conv_grad[32:64, 512:576]], axis=1)

    loss_sum, bias_sum, out_sum = totals
    bias_row = jnp.sum(bias_sum, axis=0, keepdims=True)
    bias_row = bias_row + pltpu.roll(bias_row, 64, 1)
    out_row = jnp.sum(out_sum, axis=0, keepdims=True)
    out_row = out_row + pltpu.roll(out_row, 64, 1)
    small_row = jnp.where(half_lane, bias_row, out_row)
    loss_row = jnp.broadcast_to(jnp.sum(loss_sum, keepdims=True) * (0.5 / 64.0), (1, 128))
    small_hi = small_row.astype(BF16).astype(F32)
    loss_hi = loss_row.astype(BF16).astype(F32)
    tail = jnp.concatenate(
        [small_hi, small_row - small_hi, loss_hi, loss_row - loss_hi, jnp.zeros((4, 128), F32)], axis=0
    )
    first_core = jnp.concatenate([packed_u, last, blocks[2], blocks[3], tail], axis=0)
    second_core = jnp.concatenate([packed_v, blocks[0], blocks[1], tail], axis=0)
    keep[...] = jnp.where(core == 0, first_core, second_core)
    send[...] = jnp.where(core == 0, second_core, first_core).astype(BF16)


def tile_call(*operands):
    shapes = [
        ((80, 128), F32), ((72, 128), F32), ((640, 1152), BF16), ((640, 1152), F32), ((512, 1024), BF16),
        ((512, 1024), F32), ((512, 1024), BF16), ((512, 1024), F32), ((512, 1024), F32), ((512, 1024), F32),
        ((640, 128), F32), ((72, 128), F32), ((128, 768), F32), ((208, 128), F32), ((208, 128), F32),
        ((1024, 256), BF16), ((512, 512), BF16),
    ]
    return pl.pallas_call(
        tile_kernel,
        out_shape=(jax.ShapeDtypeStruct((240, 128), F32), jax.ShapeDtypeStruct((240, 128), BF16)),
        in_specs=[pl.BlockSpec(memory_space=pltpu.VMEM)] * len(operands),
        out_specs=(pl.BlockSpec(memory_space=pltpu.VMEM),) * 2,
        scratch_shapes=[pltpu.VMEM(shape, kind) for shape, kind in shapes],
        compiler_params=pltpu.CompilerParams(vmem_limit_bytes=40 * 2**20),
        cost_estimate=pl.CostEstimate(flops=2 * 10**9, bytes_accessed=10**6, transcendentals=10**6),
        name="tiles",
    )(*operands)


def join_kernel(kept, received, out):
    first_core = lax.axis_index("band") % 2 == 0
    total = kept[...] + received[...].astype(F32)
    small = total[232:233] + total[233:234]
    loss = total[234:235] + total[235:236]
    small_hi = small.astype(BF16).astype(F32)
    loss_hi = loss.astype(BF16).astype(F32)
    tail = jnp.concatenate(
        [small_hi, small - small_hi, loss_hi, loss - loss_hi, jnp.zeros((2, 128), F32)], axis=0
    )

    def to_all(rows):
        return jnp.broadcast_to(rows[None], (CHIPS, rows.shape[0], 128))

    extra = jnp.concatenate(
        [total[72:88].reshape(CHIPS, 1, 128), total[88:104].reshape(CHIPS, 1, 128), to_all(tail)], axis=1
    )
    out[...] = jnp.concatenate(
        [
            to_all(total[0:72]),
            jnp.where(first_core, extra, to_all(total[72:80])),
            to_all(total[80:104]),
            total[104:232].reshape(CHIPS, 8, 128),
        ],
        axis=1,
    ).astype(BF16)


def join_call(kept, received):
    return pl.pallas_call(
        join_kernel,
        out_shape=jax.ShapeDtypeStruct((CHIPS, 112, 128), BF16),
        in_specs=[pl.BlockSpec(memory_space=pltpu.VMEM)] * 2,
        out_specs=pl.BlockSpec(memory_space=pltpu.VMEM),
        compiler_params=pltpu.CompilerParams(vmem_limit_bytes=16 * 2**20),
        name="join",
    )(kept, received)


def sum_kernel(parts, same, other, out, mine, theirs, bins):
    band = lax.axis_index("band")
    off = lax.axis_index("off")
    core = band % 2
    half_lane = lane_ids((1, 128)) < 64
    bins[...] = jnp.zeros(bins.shape, F32)
    split = jnp.where(core == 0, 72, 104)
    used = row_ids((104, 128)) < split
    def piece(chip):
        return parts[chip].astype(F32)[0:104] if 0 <= chip < CHIPS else 0.0

    for step in range(9):
        both = piece(2 * step) + jnp.where(core == 0, piece(2 * step + 1), piece(2 * step - 1))
        both = jnp.where(used, both, 0.0)
        start = step * 128 + 56
        bins[start : start + 104, :] += both
        bins[pl.ds(pl.multiple_of(start + split, 8), 104), :] += pltpu.roll(both, 64, 1)

    def own_half(x):
        return jnp.where(
            core == 0, jnp.where(half_lane, x, 0.0), jnp.where(half_lane, 0.0, pltpu.roll(x, 64, 1))
        ).astype(BF16)

    sibling = band + 1 - 2 * core
    mine[...] = own_half(bins[pl.ds(pl.multiple_of(64 + 64 * band + 32 * off, 32), 32), :])
    theirs[...] = own_half(bins[pl.ds(pl.multiple_of(64 + 64 * sibling + 32 * off, 32), 32), :])
    halves = bins[64:1088, :].reshape(8, 2, 2, 32, 128)

    def dense(bands):
        return jnp.where(
            half_lane, bands[:, 0].reshape(256, 128), pltpu.roll(bands[:, 1].reshape(256, 128), 64, 1)
        )

    even, odd = dense(halves[:, 0]), dense(halves[:, 1])
    product = 0.0
    for cols, bands in (
        (same, jnp.where(core == 0, even, odd)), (other, jnp.where(core == 0, odd, even))
    ):
        product = product + lax.dot_general(
            cols[:, 64:96, :].reshape(256, 128), bands.astype(BF16), (((0,), (0,)), ((), ())),
            preferred_element_type=F32,
        )
    rows = product[0:64] + pltpu.roll(product[64:128], 64, 1)
    rows = jnp.where(half_lane, rows[0:32], pltpu.roll(rows[32:64], 64, 1))
    weights = jnp.sum(parts[:, 96:112, :].astype(F32), axis=0)[8:16]
    extra = jnp.sum(parts[:, 64:80, :].astype(F32), axis=0)[8:16]
    small = extra[2:3] + extra[3:4]
    loss = extra[4:5] + extra[5:6]
    small_hi = small.astype(BF16).astype(F32)
    loss_hi = loss.astype(BF16).astype(F32)
    whole = jnp.concatenate(
        [
            rows, weights, extra[0:2], small_hi, small - small_hi, loss_hi, loss - loss_hi,
            jnp.zeros((2, 128), F32),
        ],
        axis=0,
    )
    out[...] = jnp.broadcast_to(whole.astype(BF16)[None], (CHIPS, 48, 128))


def sum_call(parts, same, other):
    return pl.pallas_call(
        sum_kernel,
        out_shape=(
            jax.ShapeDtypeStruct((CHIPS, 48, 128), BF16),
            jax.ShapeDtypeStruct((32, 128), BF16),
            jax.ShapeDtypeStruct((32, 128), BF16),
        ),
        in_specs=[pl.BlockSpec(memory_space=pltpu.VMEM)] * 3,
        out_specs=(pl.BlockSpec(memory_space=pltpu.VMEM),) * 3,
        scratch_shapes=[pltpu.VMEM((1408, 128), F32)],
        compiler_params=pltpu.CompilerParams(vmem_limit_bytes=16 * 2**20),
        name="sums",
    )(parts, same, other)


def final_kernel(
    same, other, mine, received, w_proj,
    grad_proj_hbm, grad_conv_hbm, grad_feats_hbm, bias_hbm, w_out_hbm, loss_hbm,
    grad_proj, grad_conv_t, grad_feats, bias, w_out, loss, sems,
):
    is_first = lax.axis_index("band") % 2 == 0
    half_lane = lane_ids((1, 128)) < 64
    firsts, seconds = [], []
    puts = []
    for k in range(4):
        for chip in range(4 * k, 4 * k + 4):
            here = same[chip].astype(F32)
            there = other[chip].astype(F32)
            left = jnp.where(is_first, here, there)
            right = jnp.where(is_first, there, here)
            firsts.append(left[32:48])
            seconds.append(right[32:40])
            left, right = left[0:32], right[0:32]
            row = chip * 64
            grad_proj[row : row + 32, :] = jnp.where(half_lane, left, pltpu.roll(right, 64, 1))
            grad_proj[row + 32 : row + 64, :] = jnp.where(half_lane, pltpu.roll(left, 64, 1), right)
        rows = pl.ds(k * 256, 256)
        puts.append(pltpu.make_async_copy(grad_proj.at[rows], grad_proj_hbm.at[rows], sems.at[k]))
        puts[k].start()
    wide = jnp.concatenate(seconds + [first[0:8] for first in firsts], axis=0)
    for k in range(4):
        grad_conv_t[:, k * 128 : k * 128 + 128] = wide[k * 64 : k * 64 + 64]
    last = jnp.concatenate([first[8:9] for first in firsts] + [first[9:10] for first in firsts], axis=0)
    grad_conv_t[0:32, 512:576] = last[:, 0:64]
    grad_conv_t[32:64, 512:576] = last[:, 64:128]
    puts.append(pltpu.make_async_copy(grad_conv_t, grad_conv_hbm, sems.at[4]))
    puts[4].start()
    small = firsts[0][10:11] + firsts[0][11:12]
    bias[...] = small[:, 0:64]
    w_out[...] = small[:, 64:128]
    loss[...] = (firsts[0][12:13] + firsts[0][13:14])[:, 0:1]
    for k, (held, result) in enumerate(((bias, bias_hbm), (w_out, w_out_hbm), (loss, loss_hbm))):
        puts.append(pltpu.make_async_copy(held, result, sems.at[6 + k]))
        puts[5 + k].start()
    gproj = mine[...] + received[...]
    grad_feats[...] = lax.dot_general(
        gproj, w_proj[...], (((1,), (1,)), ((), ())), preferred_element_type=F32
    ).astype(BF16)
    put_feats = pltpu.make_async_copy(grad_feats, grad_feats_hbm, sems.at[5])
    put_feats.start()
    for put in puts + [put_feats]:
        put.wait()


def final_call(*operands):
    return pl.pallas_call(
        final_kernel,
        out_shape=(
            jax.ShapeDtypeStruct((1024, 128), F32),
            jax.ShapeDtypeStruct((64, 576), F32),
            jax.ShapeDtypeStruct((32, 1024), BF16),
            jax.ShapeDtypeStruct((1, 64), F32),
            jax.ShapeDtypeStruct((1, 64), F32),
            jax.ShapeDtypeStruct((1, 1), F32),
        ),
        in_specs=[pl.BlockSpec(memory_space=pltpu.VMEM)] * len(operands),
        out_specs=(pl.BlockSpec(memory_space=pltpu.HBM),) * 6,
        scratch_shapes=[
            pltpu.VMEM((1024, 128), F32),
            pltpu.VMEM((64, 576), F32),
            pltpu.VMEM((32, 1024), BF16),
            pltpu.VMEM((1, 64), F32),
            pltpu.VMEM((1, 64), F32),
            pltpu.VMEM((1, 1), F32),
            pltpu.SemaphoreType.DMA((9,)),
        ],
        compiler_params=pltpu.CompilerParams(vmem_limit_bytes=8 * 2**20),
        name="outputs",
    )(*operands)


def body(feats, w_proj, conv_w, conv_b, w_out, target, mask):
    swap = [(2 * i + o, 2 * (i + 1 - 2 * (i % 2)) + o) for i in range(BANDS) for o in range(2)]
    same_core = [[2 * i + o for i in range(core, BANDS, 2) for o in range(2)] for core in range(2)]
    same_row = [[2 * i + o for i in range(core, BANDS, 2)] for core in range(2) for o in range(2)]
    same = lax.all_to_all(front_call(feats, w_proj), GROUP, 0, 0, tiled=True, axis_index_groups=same_row)
    ready = prep_call(mask.reshape(8, 128), target, conv_w.T)
    same, ready = lax.optimization_barrier((same, ready))
    other = lax.ppermute(same, GROUP, swap)
    kept, given = tile_call(same, other, conv_b.reshape(1, 64), w_out.reshape(1, 64), *ready)
    joined = join_call(kept, lax.ppermute(given, GROUP, swap))
    parts = lax.all_to_all(joined, GROUP, 0, 0, tiled=True, axis_index_groups=same_core)
    sums, mine, theirs = sum_call(parts, same, other)
    every = lax.all_to_all(sums, GROUP, 0, 0, tiled=True, axis_index_groups=same_core)
    every, theirs = lax.optimization_barrier((every, theirs))
    grad_proj, grad_conv_t, grad_feats, bias, w_out, loss = final_call(
        every, lax.ppermute(every, GROUP, swap), mine, lax.ppermute(theirs, GROUP, swap), w_proj
    )
    return (loss.reshape(1), grad_proj, grad_conv_t.T, bias.reshape(64), w_out.reshape(64), grad_feats)


def solution(mesh):
    placed = (
        P(("rep", "band"), None),
        P(),
        P(),
        P(),
        P(),
        P(("rep", "band"), "off", None),
        P("rep"),
    )
    return jax.shard_map(
        body,
        mesh=mesh,
        in_specs=placed,
        out_specs=(
            P("rep"),
            P("rep", None),
            P("rep", None),
            P("rep"),
            P("rep"),
            P(("rep", "band", "off"), None),
        ),
        check_vma=False,
    )
```

```python
import jax
import jax.numpy as jnp
from jax import lax
from jax.experimental import pallas as pl
from jax.experimental.pallas import tpu as pltpu
from jax.sharding import PartitionSpec as P

GELU_K = 0.7978845608028654
GELU_C = 0.044715
GROUP = ("band", "off")
CHIPS = 16
BANDS = 16
F32 = jnp.float32
BF16 = jnp.bfloat16


def gelu_parts(x, half):
    inner = GELU_K + (GELU_K * GELU_C) * (x * x)
    gate = half + half * jnp.tanh(x * inner)
    value = x * gate
    slope = gate + (value * (1.0 - gate)) * (6.0 * inner - 4.0 * GELU_K)
    return value, slope


def lane_ids(shape):
    return lax.broadcasted_iota(jnp.int32, shape, len(shape) - 1)


def row_ids(shape):
    return lax.broadcasted_iota(jnp.int32, shape, len(shape) - 2)


def dot(a, b):
    return jnp.dot(a, b, preferred_element_type=F32)


def front_kernel(feats_hbm, w_proj_hbm, out, feats, w_proj, sems):
    off = lax.axis_index("off")
    get_feats = pltpu.make_async_copy(feats_hbm, feats, sems.at[0])
    get_w = pltpu.make_async_copy(w_proj_hbm, w_proj, sems.at[1])
    get_feats.start()
    get_w.start()
    get_feats.wait()
    half_lane = lane_ids((1, 128)) < 64
    for q in range(8):
        block = feats[:, q * 128 : q * 128 + 128].astype(F32)
        top, bottom = block[0:32], block[32:64]
        low = jnp.where(half_lane, top, pltpu.roll(bottom, 64, 1))
        high = jnp.where(half_lane, pltpu.roll(top, 64, 1), bottom)
        out[q, 64:96, :] = jnp.where(off == 0, low, high).astype(BF16)
    get_w.wait()
    proj = dot(feats[...], w_proj[...]).astype(BF16)
    out[:, 0:64, :] = jnp.broadcast_to(proj[None], (8, 64, 128))


def front_call(feats, w_proj):
    return pl.pallas_call(
        front_kernel,
        out_shape=jax.ShapeDtypeStruct((8, 96, 128), BF16),
        in_specs=[pl.BlockSpec(memory_space=pltpu.HBM)] * 2,
        out_specs=pl.BlockSpec(memory_space=pltpu.VMEM),
        scratch_shapes=[
            pltpu.VMEM((64, 1024), BF16),
            pltpu.VMEM((1024, 128), BF16),
            pltpu.SemaphoreType.DMA((2,)),
        ],
        compiler_params=pltpu.CompilerParams(vmem_limit_bytes=60 * 2**20),
        name="front",
    )(feats, w_proj)


def prep_kernel(
    mask, target, conv_t, fwd_w, bwd_w, goal, row_mask, col_mask
):
    band = lax.axis_index("band")
    first = band + 2 * lax.axis_index("off")
    half_lane = lane_ids((1, 128)) < 64

    blank = jnp.zeros((64, 64), F32)
    for ty in range(3):
        taps = [conv_t[:, (3 * ty + tx) * 64 : (3 * ty + tx + 1) * 64].astype(F32) for tx in range(3)]
        low = jnp.concatenate(taps + [blank], axis=1)
        high = jnp.concatenate([blank] + taps, axis=1)
        fwd_w[ty * 256 : ty * 256 + 256, :] = jnp.concatenate([low, high], axis=0).T.astype(BF16)
        left = taps[::-1] + [blank]
        right = [blank] + taps[::-1]
        for k in range(4):
            row = ty * 256 + k * 64
            bwd_w[row : row + 64, :] = jnp.concatenate([left[k], right[k]], axis=1).astype(BF16)
    mask_all = mask[...].astype(F32)
    mask_lane = lane_ids((8, 128))
    by_band = jnp.concatenate(
        [jnp.where(mask_lane < 64, mask_all, 0.0), jnp.where(mask_lane < 64, 0.0, mask_all)], axis=0
    ).astype(BF16)
    sums_row = dot(by_band, jnp.ones((128, 128), BF16))
    sums_col = lax.dot_general(
        jnp.ones((16, 128), BF16), by_band, (((1,), (1,)), ((), ())), preferred_element_type=F32
    )
    at = lax.broadcasted_iota(jnp.int32, (16, 16), 0)
    to = lax.broadcasted_iota(jnp.int32, (16, 16), 1)
    apart = (2 * (to % 8) + to // 8) - (2 * (at % 8) + at // 8)
    near_diagonal = (apart >= 0) & (apart < 4)
    count = jnp.sum(jnp.where(near_diagonal, sums_row[:, 0:16] * sums_col, 0.0))
    scale = 1.0 / count

    def mask_rows(which):
        inside = jnp.minimum(which, 15)
        line = mask[pl.ds(inside // 2, 1), :].astype(F32)
        line = jnp.where(which < 16, line, 0.0)
        spot = row_ids((64, 128)) + 64 * (inside % 2)
        spread = jnp.where(lane_ids((64, 128)) == spot, line, 0.0)
        return dot(spread.astype(BF16), jnp.ones((128, 128), BF16))

    row_mask[...] = (
        jnp.broadcast_to(mask_rows(band)[:, None, :] * (2.0 * scale), (64, 8, 128)).reshape(512, 128)
    )
    col_all = jnp.concatenate([mask_rows(first), mask_rows(first + 1)], axis=0).reshape(8, 2, 8, 128)
    col_mask[...] = jnp.where(half_lane, col_all[:, 0].reshape(64, 128), col_all[:, 1].reshape(64, 128))

    line = jnp.concatenate([target[:, 0, :], target[:, 1, :]], axis=1)
    lines = jnp.broadcast_to(line[:, None, :], (64, 8, 128)).reshape(512, 128)
    lines = jnp.where(lane_ids((512, 128)) % 8 == row_ids((512, 128)) % 8, lines, 0.0)
    lines_hi = lines.astype(BF16)
    lines_lo = (lines - lines_hi.astype(F32)).astype(BF16)
    spread = (
        (row_ids((128, 1024)) // 8 == lane_ids((128, 1024)) // 64).astype(F32).astype(BF16)
    )
    goal[...] = dot(
        jnp.concatenate([lines_hi, lines_lo], axis=1), jnp.concatenate([spread, spread], axis=0)
    )


def prep_call(*operands):
    shapes = [
        ((768, 128), BF16), ((768, 128), BF16), ((512, 1024), F32), ((512, 128), F32), ((64, 128), F32),
    ]
    return pl.pallas_call(
        prep_kernel,
        out_shape=tuple(jax.ShapeDtypeStruct(shape, kind) for shape, kind in shapes),
        in_specs=[pl.BlockSpec(memory_space=pltpu.VMEM)] * len(operands),
        out_specs=(pl.BlockSpec(memory_space=pltpu.VMEM),) * len(shapes),
        compiler_params=pltpu.CompilerParams(vmem_limit_bytes=16 * 2**20),
        cost_estimate=pl.CostEstimate(flops=3 * 10**8, bytes_accessed=4 * 10**6, transcendentals=0),
        name="prepare",
    )(*operands)


def tile_kernel(
    same, other, conv_b, w_out, fwd_w, bwd_w, goal, row_mask, col_mask,
    keep, send,
    rows_u, cols_v, pair, slope, grads, pre, hid16, hid32, weighted, guess, grad_rows, grad_cols, grad_w,
    place_u, place_v, fwd_2, bwd_2,
):
    band = lax.axis_index("band")
    core = band % 2
    first = band + 2 * lax.axis_index("off")
    half_lane = lane_ids((1, 128)) < 64

    none = jnp.zeros((256, 128), BF16)
    for t in range(4):
        for parity in range(2):
            ty = t - parity
            fwd_2[t * 256 : t * 256 + 256, parity * 128 : parity * 128 + 128] = (
                fwd_w[ty * 256 : ty * 256 + 256, :] if 0 <= ty < 3 else none
            )
    for t, taps in enumerate(((2, None, 0, 1), (1, 2, None, 0))):
        for k, ty in enumerate(taps):
            bwd_2[t * 256 : t * 256 + 256, k * 128 : k * 128 + 128] = (
                none if ty is None else bwd_w[ty * 256 : ty * 256 + 256, :]
            )

    def channels(which, rows):
        inside = jnp.clip(which, 0, BANDS - 1)
        at = inside // 2
        return jnp.where(
            inside % 2 == core, same[at, rows, :].astype(F32), other[at, rows, :].astype(F32)
        )

    def ending(which):
        return channels(which, slice(48, 64))[8:16]

    def whole(which):
        return channels(which, slice(0, 64))

    def opening(which):
        return channels(which, slice(0, 16))[0:8]

    u = jnp.concatenate([ending(band - 1), whole(band), opening(band + 1)], axis=0)
    rows_u[...] = jnp.where(half_lane, u, pltpu.roll(u, 64, 1))
    v = jnp.concatenate(
        [ending(first - 1), whole(first), whole(first + 1), opening(first + 2)], axis=0
    ).reshape(9, 2, 8, 128)
    v_low = v[:, 0].reshape(72, 128)
    v_high = v[:, 1].reshape(72, 128)
    cols_v[...] = jnp.where(half_lane, pltpu.roll(v_low, 64, 1), v_high)

    bias2 = jnp.concatenate([conv_b[...], conv_b[...]], axis=1)
    out_w2 = jnp.concatenate([w_out[...], w_out[...]], axis=1)
    halves = ((row_ids((128, 128)) < 64) == (lane_ids((128, 128)) < 64)).astype(F32).astype(BF16)

    def pair_stage(bp):
        block = first * 8 - 1 + 2 * bp
        spot = jnp.where(half_lane, block, block + 1)
        col_in = jnp.where((spot >= 0) & (spot < 128), 0.5, 0.0)
        v_here = cols_v[bp * 8 : bp * 8 + 8, :][None]
        for aq in range(10):
            half = col_in
            if aq == 0:
                half = jnp.where(band == 0, 0.0, col_in)
            if aq == 9:
                half = jnp.where(band == BANDS - 1, 0.0, col_in)
            x = (rows_u[aq * 8 : aq * 8 + 8, :][:, None, :] + v_here).reshape(64, 128)
            value, grade = gelu_parts(x, half)
            pair[bp][aq * 64 : aq * 64 + 64, :] = value.astype(BF16)
            slope[bp][aq * 64 : aq * 64 + 64, :] = grade

    def conv_stage(bp):
        part = dot(
            jnp.concatenate(
                [
                    jnp.concatenate(
                        [held[(2 * a + t) * 64 : (2 * a + t) * 64 + 64, :] for a in range(4)], axis=0
                    )
                    for t in range(4)
                    for held in (pair[bp], pair[bp + 1])
                ],
                axis=1,
            ),
            fwd_2[...],
        )
        for a in range(4):
            for parity in range(2):
                row = (2 * a + parity) * 64
                pre[bp][row : row + 64, :] = part[a * 64 : a * 64 + 64, parity * 128 : parity * 128 + 128]

    def act_stage(bp):
        for aq in range(8):
            row = slice(aq * 64, aq * 64 + 64)
            value, grade = gelu_parts(pre[bp][row, :] + bias2, 0.5)
            hid32[bp][row, :] = value
            hid16[bp][row, :] = (value * out_w2).astype(BF16)
            weighted[bp][row, :] = grade * out_w2

    def pred_stage(bp):
        guess[bp][...] = dot(hid16[bp][...], halves)

    def loss_stage(bp, sums):
        loss_sum, bias_sum, out_sum = sums
        lane = slice(bp * 128, bp * 128 + 128)
        col_weight = col_mask[bp * 8 : bp * 8 + 8, :][None]
        for aq in range(8):
            row = slice(aq * 64, aq * 64 + 64)
            weight = (row_mask[row, :].reshape(8, 8, 128) * col_weight).reshape(64, 128)
            residue = guess[bp][row, :] - goal[row, lane]
            grad_pred = weight * residue
            grad_pre = grad_pred * weighted[bp][row, :]
            grads[bp][row, :] = grad_pre.astype(BF16)
            loss_sum = loss_sum + jnp.sum((grad_pred * residue).reshape(8, 8, 128), axis=0)
            bias_sum = bias_sum + jnp.sum(grad_pre.reshape(8, 8, 128), axis=0)
            out_sum = out_sum + jnp.sum((grad_pred * hid32[bp][row, :]).reshape(8, 8, 128), axis=0)
        return loss_sum, bias_sum, out_sum

    def weights_stage(bp):
        turned = grads[bp][...].T
        for ty in range(3):
            rows = slice(ty * 64, ty * 64 + 512)
            part = dot(turned, jnp.concatenate([pair[bp][rows, :], pair[bp + 1][rows, :]], axis=1))
            if bp == 0:
                grad_w[:, ty * 256 : ty * 256 + 256] = part
            else:
                grad_w[:, ty * 256 : ty * 256 + 256] += part

    def back_stage(bp):
        reach = [grads[k] for k in (bp - 1, bp) if 0 <= k < 8]
        rows = jnp.concatenate(
            [
                jnp.concatenate(
                    [held[(2 * a + t) * 64 : (2 * a + t) * 64 + 64, :] for a in range(4)], axis=0
                )
                for t in range(2)
                for held in reach
            ],
            axis=1,
        )
        if bp == 0:
            both = dot(rows, jnp.concatenate([bwd_2[128:256, :], bwd_2[384:512, :]], axis=0))
        elif bp == 8:
            both = dot(rows, jnp.concatenate([bwd_2[0:128, :], bwd_2[256:384, :]], axis=0))
        else:
            both = dot(rows, bwd_2[...])
        col_sum = jnp.zeros((8, 128), F32)
        for a in range(5):
            for parity in range(2):
                row = (2 * a + parity) * 64
                block = 0.0
                if a < 4:
                    block = both[a * 64 : a * 64 + 64, 256 + parity * 128 : 384 + parity * 128]
                if a > 0:
                    block = block + both[a * 64 - 64 : a * 64, parity * 128 : parity * 128 + 128]
                block = block * slope[bp][row : row + 64, :]
                if bp == 0:
                    grad_rows[row : row + 64, :] = block
                else:
                    grad_rows[row : row + 64, :] += block
                col_sum = col_sum + jnp.sum(block.reshape(8, 8, 128), axis=0)
        grad_cols[bp * 8 : bp * 8 + 8, :] = col_sum

    zero8 = jnp.zeros((8, 128), F32)
    totals = (zero8, zero8, zero8)
    for step in range(15):
        if 6 <= step:
            back_stage(step - 6)
        if step < 9:
            pair_stage(step)
        if 6 <= step < 14:
            weights_stage(step - 6)
        if 3 <= step < 11:
            act_stage(step - 3)
        if 2 <= step < 10:
            conv_stage(step - 2)
        if 5 <= step < 13:
            totals = loss_stage(step - 5, totals)
        if 4 <= step < 12:
            pred_stage(step - 4)

    row_part = jnp.sum(grad_rows[...].reshape(80, 8, 128), axis=1)
    place_u[...] = jnp.zeros(place_u.shape, F32)
    place_v[...] = jnp.zeros(place_v.shape, F32)
    place_u[pl.ds(pl.multiple_of(core * 64, 64), 80), :] = row_part + pltpu.roll(row_part, 64, 1)
    col_part = grad_cols[...]
    col_high = pltpu.roll(col_part, 64, 1).reshape(9, 1, 8, 128)
    place_v[pl.ds(pl.multiple_of(core * 64, 64), 144), :] = jnp.concatenate(
        [col_part.reshape(9, 1, 8, 128), col_high], axis=1
    ).reshape(144, 128)
    packed_u = jnp.where(half_lane, place_u[0:72, :], pltpu.roll(place_u[72:144, :], 64, 1))
    packed_v = jnp.where(half_lane, place_v[0:104, :], pltpu.roll(place_v[104:208, :], 64, 1))

    taps = []
    for ty in range(3):
        taps.append(
            grad_w[0:64, ty * 256 : ty * 256 + 192] + grad_w[64:128, ty * 256 + 64 : ty * 256 + 256]
        )
    conv_grad = jnp.concatenate(taps, axis=1)
    blocks = [conv_grad[:, k * 128 : k * 128 + 128] for k in range(4)]
    last = jnp.concatenate([conv_grad[0:32, 512:576], conv_grad[32:64, 512:576]], axis=1)

    loss_sum, bias_sum, out_sum = totals
    bias_row = jnp.sum(bias_sum, axis=0, keepdims=True)
    bias_row = bias_row + pltpu.roll(bias_row, 64, 1)
    out_row = jnp.sum(out_sum, axis=0, keepdims=True)
    out_row = out_row + pltpu.roll(out_row, 64, 1)
    small_row = jnp.where(half_lane, bias_row, out_row)
    loss_row = jnp.broadcast_to(jnp.sum(loss_sum, keepdims=True) * (0.5 / 64.0), (1, 128))
    small_hi = small_row.astype(BF16).astype(F32)
    loss_hi = loss_row.astype(BF16).astype(F32)
    tail = jnp.concatenate(
        [small_hi, small_row - small_hi, loss_hi, loss_row - loss_hi, jnp.zeros((4, 128), F32)], axis=0
    )
    first_core = jnp.concatenate([packed_u, last, blocks[2], blocks[3], tail], axis=0)
    second_core = jnp.concatenate([packed_v, blocks[0], blocks[1], tail], axis=0)
    keep[...] = jnp.where(core == 0, first_core, second_core)
    send[...] = jnp.where(core == 0, second_core, first_core).astype(BF16)


def tile_call(*operands):
    shapes = [
        ((80, 128), F32), ((72, 128), F32), [((640, 128), BF16)] * 9, [((640, 128), F32)] * 9,
        [((512, 128), BF16)] * 8, [((512, 128), F32)] * 8, [((512, 128), BF16)] * 8, [((512, 128), F32)] * 8,
        [((512, 128), F32)] * 8, [((512, 128), F32)] * 8,
        ((640, 128), F32), ((72, 128), F32), ((128, 768), F32), ((208, 128), F32), ((208, 128), F32),
        ((1024, 256), BF16), ((512, 512), BF16),
    ]
    return pl.pallas_call(
        tile_kernel,
        out_shape=(jax.ShapeDtypeStruct((240, 128), F32), jax.ShapeDtypeStruct((240, 128), BF16)),
        in_specs=[pl.BlockSpec(memory_space=pltpu.VMEM)] * len(operands),
        out_specs=(pl.BlockSpec(memory_space=pltpu.VMEM),) * 2,
        scratch_shapes=[
            [pltpu.VMEM(*one) for one in entry] if isinstance(entry, list) else pltpu.VMEM(*entry)
            for entry in shapes
        ],
        compiler_params=pltpu.CompilerParams(vmem_limit_bytes=40 * 2**20),
        cost_estimate=pl.CostEstimate(flops=2 * 10**9, bytes_accessed=10**6, transcendentals=10**6),
        name="tiles",
    )(*operands)


def join_kernel(kept, received, out):
    first_core = lax.axis_index("band") % 2 == 0
    total = kept[...] + received[...].astype(F32)
    small = total[232:233] + total[233:234]
    loss = total[234:235] + total[235:236]
    small_hi = small.astype(BF16).astype(F32)
    loss_hi = loss.astype(BF16).astype(F32)
    tail = jnp.concatenate(
        [small_hi, small - small_hi, loss_hi, loss - loss_hi, jnp.zeros((2, 128), F32)], axis=0
    )

    def to_all(rows):
        return jnp.broadcast_to(rows[None], (CHIPS, rows.shape[0], 128))

    extra = jnp.concatenate(
        [total[72:88].reshape(CHIPS, 1, 128), total[88:104].reshape(CHIPS, 1, 128), to_all(tail)], axis=1
    )
    out[...] = jnp.concatenate(
        [
            to_all(total[0:72]),
            jnp.where(first_core, extra, to_all(total[72:80])),
            to_all(total[80:104]),
            total[104:232].reshape(CHIPS, 8, 128),
        ],
        axis=1,
    ).astype(BF16)


def join_call(kept, received):
    return pl.pallas_call(
        join_kernel,
        out_shape=jax.ShapeDtypeStruct((CHIPS, 112, 128), BF16),
        in_specs=[pl.BlockSpec(memory_space=pltpu.VMEM)] * 2,
        out_specs=pl.BlockSpec(memory_space=pltpu.VMEM),
        compiler_params=pltpu.CompilerParams(vmem_limit_bytes=16 * 2**20),
        name="join",
    )(kept, received)


def sum_kernel(parts, same, other, out, mine, theirs, bins):
    band = lax.axis_index("band")
    off = lax.axis_index("off")
    core = band % 2
    half_lane = lane_ids((1, 128)) < 64
    bins[...] = jnp.zeros(bins.shape, F32)
    split = jnp.where(core == 0, 72, 104)
    used = row_ids((104, 128)) < split
    def piece(chip):
        return parts[chip].astype(F32)[0:104] if 0 <= chip < CHIPS else 0.0

    for step in range(9):
        both = piece(2 * step) + jnp.where(core == 0, piece(2 * step + 1), piece(2 * step - 1))
        both = jnp.where(used, both, 0.0)
        start = step * 128 + 56
        bins[start : start + 104, :] += both
        bins[pl.ds(pl.multiple_of(start + split, 8), 104), :] += pltpu.roll(both, 64, 1)

    def own_half(x):
        return jnp.where(
            core == 0, jnp.where(half_lane, x, 0.0), jnp.where(half_lane, 0.0, pltpu.roll(x, 64, 1))
        ).astype(BF16)

    sibling = band + 1 - 2 * core
    mine[...] = own_half(bins[pl.ds(pl.multiple_of(64 + 64 * band + 32 * off, 32), 32), :])
    theirs[...] = own_half(bins[pl.ds(pl.multiple_of(64 + 64 * sibling + 32 * off, 32), 32), :])
    halves = bins[64:1088, :].reshape(8, 2, 2, 32, 128)

    def dense(bands):
        return jnp.where(
            half_lane, bands[:, 0].reshape(256, 128), pltpu.roll(bands[:, 1].reshape(256, 128), 64, 1)
        )

    even, odd = dense(halves[:, 0]), dense(halves[:, 1])
    product = 0.0
    for cols, bands in (
        (same, jnp.where(core == 0, even, odd)), (other, jnp.where(core == 0, odd, even))
    ):
        product = product + lax.dot_general(
            cols[:, 64:96, :].reshape(256, 128), bands.astype(BF16), (((0,), (0,)), ((), ())),
            preferred_element_type=F32,
        )
    rows = product[0:64] + pltpu.roll(product[64:128], 64, 1)
    rows = jnp.where(half_lane, rows[0:32], pltpu.roll(rows[32:64], 64, 1))
    weights = jnp.sum(parts[:, 96:112, :].astype(F32), axis=0)[8:16]
    extra = jnp.sum(parts[:, 64:80, :].astype(F32), axis=0)[8:16]
    small = extra[2:3] + extra[3:4]
    loss = extra[4:5] + extra[5:6]
    small_hi = small.astype(BF16).astype(F32)
    loss_hi = loss.astype(BF16).astype(F32)
    whole = jnp.concatenate(
        [
            rows, weights, extra[0:2], small_hi, small - small_hi, loss_hi, loss - loss_hi,
            jnp.zeros((2, 128), F32),
        ],
        axis=0,
    )
    out[...] = jnp.broadcast_to(whole.astype(BF16)[None], (CHIPS, 48, 128))


def sum_call(parts, same, other):
    return pl.pallas_call(
        sum_kernel,
        out_shape=(
            jax.ShapeDtypeStruct((CHIPS, 48, 128), BF16),
            jax.ShapeDtypeStruct((32, 128), BF16),
            jax.ShapeDtypeStruct((32, 128), BF16),
        ),
        in_specs=[pl.BlockSpec(memory_space=pltpu.VMEM)] * 3,
        out_specs=(pl.BlockSpec(memory_space=pltpu.VMEM),) * 3,
        scratch_shapes=[pltpu.VMEM((1408, 128), F32)],
        compiler_params=pltpu.CompilerParams(vmem_limit_bytes=16 * 2**20),
        name="sums",
    )(parts, same, other)


def final_kernel(
    same, other, mine, received, w_proj,
    grad_proj_hbm, grad_conv_hbm, grad_feats_hbm, bias_hbm, w_out_hbm, loss_hbm,
    grad_proj, grad_conv_t, grad_feats, bias, w_out, loss, sems,
):
    is_first = lax.axis_index("band") % 2 == 0
    half_lane = lane_ids((1, 128)) < 64
    firsts, seconds = [], []
    puts = []
    for k in range(4):
        for chip in range(4 * k, 4 * k + 4):
            here = same[chip].astype(F32)
            there = other[chip].astype(F32)
            left = jnp.where(is_first, here, there)
            right = jnp.where(is_first, there, here)
            firsts.append(left[32:48])
            seconds.append(right[32:40])
            left, right = left[0:32], right[0:32]
            row = chip * 64
            grad_proj[row : row + 32, :] = jnp.where(half_lane, left, pltpu.roll(right, 64, 1))
            grad_proj[row + 32 : row + 64, :] = jnp.where(half_lane, pltpu.roll(left, 64, 1), right)
        rows = pl.ds(k * 256, 256)
        puts.append(pltpu.make_async_copy(grad_proj.at[rows], grad_proj_hbm.at[rows], sems.at[k]))
        puts[k].start()
    wide = jnp.concatenate(seconds + [first[0:8] for first in firsts], axis=0)
    for k in range(4):
        grad_conv_t[:, k * 128 : k * 128 + 128] = wide[k * 64 : k * 64 + 64]
    last = jnp.concatenate([first[8:9] for first in firsts] + [first[9:10] for first in firsts], axis=0)
    grad_conv_t[0:32, 512:576] = last[:, 0:64]
    grad_conv_t[32:64, 512:576] = last[:, 64:128]
    puts.append(pltpu.make_async_copy(grad_conv_t, grad_conv_hbm, sems.at[4]))
    puts[4].start()
    small = firsts[0][10:11] + firsts[0][11:12]
    bias[...] = small[:, 0:64]
    w_out[...] = small[:, 64:128]
    loss[...] = (firsts[0][12:13] + firsts[0][13:14])[:, 0:1]
    for k, (held, result) in enumerate(((bias, bias_hbm), (w_out, w_out_hbm), (loss, loss_hbm))):
        puts.append(pltpu.make_async_copy(held, result, sems.at[6 + k]))
        puts[5 + k].start()
    gproj = mine[...] + received[...]
    grad_feats[...] = lax.dot_general(
        gproj, w_proj[...], (((1,), (1,)), ((), ())), preferred_element_type=F32
    ).astype(BF16)
    put_feats = pltpu.make_async_copy(grad_feats, grad_feats_hbm, sems.at[5])
    put_feats.start()
    for put in puts + [put_feats]:
        put.wait()


def final_call(*operands):
    return pl.pallas_call(
        final_kernel,
        out_shape=(
            jax.ShapeDtypeStruct((1024, 128), F32),
            jax.ShapeDtypeStruct((64, 576), F32),
            jax.ShapeDtypeStruct((32, 1024), BF16),
            jax.ShapeDtypeStruct((1, 64), F32),
            jax.ShapeDtypeStruct((1, 64), F32),
            jax.ShapeDtypeStruct((1, 1), F32),
        ),
        in_specs=[pl.BlockSpec(memory_space=pltpu.VMEM)] * len(operands),
        out_specs=(pl.BlockSpec(memory_space=pltpu.HBM),) * 6,
        scratch_shapes=[
            pltpu.VMEM((1024, 128), F32),
            pltpu.VMEM((64, 576), F32),
            pltpu.VMEM((32, 1024), BF16),
            pltpu.VMEM((1, 64), F32),
            pltpu.VMEM((1, 64), F32),
            pltpu.VMEM((1, 1), F32),
            pltpu.SemaphoreType.DMA((9,)),
        ],
        compiler_params=pltpu.CompilerParams(vmem_limit_bytes=8 * 2**20),
        name="outputs",
    )(*operands)


def body(feats, w_proj, conv_w, conv_b, w_out, target, mask):
    swap = [(2 * i + o, 2 * (i + 1 - 2 * (i % 2)) + o) for i in range(BANDS) for o in range(2)]
    same_core = [[2 * i + o for i in range(core, BANDS, 2) for o in range(2)] for core in range(2)]
    same_row = [[2 * i + o for i in range(core, BANDS, 2)] for core in range(2) for o in range(2)]
    same = lax.all_to_all(front_call(feats, w_proj), GROUP, 0, 0, tiled=True, axis_index_groups=same_row)
    ready = prep_call(mask.reshape(8, 128), target, conv_w.T)
    same, ready = lax.optimization_barrier((same, ready))
    other = lax.ppermute(same, GROUP, swap)
    kept, given = tile_call(same, other, conv_b.reshape(1, 64), w_out.reshape(1, 64), *ready)
    joined = join_call(kept, lax.ppermute(given, GROUP, swap))
    parts = lax.all_to_all(joined, GROUP, 0, 0, tiled=True, axis_index_groups=same_core)
    sums, mine, theirs = sum_call(parts, same, other)
    every = lax.all_to_all(sums, GROUP, 0, 0, tiled=True, axis_index_groups=same_core)
    every, theirs = lax.optimization_barrier((every, theirs))
    grad_proj, grad_conv_t, grad_feats, bias, w_out, loss = final_call(
        every, lax.ppermute(every, GROUP, swap), mine, lax.ppermute(theirs, GROUP, swap), w_proj
    )
    return (loss.reshape(1), grad_proj, grad_conv_t.T, bias.reshape(64), w_out.reshape(64), grad_feats)


def solution(mesh):
    placed = (
        P(("rep", "band"), None),
        P(),
        P(),
        P(),
        P(),
        P(("rep", "band"), "off", None),
        P("rep"),
    )
    return jax.shard_map(
        body,
        mesh=mesh,
        in_specs=placed,
        out_specs=(
            P("rep"),
            P("rep", None),
            P("rep", None),
            P("rep"),
            P("rep"),
            P(("rep", "band", "off"), None),
        ),
        check_vma=False,
    )
```

```python
import jax
import jax.numpy as jnp
from jax import lax
from jax.experimental import pallas as pl
from jax.experimental.pallas import tpu as pltpu
from jax.sharding import PartitionSpec as P

GELU_K = 0.7978845608028654
GELU_C = 0.044715
GROUP = ("band", "off")
CHIPS = 16
BANDS = 16
F32 = jnp.float32
BF16 = jnp.bfloat16


def gelu_parts(x, half):
    inner = GELU_K + (GELU_K * GELU_C) * (x * x)
    gate = half + half * jnp.tanh(x * inner)
    value = x * gate
    slope = gate + (value * (1.0 - gate)) * (6.0 * inner - 4.0 * GELU_K)
    return value, slope


def lane_ids(shape):
    return lax.broadcasted_iota(jnp.int32, shape, len(shape) - 1)


def row_ids(shape):
    return lax.broadcasted_iota(jnp.int32, shape, len(shape) - 2)


def dot(a, b):
    return jnp.dot(a, b, preferred_element_type=F32)


def front_kernel(feats_hbm, w_proj_hbm, out, feats, w_proj, sems):
    off = lax.axis_index("off")
    get_feats = pltpu.make_async_copy(feats_hbm, feats, sems.at[0])
    get_w = pltpu.make_async_copy(w_proj_hbm, w_proj, sems.at[1])
    get_feats.start()
    get_w.start()
    get_feats.wait()
    get_w.wait()
    proj = dot(feats[...], w_proj[...]).astype(BF16)
    half_lane = lane_ids((1, 128)) < 64
    for q in range(8):
        block = feats[:, q * 128 : q * 128 + 128].astype(F32)
        top, bottom = block[0:32], block[32:64]
        low = jnp.where(half_lane, top, pltpu.roll(bottom, 64, 1))
        high = jnp.where(half_lane, pltpu.roll(top, 64, 1), bottom)
        out[q, 64:96, :] = jnp.where(off == 0, low, high).astype(BF16)
    out[:, 0:64, :] = jnp.broadcast_to(proj[None], (8, 64, 128))


def front_call(feats, w_proj):
    return pl.pallas_call(
        front_kernel,
        out_shape=jax.ShapeDtypeStruct((8, 96, 128), BF16),
        in_specs=[pl.BlockSpec(memory_space=pltpu.HBM)] * 2,
        out_specs=pl.BlockSpec(memory_space=pltpu.VMEM),
        scratch_shapes=[
            pltpu.VMEM((64, 1024), BF16),
            pltpu.VMEM((1024, 128), BF16),
            pltpu.SemaphoreType.DMA((2,)),
        ],
        compiler_params=pltpu.CompilerParams(vmem_limit_bytes=60 * 2**20),
        name="front",
    )(feats, w_proj)


def prep_kernel(
    mask, target, conv_t, fwd_w, bwd_w, goal, row_mask, col_mask
):
    band = lax.axis_index("band")
    first = band + 2 * lax.axis_index("off")
    half_lane = lane_ids((1, 128)) < 64

    blank = jnp.zeros((64, 64), F32)
    for ty in range(3):
        taps = [conv_t[:, (3 * ty + tx) * 64 : (3 * ty + tx + 1) * 64].astype(F32) for tx in range(3)]
        low = jnp.concatenate(taps + [blank], axis=1)
        high = jnp.concatenate([blank] + taps, axis=1)
        fwd_w[ty * 256 : ty * 256 + 256, :] = jnp.concatenate([low, high], axis=0).T.astype(BF16)
        left = taps[::-1] + [blank]
        right = [blank] + taps[::-1]
        for k in range(4):
            row = ty * 256 + k * 64
            bwd_w[row : row + 64, :] = jnp.concatenate([left[k], right[k]], axis=1).astype(BF16)
    mask_all = mask[...].astype(F32)
    mask_lane = lane_ids((8, 128))
    by_band = jnp.concatenate(
        [jnp.where(mask_lane < 64, mask_all, 0.0), jnp.where(mask_lane < 64, 0.0, mask_all)], axis=0
    ).astype(BF16)
    sums_row = dot(by_band, jnp.ones((128, 128), BF16))
    sums_col = lax.dot_general(
        jnp.ones((16, 128), BF16), by_band, (((1,), (1,)), ((), ())), preferred_element_type=F32
    )
    at = lax.broadcasted_iota(jnp.int32, (16, 16), 0)
    to = lax.broadcasted_iota(jnp.int32, (16, 16), 1)
    apart = (2 * (to % 8) + to // 8) - (2 * (at % 8) + at // 8)
    near_diagonal = (apart >= 0) & (apart < 4)
    count = jnp.sum(jnp.where(near_diagonal, sums_row[:, 0:16] * sums_col, 0.0))
    scale = 1.0 / count

    def mask_rows(which):
        inside = jnp.minimum(which, 15)
        line = mask[pl.ds(inside // 2, 1), :].astype(F32)
        line = jnp.where(which < 16, line, 0.0)
        spot = row_ids((64, 128)) + 64 * (inside % 2)
        spread = jnp.where(lane_ids((64, 128)) == spot, line, 0.0)
        return dot(spread.astype(BF16), jnp.ones((128, 128), BF16))

    row_mask[...] = (
        jnp.broadcast_to(mask_rows(band)[:, None, :] * (2.0 * scale), (64, 8, 128)).reshape(512, 128)
    )
    col_all = jnp.concatenate([mask_rows(first), mask_rows(first + 1)], axis=0).reshape(8, 2, 8, 128)
    col_mask[...] = jnp.where(half_lane, col_all[:, 0].reshape(64, 128), col_all[:, 1].reshape(64, 128))

    line = jnp.concatenate([target[:, 0, :], target[:, 1, :]], axis=1)
    lines = jnp.broadcast_to(line[:, None, :], (64, 8, 128)).reshape(512, 128)
    lines = jnp.where(lane_ids((512, 128)) % 8 == row_ids((512, 128)) % 8, lines, 0.0)
    lines_hi = lines.astype(BF16)
    lines_lo = (lines - lines_hi.astype(F32)).astype(BF16)
    spread = (
        (row_ids((128, 1024)) // 8 == lane_ids((128, 1024)) // 64).astype(F32).astype(BF16)
    )
    goal[...] = dot(
        jnp.concatenate([lines_hi, lines_lo], axis=1), jnp.concatenate([spread, spread], axis=0)
    )


def prep_call(*operands):
    shapes = [
        ((768, 128), BF16), ((768, 128), BF16), ((512, 1024), F32), ((512, 128), F32), ((64, 128), F32),
    ]
    return pl.pallas_call(
        prep_kernel,
        out_shape=tuple(jax.ShapeDtypeStruct(shape, kind) for shape, kind in shapes),
        in_specs=[pl.BlockSpec(memory_space=pltpu.VMEM)] * len(operands),
        out_specs=(pl.BlockSpec(memory_space=pltpu.VMEM),) * len(shapes),
        compiler_params=pltpu.CompilerParams(vmem_limit_bytes=16 * 2**20),
        cost_estimate=pl.CostEstimate(flops=3 * 10**8, bytes_accessed=4 * 10**6, transcendentals=0),
        name="prepare",
    )(*operands)


def tile_kernel(
    same, other, conv_b, w_out, fwd_w, bwd_w, goal, row_mask, col_mask,
    keep, send,
    rows_u, cols_v, pair, slope, grads, pre, hid16, hid32, weighted, guess, grad_rows, grad_cols, grad_w,
    place_u, place_v, fwd_2, bwd_2,
):
    band = lax.axis_index("band")
    core = band % 2
    first = band + 2 * lax.axis_index("off")
    half_lane = lane_ids((1, 128)) < 64

    none = jnp.zeros((256, 128), BF16)
    for t in range(4):
        for parity in range(2):
            ty = t - parity
            fwd_2[t * 256 : t * 256 + 256, parity * 128 : parity * 128 + 128] = (
                fwd_w[ty * 256 : ty * 256 + 256, :] if 0 <= ty < 3 else none
            )
    for t, taps in enumerate(((2, None, 0, 1), (1, 2, None, 0))):
        for k, ty in enumerate(taps):
            bwd_2[t * 256 : t * 256 + 256, k * 128 : k * 128 + 128] = (
                none if ty is None else bwd_w[ty * 256 : ty * 256 + 256, :]
            )

    def channels(which, rows):
        inside = jnp.clip(which, 0, BANDS - 1)
        at = inside // 2
        return jnp.where(
            inside % 2 == core, same[at, rows, :].astype(F32), other[at, rows, :].astype(F32)
        )

    def ending(which):
        return channels(which, slice(48, 64))[8:16]

    def whole(which):
        return channels(which, slice(0, 64))

    def opening(which):
        return channels(which, slice(0, 16))[0:8]

    u = jnp.concatenate([ending(band - 1), whole(band), opening(band + 1)], axis=0)
    rows_u[...] = jnp.where(half_lane, u, pltpu.roll(u, 64, 1))
    v = jnp.concatenate(
        [ending(first - 1), whole(first), whole(first + 1), opening(first + 2)], axis=0
    ).reshape(9, 2, 8, 128)
    v_low = v[:, 0].reshape(72, 128)
    v_high = v[:, 1].reshape(72, 128)
    cols_v[...] = jnp.where(half_lane, pltpu.roll(v_low, 64, 1), v_high)

    bias2 = jnp.concatenate([conv_b[...], conv_b[...]], axis=1)
    out_w2 = jnp.concatenate([w_out[...], w_out[...]], axis=1)
    halves = ((row_ids((128, 128)) < 64) == (lane_ids((128, 128)) < 64)).astype(F32).astype(BF16)

    def pair_stage(bp):
        block = first * 8 - 1 + 2 * bp
        spot = jnp.where(half_lane, block, block + 1)
        col_in = jnp.where((spot >= 0) & (spot < 128), 0.5, 0.0)
        v_here = cols_v[bp * 8 : bp * 8 + 8, :][None]
        for aq in range(10):
            half = col_in
            if aq == 0:
                half = jnp.where(band == 0, 0.0, col_in)
            if aq == 9:
                half = jnp.where(band == BANDS - 1, 0.0, col_in)
            x = (rows_u[aq * 8 : aq * 8 + 8, :][:, None, :] + v_here).reshape(64, 128)
            value, grade = gelu_parts(x, half)
            pair[bp][aq * 64 : aq * 64 + 64, :] = value.astype(BF16)
            slope[bp][aq * 64 : aq * 64 + 64, :] = grade

    def conv_stage(bp):
        part = dot(
            jnp.concatenate(
                [
                    jnp.concatenate(
                        [held[(2 * a + t) * 64 : (2 * a + t) * 64 + 64, :] for a in range(4)], axis=0
                    )
                    for t in range(4)
                    for held in (pair[bp], pair[bp + 1])
                ],
                axis=1,
            ),
            fwd_2[...],
        )
        for a in range(4):
            for parity in range(2):
                row = (2 * a + parity) * 64
                pre[bp][row : row + 64, :] = part[a * 64 : a * 64 + 64, parity * 128 : parity * 128 + 128]

    def act_stage(bp):
        for aq in range(8):
            row = slice(aq * 64, aq * 64 + 64)
            value, grade = gelu_parts(pre[bp][row, :] + bias2, 0.5)
            hid32[bp][row, :] = value
            hid16[bp][row, :] = (value * out_w2).astype(BF16)
            weighted[bp][row, :] = grade * out_w2

    def pred_stage(bp):
        guess[bp][...] = dot(hid16[bp][...], halves)

    def loss_stage(bp, sums):
        loss_sum, bias_sum, out_sum = sums
        lane = slice(bp * 128, bp * 128 + 128)
        col_weight = col_mask[bp * 8 : bp * 8 + 8, :][None]
        for aq in range(8):
            row = slice(aq * 64, aq * 64 + 64)
            weight = (row_mask[row, :].reshape(8, 8, 128) * col_weight).reshape(64, 128)
            residue = guess[bp][row, :] - goal[row, lane]
            grad_pred = weight * residue
            grad_pre = grad_pred * weighted[bp][row, :]
            grads[bp][row, :] = grad_pre.astype(BF16)
            loss_sum = loss_sum + jnp.sum((grad_pred * residue).reshape(8, 8, 128), axis=0)
            bias_sum = bias_sum + jnp.sum(grad_pre.reshape(8, 8, 128), axis=0)
            out_sum = out_sum + jnp.sum((grad_pred * hid32[bp][row, :]).reshape(8, 8, 128), axis=0)
        return loss_sum, bias_sum, out_sum

    def weights_stage(bp):
        turned = grads[bp][...].T
        for ty in range(3):
            rows = slice(ty * 64, ty * 64 + 512)
            part = dot(turned, jnp.concatenate([pair[bp][rows, :], pair[bp + 1][rows, :]], axis=1))
            if bp == 0:
                grad_w[:, ty * 256 : ty * 256 + 256] = part
            else:
                grad_w[:, ty * 256 : ty * 256 + 256] += part

    def back_stage(bp):
        reach = [grads[k] for k in (bp - 1, bp) if 0 <= k < 8]
        rows = jnp.concatenate(
            [
                jnp.concatenate(
                    [held[(2 * a + t) * 64 : (2 * a + t) * 64 + 64, :] for a in range(4)], axis=0
                )
                for t in range(2)
                for held in reach
            ],
            axis=1,
        )
        if bp == 0:
            both = dot(rows, jnp.concatenate([bwd_2[128:256, :], bwd_2[384:512, :]], axis=0))
        elif bp == 8:
            both = dot(rows, jnp.concatenate([bwd_2[0:128, :], bwd_2[256:384, :]], axis=0))
        else:
            both = dot(rows, bwd_2[...])
        col_sum = jnp.zeros((8, 128), F32)
        for a in range(5):
            for parity in range(2):
                row = (2 * a + parity) * 64
                block = 0.0
                if a < 4:
                    block = both[a * 64 : a * 64 + 64, 256 + parity * 128 : 384 + parity * 128]
                if a > 0:
                    block = block + both[a * 64 - 64 : a * 64, parity * 128 : parity * 128 + 128]
                block = block * slope[bp][row : row + 64, :]
                if bp == 0:
                    grad_rows[row : row + 64, :] = block
                else:
                    grad_rows[row : row + 64, :] += block
                col_sum = col_sum + jnp.sum(block.reshape(8, 8, 128), axis=0)
        grad_cols[bp * 8 : bp * 8 + 8, :] = col_sum

    zero8 = jnp.zeros((8, 128), F32)
    totals = (zero8, zero8, zero8)
    for step in range(15):
        if 6 <= step:
            back_stage(step - 6)
        if step < 9:
            pair_stage(step)
        if 6 <= step < 14:
            weights_stage(step - 6)
        if 3 <= step < 11:
            act_stage(step - 3)
        if 2 <= step < 10:
            conv_stage(step - 2)
        if 5 <= step < 13:
            totals = loss_stage(step - 5, totals)
        if 4 <= step < 12:
            pred_stage(step - 4)

    row_part = jnp.sum(grad_rows[...].reshape(80, 8, 128), axis=1)
    place_u[...] = jnp.zeros(place_u.shape, F32)
    place_v[...] = jnp.zeros(place_v.shape, F32)
    place_u[pl.ds(pl.multiple_of(core * 64, 64), 80), :] = row_part + pltpu.roll(row_part, 64, 1)
    col_part = grad_cols[...]
    col_high = pltpu.roll(col_part, 64, 1).reshape(9, 1, 8, 128)
    place_v[pl.ds(pl.multiple_of(core * 64, 64), 144), :] = jnp.concatenate(
        [col_part.reshape(9, 1, 8, 128), col_high], axis=1
    ).reshape(144, 128)
    packed_u = jnp.where(half_lane, place_u[0:72, :], pltpu.roll(place_u[72:144, :], 64, 1))
    packed_v = jnp.where(half_lane, place_v[0:104, :], pltpu.roll(place_v[104:208, :], 64, 1))

    taps = []
    for ty in range(3):
        taps.append(
            grad_w[0:64, ty * 256 : ty * 256 + 192] + grad_w[64:128, ty * 256 + 64 : ty * 256 + 256]
        )
    conv_grad = jnp.concatenate(taps, axis=1)
    blocks = [conv_grad[:, k * 128 : k * 128 + 128] for k in range(4)]
    last = jnp.concatenate([conv_grad[0:32, 512:576], conv_grad[32:64, 512:576]], axis=1)

    loss_sum, bias_sum, out_sum = totals
    bias_row = jnp.sum(bias_sum, axis=0, keepdims=True)
    bias_row = bias_row + pltpu.roll(bias_row, 64, 1)
    out_row = jnp.sum(out_sum, axis=0, keepdims=True)
    out_row = out_row + pltpu.roll(out_row, 64, 1)
    small_row = jnp.where(half_lane, bias_row, out_row)
    loss_row = jnp.broadcast_to(jnp.sum(loss_sum, keepdims=True) * (0.5 / 64.0), (1, 128))
    small_hi = small_row.astype(BF16).astype(F32)
    loss_hi = loss_row.astype(BF16).astype(F32)
    tail = jnp.concatenate(
        [small_hi, small_row - small_hi, loss_hi, loss_row - loss_hi, jnp.zeros((4, 128), F32)], axis=0
    )
    first_core = jnp.concatenate([packed_u, last, blocks[2], blocks[3], tail], axis=0)
    second_core = jnp.concatenate([packed_v, blocks[0], blocks[1], tail], axis=0)
    keep[...] = jnp.where(core == 0, first_core, second_core)
    send[...] = jnp.where(core == 0, second_core, first_core).astype(BF16)


def tile_call(*operands):
    shapes = [
        ((80, 128), F32), ((72, 128), F32), [((640, 128), BF16)] * 9, [((640, 128), F32)] * 9,
        [((512, 128), BF16)] * 8, [((512, 128), F32)] * 8, [((512, 128), BF16)] * 8, [((512, 128), F32)] * 8,
        [((512, 128), F32)] * 8, [((512, 128), F32)] * 8,
        ((640, 128), F32), ((72, 128), F32), ((128, 768), F32), ((208, 128), F32), ((208, 128), F32),
        ((1024, 256), BF16), ((512, 512), BF16),
    ]
    return pl.pallas_call(
        tile_kernel,
        out_shape=(jax.ShapeDtypeStruct((240, 128), F32), jax.ShapeDtypeStruct((240, 128), BF16)),
        in_specs=[pl.BlockSpec(memory_space=pltpu.VMEM)] * len(operands),
        out_specs=(pl.BlockSpec(memory_space=pltpu.VMEM),) * 2,
        scratch_shapes=[
            [pltpu.VMEM(*one) for one in entry] if isinstance(entry, list) else pltpu.VMEM(*entry)
            for entry in shapes
        ],
        compiler_params=pltpu.CompilerParams(vmem_limit_bytes=40 * 2**20),
        cost_estimate=pl.CostEstimate(flops=2 * 10**9, bytes_accessed=10**6, transcendentals=10**6),
        name="tiles",
    )(*operands)


def join_kernel(kept, received, out):
    first_core = lax.axis_index("band") % 2 == 0
    total = kept[...] + received[...].astype(F32)
    small = total[232:233] + total[233:234]
    loss = total[234:235] + total[235:236]
    small_hi = small.astype(BF16).astype(F32)
    loss_hi = loss.astype(BF16).astype(F32)
    tail = jnp.concatenate(
        [small_hi, small - small_hi, loss_hi, loss - loss_hi, jnp.zeros((2, 128), F32)], axis=0
    )

    def to_all(rows):
        return jnp.broadcast_to(rows[None], (CHIPS, rows.shape[0], 128))

    extra = jnp.concatenate(
        [total[72:88].reshape(CHIPS, 1, 128), total[88:104].reshape(CHIPS, 1, 128), to_all(tail)], axis=1
    )
    out[...] = jnp.concatenate(
        [
            to_all(total[0:72]),
            jnp.where(first_core, extra, to_all(total[72:80])),
            to_all(total[80:104]),
            total[104:232].reshape(CHIPS, 8, 128),
        ],
        axis=1,
    ).astype(BF16)


def join_call(kept, received):
    return pl.pallas_call(
        join_kernel,
        out_shape=jax.ShapeDtypeStruct((CHIPS, 112, 128), BF16),
        in_specs=[pl.BlockSpec(memory_space=pltpu.VMEM)] * 2,
        out_specs=pl.BlockSpec(memory_space=pltpu.VMEM),
        compiler_params=pltpu.CompilerParams(vmem_limit_bytes=16 * 2**20),
        name="join",
    )(kept, received)


def sum_kernel(parts, same, other, out, mine, theirs, bins):
    band = lax.axis_index("band")
    off = lax.axis_index("off")
    core = band % 2
    half_lane = lane_ids((1, 128)) < 64
    bins[...] = jnp.zeros(bins.shape, F32)
    split = jnp.where(core == 0, 72, 104)
    used = row_ids((104, 128)) < split
    def piece(chip):
        return parts[chip].astype(F32)[0:104] if 0 <= chip < CHIPS else 0.0

    for step in range(9):
        both = piece(2 * step) + jnp.where(core == 0, piece(2 * step + 1), piece(2 * step - 1))
        both = jnp.where(used, both, 0.0)
        start = step * 128 + 56
        bins[start : start + 104, :] += both
        bins[pl.ds(pl.multiple_of(start + split, 8), 104), :] += pltpu.roll(both, 64, 1)

    def own_half(x):
        return jnp.where(
            core == 0, jnp.where(half_lane, x, 0.0), jnp.where(half_lane, 0.0, pltpu.roll(x, 64, 1))
        ).astype(BF16)

    sibling = band + 1 - 2 * core
    mine[...] = own_half(bins[pl.ds(pl.multiple_of(64 + 64 * band + 32 * off, 32), 32), :])
    theirs[...] = own_half(bins[pl.ds(pl.multiple_of(64 + 64 * sibling + 32 * off, 32), 32), :])
    halves = bins[64:1088, :].reshape(8, 2, 2, 32, 128)

    def dense(bands):
        return jnp.where(
            half_lane, bands[:, 0].reshape(256, 128), pltpu.roll(bands[:, 1].reshape(256, 128), 64, 1)
        )

    even, odd = dense(halves[:, 0]), dense(halves[:, 1])
    product = 0.0
    for cols, bands in (
        (same, jnp.where(core == 0, even, odd)), (other, jnp.where(core == 0, odd, even))
    ):
        product = product + lax.dot_general(
            cols[:, 64:96, :].reshape(256, 128), bands.astype(BF16), (((0,), (0,)), ((), ())),
            preferred_element_type=F32,
        )
    rows = product[0:64] + pltpu.roll(product[64:128], 64, 1)
    rows = jnp.where(half_lane, rows[0:32], pltpu.roll(rows[32:64], 64, 1))
    weights = jnp.sum(parts[:, 96:112, :].astype(F32), axis=0)[8:16]
    extra = jnp.sum(parts[:, 64:80, :].astype(F32), axis=0)[8:16]
    small = extra[2:3] + extra[3:4]
    loss = extra[4:5] + extra[5:6]
    small_hi = small.astype(BF16).astype(F32)
    loss_hi = loss.astype(BF16).astype(F32)
    whole = jnp.concatenate(
        [
            rows, weights, extra[0:2], small_hi, small - small_hi, loss_hi, loss - loss_hi,
            jnp.zeros((2, 128), F32),
        ],
        axis=0,
    )
    out[...] = jnp.broadcast_to(whole.astype(BF16)[None], (CHIPS, 48, 128))


def sum_call(parts, same, other):
    return pl.pallas_call(
        sum_kernel,
        out_shape=(
            jax.ShapeDtypeStruct((CHIPS, 48, 128), BF16),
            jax.ShapeDtypeStruct((32, 128), BF16),
            jax.ShapeDtypeStruct((32, 128), BF16),
        ),
        in_specs=[pl.BlockSpec(memory_space=pltpu.VMEM)] * 3,
        out_specs=(pl.BlockSpec(memory_space=pltpu.VMEM),) * 3,
        scratch_shapes=[pltpu.VMEM((1408, 128), F32)],
        compiler_params=pltpu.CompilerParams(vmem_limit_bytes=16 * 2**20),
        name="sums",
    )(parts, same, other)


def final_kernel(
    same, other, mine, received, w_proj,
    grad_proj_hbm, grad_conv_hbm, grad_feats_hbm, bias_hbm, w_out_hbm, loss_hbm,
    grad_proj, grad_conv_t, grad_feats, bias, w_out, loss, sems,
):
    is_first = lax.axis_index("band") % 2 == 0
    half_lane = lane_ids((1, 128)) < 64
    firsts, seconds = [], []
    puts = []
    for k in range(1):
        for chip in range(16 * k, 16 * k + 16):
            here = same[chip].astype(F32)
            there = other[chip].astype(F32)
            left = jnp.where(is_first, here, there)
            right = jnp.where(is_first, there, here)
            firsts.append(left[32:48])
            seconds.append(right[32:40])
            left, right = left[0:32], right[0:32]
            row = chip * 64
            grad_proj[row : row + 32, :] = jnp.where(half_lane, left, pltpu.roll(right, 64, 1))
            grad_proj[row + 32 : row + 64, :] = jnp.where(half_lane, pltpu.roll(left, 64, 1), right)
        rows = pl.ds(k * 1024, 1024)
        puts.append(pltpu.make_async_copy(grad_proj.at[rows], grad_proj_hbm.at[rows], sems.at[k]))
        puts[k].start()
    wide = jnp.concatenate(seconds + [first[0:8] for first in firsts], axis=0)
    for k in range(4):
        grad_conv_t[:, k * 128 : k * 128 + 128] = wide[k * 64 : k * 64 + 64]
    last = jnp.concatenate([first[8:9] for first in firsts] + [first[9:10] for first in firsts], axis=0)
    grad_conv_t[0:32, 512:576] = last[:, 0:64]
    grad_conv_t[32:64, 512:576] = last[:, 64:128]
    puts.append(pltpu.make_async_copy(grad_conv_t, grad_conv_hbm, sems.at[4]))
    puts[1].start()
    small = firsts[0][10:11] + firsts[0][11:12]
    bias[...] = small[:, 0:64]
    w_out[...] = small[:, 64:128]
    loss[...] = (firsts[0][12:13] + firsts[0][13:14])[:, 0:1]
    for k, (held, result) in enumerate(((bias, bias_hbm), (w_out, w_out_hbm), (loss, loss_hbm))):
        puts.append(pltpu.make_async_copy(held, result, sems.at[6 + k]))
        puts[2 + k].start()
    gproj = mine[...] + received[...]
    grad_feats[...] = lax.dot_general(
        gproj, w_proj[...], (((1,), (1,)), ((), ())), preferred_element_type=F32
    ).astype(BF16)
    put_feats = pltpu.make_async_copy(grad_feats, grad_feats_hbm, sems.at[5])
    put_feats.start()
    for put in puts + [put_feats]:
        put.wait()


def final_call(*operands):
    return pl.pallas_call(
        final_kernel,
        out_shape=(
            jax.ShapeDtypeStruct((1024, 128), F32),
            jax.ShapeDtypeStruct((64, 576), F32),
            jax.ShapeDtypeStruct((32, 1024), BF16),
            jax.ShapeDtypeStruct((1, 64), F32),
            jax.ShapeDtypeStruct((1, 64), F32),
            jax.ShapeDtypeStruct((1, 1), F32),
        ),
        in_specs=[pl.BlockSpec(memory_space=pltpu.VMEM)] * len(operands),
        out_specs=(pl.BlockSpec(memory_space=pltpu.HBM),) * 6,
        scratch_shapes=[
            pltpu.VMEM((1024, 128), F32),
            pltpu.VMEM((64, 576), F32),
            pltpu.VMEM((32, 1024), BF16),
            pltpu.VMEM((1, 64), F32),
            pltpu.VMEM((1, 64), F32),
            pltpu.VMEM((1, 1), F32),
            pltpu.SemaphoreType.DMA((9,)),
        ],
        compiler_params=pltpu.CompilerParams(vmem_limit_bytes=8 * 2**20),
        name="outputs",
    )(*operands)


def body(feats, w_proj, conv_w, conv_b, w_out, target, mask):
    swap = [(2 * i + o, 2 * (i + 1 - 2 * (i % 2)) + o) for i in range(BANDS) for o in range(2)]
    same_core = [[2 * i + o for i in range(core, BANDS, 2) for o in range(2)] for core in range(2)]
    same_row = [[2 * i + o for i in range(core, BANDS, 2)] for core in range(2) for o in range(2)]
    same = lax.all_to_all(front_call(feats, w_proj), GROUP, 0, 0, tiled=True, axis_index_groups=same_row)
    ready = prep_call(mask.reshape(8, 128), target, conv_w.T)
    same, ready = lax.optimization_barrier((same, ready))
    other = lax.ppermute(same, GROUP, swap)
    kept, given = tile_call(same, other, conv_b.reshape(1, 64), w_out.reshape(1, 64), *ready)
    joined = join_call(kept, lax.ppermute(given, GROUP, swap))
    parts = lax.all_to_all(joined, GROUP, 0, 0, tiled=True, axis_index_groups=same_core)
    sums, mine, theirs = sum_call(parts, same, other)
    every = lax.all_to_all(sums, GROUP, 0, 0, tiled=True, axis_index_groups=same_core)
    every, theirs = lax.optimization_barrier((every, theirs))
    grad_proj, grad_conv_t, grad_feats, bias, w_out, loss = final_call(
        every, lax.ppermute(every, GROUP, swap), mine, lax.ppermute(theirs, GROUP, swap), w_proj
    )
    return (loss.reshape(1), grad_proj, grad_conv_t.T, bias.reshape(64), w_out.reshape(64), grad_feats)


def solution(mesh):
    placed = (
        P(("rep", "band"), None),
        P(),
        P(),
        P(),
        P(),
        P(("rep", "band"), "off", None),
        P("rep"),
    )
    return jax.shard_map(
        body,
        mesh=mesh,
        in_specs=placed,
        out_specs=(
            P("rep"),
            P("rep", None),
            P("rep", None),
            P("rep"),
            P("rep"),
            P(("rep", "band", "off"), None),
        ),
        check_vma=False,
    )
```
